32 devices in a mesh: seq: 8 (over y, x, core), db: 4 (over z).
Axes of the slice: x: 2, y: 2, z: 4, core: 2. Of those that a mesh axis runs over, the one named last changes fastest.
Arguments:
- hidden_in: bfloat16 [2048, 4096], P('seq'), may hold values from -4 to 4
- query_rows: bfloat16 [2048, 4096], P('seq', 'db'), may hold values from -32 to 32
- key_rows: bfloat16 [2048, 4096], P('seq', 'db'), may hold values from -32 to 32
- value_rows: bfloat16 [2048, 4096], P('seq', 'db'), may hold values from -6 to 6
- w_self_out: bfloat16 [4096, 4096], P('db'), may hold values from -0.1796875 to 0.1796875
- norm_gain: bfloat16 [4096], replicated, may hold values from 0.099609375 to 1.8984375
- w_cross_q: bfloat16 [4096, 4096], P(None, 'db'), may hold values from -2 to 2
- w_cross_k: bfloat16 [1024, 4096], P(None, 'db'), may hold values from -1 to 1
- w_cross_v: bfloat16 [1024, 4096], P(None, 'db'), may hold values from -0.1875 to 0.1875
- w_cross_out: bfloat16 [4096, 4096], P('db'), may hold values from -0.09375 to 0.09375
- enc_table: bfloat16 [32, 128, 1024], P('db'), may hold values from -6 to 6
- nb_shard: int32 [32, 2], P('seq'), may hold values from 0 to 3, all different within a row; in each aligned block of 4 rows (0 to 3, 4 to 7, ...) at most 4 rows name the same one
- nb_row: int32 [32, 2], P('seq'), may hold values from 0 to 7
Outputs:
- block_out: float32 [2048, 4096], P(('seq', 'db'))
The draws below stay inside these ranges and needn't reach their ends.
Inputs may be any that keep to these rules, and one draw needn't show every extreme that they name: `nb_shard`: the spans held by one index of seq name each shard at most 4 times, and in the spans of some indices one shard exactly 4 times; the 2 neighbours of a span lie in different shards.
All inputs are finite; a program needn't handle non-finite values.
Results may differ from the reference program's by a relative error of at most 0.038.
Values may be sent and summed in bfloat16 or wider, within the bound.
No kernel may reach another device: no remote copies, remote signals or barrier semaphores. Data moves between devices by JAX's collectives and lax.ppermute only.
A program may use at most 128 MiB of HBM per device.

```python
import math
import jax
import jax.numpy as jnp
import numpy as np
from jax import lax

D = 4096
H = 32
HD = 128
D_ENC = 1024
SPAN = 64
NEIGH = 2
NLEN = 128
ROWS_SHARD = 8
TOKENS = 2048
SPANS_DEV = 4
SPANS = 32
CAP = 4
DB_ROWS = 32
N_DB = 4


def drawn_pair(key):
    query_base = jnp.clip(jax.random.normal(jax.random.fold_in(key, 11), (TOKENS, H * HD), jnp.float32), -4.0, 4.0)
    key_base = jnp.clip(jax.random.normal(jax.random.fold_in(key, 12), (TOKENS, H * HD), jnp.float32), -4.0, 4.0)
    return (query_base, key_base)


def draw_query_rows(key, part):
    return drawn_pair(key)[0].astype(jnp.bfloat16)


def draw_key_rows(key, part):
    return drawn_pair(key)[1].astype(jnp.bfloat16)


def draw_hidden_in(key, part):
    base = 0.35 * jnp.clip(jax.random.normal(jax.random.fold_in(key, 24), (TOKENS, D), jnp.float32), -8.0, 8.0)
    return base.astype(jnp.bfloat16)


def draw_enc_table(key, part):
    base = jnp.clip(jax.random.normal(jax.random.fold_in(key, 26), (DB_ROWS, NLEN, D_ENC), jnp.float32), -6.0, 6.0)
    return base.astype(jnp.bfloat16)


def draw_w_cross_q(key, part):
    base = 2.0 * jnp.clip(jax.random.normal(jax.random.fold_in(key, 30), (D, H * HD), jnp.float32), -6.0, 6.0) / D ** 0.5
    return base.astype(jnp.bfloat16)


def draw_w_cross_k(key, part):
    base = jnp.clip(jax.random.normal(jax.random.fold_in(key, 29), (D_ENC, H * HD), jnp.float32), -6.0, 6.0) / D_ENC ** 0.5
    return base.astype(jnp.bfloat16)


def touch_ends(values, own_key, low, largest):
    longest = values.shape.index(max(values.shape))
    spots = []
    for shift in (0, 1):
        where = [jax.random.randint(jax.random.fold_in(own_key, axis), (), 0, length) for axis, length in enumerate(values.shape)]
        where[longest] = (where[longest] + shift) % values.shape[longest]
        spots.append(tuple(where))
    return values.at[spots[0]].set(low).at[spots[1]].set(largest)


def block_scale(stream_key, shape, split, low, high):
    factor_of, own = 1.0, jax.random.fold_in(stream_key, 6)
    for dim, blocks in split:
        draws = jnp.exp(jax.random.uniform(jax.random.fold_in(own, dim), (blocks,), jnp.float32, low / len(split), high / len(split)))
        factor_of = factor_of * jnp.repeat(draws, shape[dim] // blocks).reshape([-1 if axis == dim else 1 for axis in range(len(shape))])
    return factor_of


def routed_block(rng, own, number, rows, count, top, bound, skew):
    order = jax.random.permutation(rng, count)
    packed, ordinary = shares(count, rows * top, bound, skew, True), shares(count, rows * top, bound, skew, False)
    places = jnp.arange(count)

    def named(lengths, rotation):
        used = int((lengths > 0).sum())
        fixed = max(1, used // 4)
        shifted = fixed + (places - fixed + rotation * (used - fixed)) % max(1, count - fixed)
        return jnp.zeros((count,), jnp.int32).at[order[jnp.where(places < fixed, places, shifted)]].set(jnp.asarray(lengths, jnp.int32))

    lengths = jnp.where(number % 4 == 0, named(packed, number // 4), named(ordinary, number - number // 4 - 1))
    mixed = jax.random.permutation(jax.random.fold_in(own, 3), count)
    giver, sink = mixed[0:count // 2 * 2:2], mixed[1:count // 2 * 2:2]
    room = jnp.minimum(lengths[giver] - 1, bound - lengths[sink]) // 2
    room = jnp.where((giver == order[0]) | (sink == order[0]) | (lengths[sink] == 0), 0, jnp.maximum(room, 0))
    shifted = jax.random.randint(jax.random.fold_in(own, 4), (count // 2,), 0, 1 << 20) % (room + 1)
    lengths = lengths.at[giver].add(-shifted).at[sink].add(shifted)
    members = jnp.searchsorted(jnp.cumsum(lengths), jnp.arange(rows * top), side="right").astype(jnp.int32)
    table = members.reshape(top, rows).T
    table = table[jax.random.permutation(jax.random.fold_in(own, 1), rows)]
    rotation = jax.random.randint(jax.random.fold_in(own, 2), (rows, 1), 0, top)
    return jnp.take_along_axis(table, (jnp.arange(top)[None, :] + rotation) % top, axis=1)


def shares(number_of, total, limit, skew, full):
    loads = [(1 << 20) // math.isqrt(standing ** skew) + 1 for standing in range(1, number_of + 1)]
    largest = limit if full else min(limit, max(-(-total // number_of), total * loads[0] // sum(loads)))
    least = 1 if total - largest >= number_of - 1 else 0
    given, rest = [largest] + [least] * (number_of - 1), total - largest - least * (number_of - 1)
    while rest > 0:
        movable = [i for i in range(1, number_of) if given[i] < largest] or [i for i in range(1, number_of) if given[i] < limit]
        mass, left = sum([loads[i] for i in movable]), rest
        for i in movable:
            extra = min(limit - given[i], max(1, left * loads[i] // mass), rest)
            given[i] = given[i] + extra
            rest = rest - extra
    return np.array(given)


def scatter_about(stream_key, shape, scale, bound, pieces=(), held_as=jnp.bfloat16):
    result = scale * jax.random.normal(stream_key, shape, jnp.float32)
    if pieces:
        result = result * block_scale(stream_key, shape, pieces, -0.22, 0.18)
    return jnp.clip(result, -bound, bound).astype(held_as)


def setup_inputs(seed: int = 0) -> dict:
    seeds = jax.random.split(jax.random.key(seed), 14)
    hidden_in = draw_hidden_in(jax.random.fold_in(seeds[13], 71), 0)
    query_rows = draw_query_rows(jax.random.fold_in(seeds[13], 71), 0)
    key_rows = draw_key_rows(jax.random.fold_in(seeds[13], 71), 0)
    value_rows = scatter_about(seeds[3], (TOKENS, H * HD), 1.0, 6.0, ((0, 8), (1, 4)))
    w_self_out = scatter_about(seeds[4], (H * HD, D), 0.03, 0.1796875, ((0, 4),))
    norm_gain = jnp.clip(1.0 + 0.18 * jax.random.normal(seeds[5], (D,), jnp.float32), 0.099609375, 1.8984375).astype(jnp.bfloat16)
    w_cross_q = draw_w_cross_q(jax.random.fold_in(seeds[13], 71), 0)
    w_cross_k = draw_w_cross_k(jax.random.fold_in(seeds[13], 71), 0)
    w_cross_v = scatter_about(seeds[8], (D_ENC, H * HD), D_ENC ** -0.5, 0.1875, ((1, 4),))
    w_cross_out = scatter_about(seeds[9], (H * HD, D), (H * HD) ** -0.5, 0.09375, ((0, 4),))
    enc_table = draw_enc_table(jax.random.fold_in(seeds[13], 71), 0)
    nb_shard_keys = jax.random.split(jax.random.fold_in(seeds[11], 1), SPANS // SPANS_DEV)
    nb_shard_turns = jax.random.permutation(jax.random.fold_in(seeds[11], 3), SPANS // SPANS_DEV)
    nb_shard = jax.vmap(lambda own, number: routed_block(jax.random.fold_in(seeds[11], 2), own, number, SPANS_DEV, N_DB, NEIGH, CAP, 2))(nb_shard_keys, nb_shard_turns).reshape((SPANS, NEIGH))
    nb_row = touch_ends(jax.random.randint(seeds[12], (SPANS, NEIGH), 0, ROWS_SHARD), jax.random.fold_in(seeds[12], 1), 0, ROWS_SHARD - 1).astype(jnp.int32)
    return dict(hidden_in=hidden_in, query_rows=query_rows, key_rows=key_rows, value_rows=value_rows, w_self_out=w_self_out, norm_gain=norm_gain, w_cross_q=w_cross_q, w_cross_k=w_cross_k, w_cross_v=w_cross_v, w_cross_out=w_cross_out, enc_table=enc_table, nb_shard=nb_shard, nb_row=nb_row)


NEG_BIG = -1e+30

def reference(hidden_in, query_rows, key_rows, value_rows, w_self_out, norm_gain, w_cross_q, w_cross_k, w_cross_v, w_cross_out, enc_table, nb_shard, nb_row):
    score_scale = 1.0 / math.sqrt(HD)
    query_heads = query_rows.reshape(TOKENS, H, HD).transpose(1, 0, 2)
    key_heads = key_rows.reshape(TOKENS, H, HD).transpose(1, 0, 2)
    value_heads = value_rows.reshape(TOKENS, H, HD).transpose(1, 0, 2)
    positions = jnp.arange(TOKENS, dtype=jnp.int32)
    causal = positions[None, :] <= positions[:, None]

    def head_attend(operands):
        query_one, key_one, value_one = operands
        scores = jnp.dot(query_one, key_one.T, preferred_element_type=jnp.float32) * score_scale
        scores = jnp.where(causal, scores, NEG_BIG)
        top_score = lax.optimization_barrier(jnp.max(scores, axis=-1, keepdims=True))
        weights = jnp.exp(scores - top_score)
        totals = lax.optimization_barrier(jnp.sum(weights, axis=-1, keepdims=True))
        mixed = jnp.dot(weights.astype(jnp.bfloat16), value_one, preferred_element_type=jnp.float32) / totals
        return mixed.astype(jnp.bfloat16)
    head_outputs = lax.map(head_attend, (query_heads, key_heads, value_heads))
    attended = head_outputs.transpose(1, 0, 2).reshape(TOKENS, H * HD)
    attn_total = jnp.dot(attended, w_self_out, preferred_element_type=jnp.float32)
    residual = hidden_in.astype(jnp.float32) + attn_total
    mean_square = lax.optimization_barrier(jnp.mean(residual * residual, axis=-1, keepdims=True))
    normed = (residual * lax.rsqrt(mean_square + 1e-05) * norm_gain.astype(jnp.float32)).astype(jnp.bfloat16)
    cross_query = jnp.dot(normed, w_cross_q, preferred_element_type=jnp.float32).astype(jnp.bfloat16)
    table_rows = (nb_shard * ROWS_SHARD + nb_row).reshape(SPANS * NEIGH).astype(jnp.int32)
    encodings = jnp.take(enc_table, table_rows, axis=0).reshape(SPANS * NEIGH * NLEN, D_ENC)
    cross_keys = jnp.dot(encodings, w_cross_k, preferred_element_type=jnp.float32).astype(jnp.bfloat16)
    cross_values = jnp.dot(encodings, w_cross_v, preferred_element_type=jnp.float32).astype(jnp.bfloat16)
    zero_group = jnp.zeros((1, NEIGH * NLEN, H, HD), jnp.bfloat16)
    group_keys = jnp.concatenate((zero_group, cross_keys.reshape(SPANS, NEIGH * NLEN, H, HD)), axis=0)
    group_values = jnp.concatenate((zero_group, cross_values.reshape(SPANS, NEIGH * NLEN, H, HD)), axis=0)
    padded = jnp.pad(cross_query, ((1, SPAN - 1), (0, 0))).reshape(SPANS + 1, SPAN, H, HD)

    def group_attend(operands):
        query_group, key_group, value_group = operands
        scores = jnp.einsum('qhd,khd->hqk', query_group.astype(jnp.float32), key_group.astype(jnp.float32)) * score_scale
        top_score = lax.optimization_barrier(jnp.max(scores, axis=-1, keepdims=True))
        weights = jnp.exp(scores - top_score)
        totals = lax.optimization_barrier(jnp.sum(weights, axis=-1, keepdims=True))
        rounded = lax.optimization_barrier(weights.astype(jnp.bfloat16)).astype(jnp.float32)
        mixed = jnp.einsum('hqk,khd->hqd', rounded, value_group.astype(jnp.float32)) / totals
        return mixed.transpose(1, 0, 2).reshape(SPAN, H * HD).astype(jnp.bfloat16)
    grouped = lax.map(group_attend, (padded, group_keys, group_values))
    cross_mixed = grouped.reshape((SPANS + 1) * SPAN, H * HD)[1:TOKENS + 1]
    cross_total = jnp.dot(cross_mixed, w_cross_out, preferred_element_type=jnp.float32)
    return residual + cross_total
```

```python
import functools
import math

import jax
import jax.numpy as jnp
from jax import lax
from jax.experimental import pallas as pl
from jax.experimental.pallas import tpu as pltpu
from jax.sharding import PartitionSpec as P

HD = 128
SPAN = 64
NEIGH = 2
NLEN = 128
GROUP = NEIGH * NLEN

NEG_BIG = -1e30
LOG2E = 1.4426950408889634
VMEM_BYTES = 48 * 1024 * 1024


def shift(block, axis, distance, senders):
    size = lax.axis_size(axis)
    route = [(k, k + distance) for k in senders if 0 <= k + distance < size]
    return lax.ppermute(block, axis, route)


def add_rounded(first, second):
    return (first.astype(jnp.float32) + second.astype(jnp.float32)).astype(jnp.bfloat16)


def line_reduce_scatter(blocks):
    size = lax.axis_size("db")
    me = lax.axis_index("db")

    def pick(d):
        return lax.dynamic_index_in_dim(blocks, jnp.clip(d, 0, size - 1), 0, keepdims=False)

    up = down = None
    for step in range(size - 1):
        far = size - 1 - step
        up_block, down_block = pick(me + far), pick(me - far)
        if step:
            up_block, down_block = add_rounded(up_block, up), add_rounded(down_block, down)
        up = shift(up_block, "db", 1, range(step + 1))
        down = shift(down_block, "db", -1, range(size - 1 - step, size))
    total = pick(me).astype(jnp.float32)
    return total + up.astype(jnp.float32) + down.astype(jnp.float32)


def line_all_gather(block):
    size = lax.axis_size("db")
    me = lax.axis_index("db")
    whole = jnp.zeros((size,) + block.shape, block.dtype)
    whole = lax.dynamic_update_index_in_dim(whole, block, me, 0)
    up = down = block
    pieces = []
    for step in range(size - 1):
        up = shift(up, "db", 1, range(step, size))
        down = shift(down, "db", -1, range(0, size - step))
        pieces.append((step + 1, up, down))
    parts = []
    for owner in range(size):
        chosen = block
        for distance, from_low, from_high in pieces:
            chosen = jnp.where(me - owner == distance, from_low, chosen)
            chosen = jnp.where(owner - me == distance, from_high, chosen)
        parts.append(chosen)
    return jnp.stack(parts)


def self_kernel(qkv_ref, out_ref, *, blocks, rows, scale):
    for block in range(blocks):
        query = qkv_ref[block, 0]
        live = (block + 1) * rows
        keys = qkv_ref[0 : block + 1, 1].reshape(live, HD)
        values = qkv_ref[0 : block + 1, 2].reshape(live, HD)
        scores = lax.dot_general(
            query, keys, (((1,), (1,)), ((), ())), preferred_element_type=jnp.float32
        )
        query_pos = block * rows + lax.broadcasted_iota(jnp.int32, (rows, live), 0)
        key_pos = lax.broadcasted_iota(jnp.int32, (rows, live), 1)
        scores = jnp.where(key_pos <= query_pos, scores * (scale * LOG2E), NEG_BIG)
        top = jnp.max(scores, axis=-1, keepdims=True)
        weights = jnp.exp2(scores - top)
        total = jnp.sum(weights, axis=-1, keepdims=True)
        mixed = jnp.dot(weights.astype(jnp.bfloat16), values, preferred_element_type=jnp.float32)
        out_ref[block] = (mixed / total).astype(jnp.bfloat16)


def self_attend_head(qkv, scale):
    blocks, _, rows, _ = qkv.shape
    return pl.pallas_call(
        functools.partial(self_kernel, blocks=blocks, rows=rows, scale=scale),
        out_shape=jax.ShapeDtypeStruct((blocks, rows, HD), jnp.bfloat16),
        in_specs=[pl.BlockSpec(memory_space=pltpu.VMEM)],
        out_specs=pl.BlockSpec(memory_space=pltpu.VMEM),
        compiler_params=pltpu.CompilerParams(vmem_limit_bytes=VMEM_BYTES),
        cost_estimate=pl.CostEstimate(
            flops=2 * blocks * blocks * rows * rows * HD,
            bytes_accessed=8 * blocks * rows * HD,
            transcendentals=blocks * blocks * rows * rows // 2,
        ),
        name="self_attend",
    )(qkv)


def self_attention_by_head(query_rows, key_rows, value_rows, scale):
    rows, width = query_rows.shape
    count = lax.axis_size("seq")
    packed = jnp.stack((query_rows, key_rows, value_rows)).reshape(3, rows, count, HD)
    packed = packed.transpose(2, 0, 1, 3)
    held = lax.all_to_all(packed, "seq", 0, 0, tiled=True)
    mixed = self_attend_head(held, scale)
    back = lax.all_to_all(mixed, "seq", 0, 0, tiled=True)
    return back.transpose(1, 0, 2).reshape(rows, width)


def self_attention_gathered(query_rows, key_rows, value_rows, scale):
    rows, width = query_rows.shape
    heads = width // HD
    keys = lax.all_gather(key_rows, "seq", axis=0, tiled=True)
    values = lax.all_gather(value_rows, "seq", axis=0, tiled=True)
    count = keys.shape[0]
    query_pos = lax.axis_index("seq") * rows + jnp.arange(rows, dtype=jnp.int32)
    allowed = jnp.arange(count, dtype=jnp.int32)[None, :] <= query_pos[:, None]
    scores = (
        jnp.einsum(
            "qhd,khd->hqk",
            query_rows.reshape(rows, heads, HD),
            keys.reshape(count, heads, HD),
            preferred_element_type=jnp.float32,
        )
        * scale
    )
    scores = jnp.where(allowed[None], scores, NEG_BIG)
    weights = jnp.exp(scores - jnp.max(scores, axis=-1, keepdims=True))
    total = jnp.sum(weights, axis=-1)
    mixed = jnp.einsum(
        "hqk,khd->hqd",
        weights.astype(jnp.bfloat16),
        values.reshape(count, heads, HD),
        preferred_element_type=jnp.float32,
    )
    return (mixed / total[..., None]).transpose(1, 0, 2).reshape(rows, width).astype(jnp.bfloat16)


def project_kernel(where_ref, first_ref, second_ref, wk_ref, wv_ref, keys_ref, values_ref):
    depth = first_ref.shape[-1]
    rows = jnp.concatenate(
        (first_ref[...].reshape(NLEN, depth), second_ref[...].reshape(NLEN, depth)), axis=0
    )
    keys_ref[...] = jnp.dot(rows, wk_ref[...], preferred_element_type=jnp.float32).astype(
        jnp.bfloat16
    )
    values_ref[...] = jnp.dot(rows, wv_ref[...], preferred_element_type=jnp.float32).astype(
        jnp.bfloat16
    )


def project_encodings(where, table, w_cross_k, w_cross_v):
    groups = where.shape[0] // (2 * NEIGH)
    _, cuts, _, piece, depth = table.shape
    width = w_cross_k.shape[1]

    def entry(neighbour):
        def index(group, where_ref):
            at = 2 * (NEIGH * group + neighbour)
            return (where_ref[at], 0, where_ref[at + 1], 0, 0)

        return pl.BlockSpec((1, cuts, 1, piece, depth), index)

    fixed = pl.BlockSpec((depth, width), lambda group, where_ref: (0, 0))
    made = pl.BlockSpec((GROUP, width), lambda group, where_ref: (group, 0))
    return pl.pallas_call(
        project_kernel,
        out_shape=[jax.ShapeDtypeStruct((groups * GROUP, width), jnp.bfloat16)] * 2,
        grid_spec=pltpu.PrefetchScalarGridSpec(
            num_scalar_prefetch=1,
            grid=(groups,),
            in_specs=[entry(0), entry(1), fixed, fixed],
            out_specs=[made, made],
        ),
        compiler_params=pltpu.CompilerParams(
            vmem_limit_bytes=VMEM_BYTES, dimension_semantics=("arbitrary",)
        ),
        cost_estimate=pl.CostEstimate(
            flops=4 * groups * GROUP * depth * width,
            bytes_accessed=2 * (groups * GROUP * (depth + 2 * width) + 2 * depth * width),
            transcendentals=0,
        ),
        name="project_encodings",
    )(where, table, table, w_cross_k, w_cross_v)


def cross_kernel(live_ref, query_ref, keys_ref, values_ref, out_ref, *, spans, heads, scale):
    row = lax.broadcasted_iota(jnp.int32, (SPAN, 2 * GROUP), 0)
    column = lax.broadcasted_iota(jnp.int32, (SPAN, 2 * GROUP), 1)
    allowed = (column >= GROUP) == (row == SPAN - 1)
    for span in range(spans):
        for head in range(heads):
            lanes = slice(head * HD, (head + 1) * HD)
            query = query_ref[span * SPAN : (span + 1) * SPAN, lanes]
            keys = keys_ref[span * GROUP : (span + 2) * GROUP, lanes]
            values = values_ref[span * GROUP : (span + 2) * GROUP, lanes]
            scores = lax.dot_general(
                query, keys, (((1,), (1,)), ((), ())), preferred_element_type=jnp.float32
            )
            scores = jnp.where(allowed, scores * (scale * LOG2E), NEG_BIG)
            top = jnp.max(scores, axis=-1, keepdims=True)
            weights = jnp.exp2(scores - top)
            total = jnp.sum(weights, axis=-1, keepdims=True)
            mixed = jnp.dot(
                weights.astype(jnp.bfloat16), values, preferred_element_type=jnp.float32
            )
            mixed = mixed / total
            if span == 0:
                own = lax.broadcasted_iota(jnp.int32, (SPAN, HD), 0) == SPAN - 1
                mixed = jnp.where(own | (live_ref[0] > 0), mixed, 0.0)
            out_ref[span * SPAN : (span + 1) * SPAN, lanes] = mixed.astype(jnp.bfloat16)


def cross_attend(live, query, keys, values, scale):
    rows, width = query.shape
    vmem = pl.BlockSpec(memory_space=pltpu.VMEM)
    return pl.pallas_call(
        functools.partial(
            cross_kernel, spans=rows // SPAN, heads=width // HD, scale=scale
        ),
        out_shape=jax.ShapeDtypeStruct((rows, width), jnp.bfloat16),
        in_specs=[pl.BlockSpec(memory_space=pltpu.SMEM), vmem, vmem, vmem],
        out_specs=vmem,
        compiler_params=pltpu.CompilerParams(vmem_limit_bytes=VMEM_BYTES),
        cost_estimate=pl.CostEstimate(
            flops=8 * rows * GROUP * width,
            bytes_accessed=2 * (2 * rows + 2 * keys.shape[0]) * width,
            transcendentals=2 * rows * GROUP * width // HD,
        ),
        name="cross_attend",
    )(live, query, keys, values)


def per_device(
    hidden_in,
    query_rows,
    key_rows,
    value_rows,
    w_self_out,
    norm_gain,
    w_cross_q,
    w_cross_k,
    w_cross_v,
    w_cross_out,
    enc_table,
    nb_shard,
    nb_row,
):
    rows, features = hidden_in.shape
    width = query_rows.shape[1]
    heads = width // HD
    n_seq, n_db = lax.axis_size("seq"), lax.axis_size("db")
    seq_index, db_index = lax.axis_index("seq"), lax.axis_index("db")
    scale = 1.0 / math.sqrt(HD)
    share = rows // n_db

    rows_shard, _, depth = enc_table.shape
    piece = rows_shard * NLEN // n_seq
    part = lax.dynamic_slice_in_dim(
        enc_table.reshape(rows_shard * NLEN, depth), seq_index * piece, piece, 0
    )
    along_db = lax.all_gather(part, "db", axis=0)
    wanted = jnp.stack((nb_row, nb_shard), axis=-1).astype(jnp.int32)
    before = shift(wanted[-1], "seq", 1, range(n_seq))
    where = jnp.concatenate((before[None], wanted), axis=0).reshape(-1)

    if heads == n_seq:
        attended = self_attention_by_head(query_rows, key_rows, value_rows, scale)
    else:
        attended = self_attention_gathered(query_rows, key_rows, value_rows, scale)

    along_db, attended = lax.optimization_barrier((along_db, attended))
    table = lax.all_gather(along_db, "seq", axis=0).reshape(
        rows_shard, NLEN // piece, n_db, piece, depth
    )

    partial = jnp.dot(attended, w_self_out, preferred_element_type=jnp.float32).astype(jnp.bfloat16)
    attn_share = line_reduce_scatter(partial.reshape(n_db, share, features))
    residual = (
        lax.dynamic_slice_in_dim(hidden_in, db_index * share, share, 0).astype(jnp.float32)
        + attn_share
    )
    mean_square = jnp.mean(residual * residual, axis=-1, keepdims=True)
    normed_share = (
        residual * lax.rsqrt(mean_square + 1e-05) * norm_gain.astype(jnp.float32)
    ).astype(jnp.bfloat16)
    normed = line_all_gather(normed_share).reshape(rows, features)
    cross_query = jnp.dot(normed, w_cross_q, preferred_element_type=jnp.float32).astype(
        jnp.bfloat16
    )
    keys, values = project_encodings(where, table, w_cross_k, w_cross_v)
    live = (seq_index > 0).astype(jnp.int32).reshape(1)
    mixed = cross_attend(live, cross_query, keys, values, scale)
    out_partial = jnp.dot(mixed, w_cross_out, preferred_element_type=jnp.float32).astype(
        jnp.bfloat16
    )
    return residual + line_reduce_scatter(out_partial.reshape(n_db, share, features))


def solution(mesh):
    placed = (
        P("seq", None),
        P("seq", "db"),
        P("seq", "db"),
        P("seq", "db"),
        P("db", None),
        P(),
        P(None, "db"),
        P(None, "db"),
        P(None, "db"),
        P("db", None),
        P("db", None, None),
        P("seq", None),
        P("seq", None),
    )
    return jax.shard_map(
        per_device, mesh=mesh, in_specs=placed, out_specs=P(("seq", "db"), None), check_vma=False
    )
```

```python
import functools
import math

import jax
import jax.numpy as jnp
from jax import lax
from jax.experimental import pallas as pl
from jax.experimental.pallas import tpu as pltpu
from jax.sharding import PartitionSpec as P

HD = 128
SPAN = 64
NEIGH = 2
NLEN = 128
GROUP = NEIGH * NLEN

NEG_BIG = -1e30
LOG2E = 1.4426950408889634
VMEM_BYTES = 48 * 1024 * 1024


def shift(block, axis, distance, senders):
    size = lax.axis_size(axis)
    route = [(k, k + distance) for k in senders if 0 <= k + distance < size]
    return lax.ppermute(block, axis, route)


def add_rounded(first, second):
    return (first.astype(jnp.float32) + second.astype(jnp.float32)).astype(jnp.bfloat16)


def line_reduce_scatter(blocks):
    size = lax.axis_size("db")
    me = lax.axis_index("db")

    def pick(d):
        return lax.dynamic_index_in_dim(blocks, jnp.clip(d, 0, size - 1), 0, keepdims=False)

    up = down = None
    for step in range(size - 1):
        far = size - 1 - step
        up_block, down_block = pick(me + far), pick(me - far)
        if step:
            up_block, down_block = add_rounded(up_block, up), add_rounded(down_block, down)
        up = shift(up_block, "db", 1, range(step + 1))
        down = shift(down_block, "db", -1, range(size - 1 - step, size))
        up, down = lax.optimization_barrier((up, down))
    total = pick(me).astype(jnp.float32)
    return total + up.astype(jnp.float32) + down.astype(jnp.float32)


def line_all_gather(block, beside):
    size = lax.axis_size("db")
    me = lax.axis_index("db")
    up = down = block
    pieces = []
    for step in range(size - 1):
        up = shift(up, "db", 1, range(step, size))
        down = shift(down, "db", -1, range(0, size - step))
        if step == (size - 1) // 2:
            up, down, beside = lax.optimization_barrier((up, down, beside))
        else:
            up, down = lax.optimization_barrier((up, down))
        pieces.append((step + 1, up, down))
    parts = []
    for owner in range(size):
        chosen = block
        for distance, from_low, from_high in pieces:
            chosen = jnp.where(me - owner == distance, from_low, chosen)
            chosen = jnp.where(owner - me == distance, from_high, chosen)
        parts.append(chosen)
    return jnp.stack(parts), beside


def self_kernel(qkv_ref, out_ref, *, blocks, rows, scale):
    for block in range(blocks):
        query = qkv_ref[block, 0]
        live = (block + 1) * rows
        keys = qkv_ref[0 : block + 1, 1].reshape(live, HD)
        values = qkv_ref[0 : block + 1, 2].reshape(live, HD)
        scores = lax.dot_general(
            query, keys, (((1,), (1,)), ((), ())), preferred_element_type=jnp.float32
        )
        query_pos = block * rows + lax.broadcasted_iota(jnp.int32, (rows, live), 0)
        key_pos = lax.broadcasted_iota(jnp.int32, (rows, live), 1)
        scores = jnp.where(key_pos <= query_pos, scores * (scale * LOG2E), NEG_BIG)
        top = jnp.max(scores, axis=-1, keepdims=True)
        weights = jnp.exp2(scores - top)
        total = jnp.sum(weights, axis=-1, keepdims=True)
        mixed = jnp.dot(weights.astype(jnp.bfloat16), values, preferred_element_type=jnp.float32)
        out_ref[block] = (mixed / total).astype(jnp.bfloat16)


def self_attend_head(qkv, scale):
    blocks, _, rows, _ = qkv.shape
    return pl.pallas_call(
        functools.partial(self_kernel, blocks=blocks, rows=rows, scale=scale),
        out_shape=jax.ShapeDtypeStruct((blocks, rows, HD), jnp.bfloat16),
        in_specs=[pl.BlockSpec(memory_space=pltpu.VMEM)],
        out_specs=pl.BlockSpec(memory_space=pltpu.VMEM),
        compiler_params=pltpu.CompilerParams(vmem_limit_bytes=VMEM_BYTES),
        cost_estimate=pl.CostEstimate(
            flops=2 * blocks * blocks * rows * rows * HD,
            bytes_accessed=8 * blocks * rows * HD,
            transcendentals=blocks * blocks * rows * rows // 2,
        ),
        name="self_attend",
    )(qkv)


def pack_kernel(query_ref, key_ref, value_ref, out_ref, sems, *, heads):
    copies = []
    for head in range(heads):
        for which, ref in enumerate((query_ref, key_ref, value_ref)):
            copies.append(
                pltpu.make_async_copy(
                    ref.at[:, pl.ds(head * HD, HD)], out_ref.at[head, which], sems.at[head, which]
                )
            )
    for copy in copies:
        copy.start()
    for copy in copies:
        copy.wait()


def pack_heads(query_rows, key_rows, value_rows):
    rows, width = query_rows.shape
    heads = width // HD
    anywhere = pl.BlockSpec(memory_space=pl.ANY)
    return pl.pallas_call(
        functools.partial(pack_kernel, heads=heads),
        out_shape=jax.ShapeDtypeStruct((heads, 3, rows, HD), jnp.bfloat16),
        in_specs=[anywhere] * 3,
        out_specs=anywhere,
        scratch_shapes=[pltpu.SemaphoreType.DMA((heads, 3))],
        cost_estimate=pl.CostEstimate(
            flops=0, bytes_accessed=12 * rows * width, transcendentals=0
        ),
        name="pack_heads",
    )(query_rows, key_rows, value_rows)


def self_attention_by_head(query_rows, key_rows, value_rows, scale):
    rows, width = query_rows.shape
    packed = pack_heads(query_rows, key_rows, value_rows)
    held = lax.all_to_all(packed, "seq", 0, 0, tiled=True)
    mixed = self_attend_head(held, scale)
    back = lax.all_to_all(mixed, "seq", 0, 0, tiled=True)
    return back.transpose(1, 0, 2).reshape(rows, width)


def self_attention_gathered(query_rows, key_rows, value_rows, scale):
    rows, width = query_rows.shape
    heads = width // HD
    keys = lax.all_gather(key_rows, "seq", axis=0, tiled=True)
    values = lax.all_gather(value_rows, "seq", axis=0, tiled=True)
    count = keys.shape[0]
    query_pos = lax.axis_index("seq") * rows + jnp.arange(rows, dtype=jnp.int32)
    allowed = jnp.arange(count, dtype=jnp.int32)[None, :] <= query_pos[:, None]
    scores = (
        jnp.einsum(
            "qhd,khd->hqk",
            query_rows.reshape(rows, heads, HD),
            keys.reshape(count, heads, HD),
            preferred_element_type=jnp.float32,
        )
        * scale
    )
    scores = jnp.where(allowed[None], scores, NEG_BIG)
    weights = jnp.exp(scores - jnp.max(scores, axis=-1, keepdims=True))
    total = jnp.sum(weights, axis=-1)
    mixed = jnp.einsum(
        "hqk,khd->hqd",
        weights.astype(jnp.bfloat16),
        values.reshape(count, heads, HD),
        preferred_element_type=jnp.float32,
    )
    return (mixed / total[..., None]).transpose(1, 0, 2).reshape(rows, width).astype(jnp.bfloat16)


def project_kernel(where_ref, first_ref, second_ref, wk_ref, wv_ref, keys_ref, values_ref):
    depth = first_ref.shape[-1]
    rows = jnp.concatenate(
        (first_ref[...].reshape(NLEN, depth), second_ref[...].reshape(NLEN, depth)), axis=0
    )
    keys_ref[...] = jnp.dot(rows, wk_ref[...], preferred_element_type=jnp.float32).astype(
        jnp.bfloat16
    )
    values_ref[...] = jnp.dot(rows, wv_ref[...], preferred_element_type=jnp.float32).astype(
        jnp.bfloat16
    )


def project_encodings(where, table, w_cross_k, w_cross_v):
    groups = where.shape[0] // (2 * NEIGH)
    _, cuts, _, piece, depth = table.shape
    width = w_cross_k.shape[1]

    def entry(neighbour):
        def index(group, where_ref):
            at = 2 * (NEIGH * group + neighbour)
            return (where_ref[at], 0, where_ref[at + 1], 0, 0)

        return pl.BlockSpec((1, cuts, 1, piece, depth), index)

    fixed = pl.BlockSpec((depth, width), lambda group, where_ref: (0, 0))
    made = pl.BlockSpec((GROUP, width), lambda group, where_ref: (group, 0))
    return pl.pallas_call(
        project_kernel,
        out_shape=[jax.ShapeDtypeStruct((groups * GROUP, width), jnp.bfloat16)] * 2,
        grid_spec=pltpu.PrefetchScalarGridSpec(
            num_scalar_prefetch=1,
            grid=(groups,),
            in_specs=[entry(0), entry(1), fixed, fixed],
            out_specs=[made, made],
        ),
        compiler_params=pltpu.CompilerParams(
            vmem_limit_bytes=VMEM_BYTES, dimension_semantics=("arbitrary",)
        ),
        cost_estimate=pl.CostEstimate(
            flops=4 * groups * GROUP * depth * width,
            bytes_accessed=2 * (groups * GROUP * (depth + 2 * width) + 2 * depth * width),
            transcendentals=0,
        ),
        name="project_encodings",
    )(where, table, table, w_cross_k, w_cross_v)


def cross_group(query, keys, values, scale):
    rows = query.shape[0]
    first = lax.broadcasted_iota(jnp.int32, (rows, 2 * HD), 1) < HD
    nothing = jnp.zeros_like(query)
    apart = jnp.concatenate(
        (jnp.where(first, query, nothing), jnp.where(first, nothing, query)), axis=0
    )
    scores = lax.dot_general(
        apart, keys, (((1,), (1,)), ((), ())), preferred_element_type=jnp.float32
    ) * (scale * LOG2E)
    weights = jnp.exp2(scores - jnp.max(scores, axis=-1, keepdims=True))
    total = jnp.sum(weights, axis=-1, keepdims=True)
    mixed = jnp.dot(weights.astype(jnp.bfloat16), values, preferred_element_type=jnp.float32)
    mixed = mixed / total
    return jnp.where(first, mixed[:rows], mixed[rows:])


def cross_kernel(live_ref, query_ref, keys_ref, values_ref, out_ref, *, spans, heads, scale):
    tail = 16
    row = lax.broadcasted_iota(jnp.int32, (tail, 2 * HD), 0)
    for span in range(spans):
        top = span * SPAN
        for pair in range(heads // 2):
            lanes = slice(2 * pair * HD, 2 * (pair + 1) * HD)
            here, after = (slice((span + k) * GROUP, (span + k + 1) * GROUP) for k in (0, 1))
            query = query_ref[top : top + SPAN, lanes]
            mixed = cross_group(query, keys_ref[here, lanes], values_ref[here, lanes], scale)
            last = cross_group(
                query[SPAN - tail :], keys_ref[after, lanes], values_ref[after, lanes], scale
            )
            if span == 0:
                mixed = jnp.where(live_ref[0] > 0, mixed, 0.0)
            last = jnp.where(row == tail - 1, last, mixed[SPAN - tail :])
            out_ref[top : top + SPAN - tail, lanes] = mixed[: SPAN - tail].astype(jnp.bfloat16)
            out_ref[top + SPAN - tail : top + SPAN, lanes] = last.astype(jnp.bfloat16)


def cross_attend(live, query, keys, values, scale):
    rows, width = query.shape
    vmem = pl.BlockSpec(memory_space=pltpu.VMEM)
    return pl.pallas_call(
        functools.partial(
            cross_kernel, spans=rows // SPAN, heads=width // HD, scale=scale
        ),
        out_shape=jax.ShapeDtypeStruct((rows, width), jnp.bfloat16),
        in_specs=[pl.BlockSpec(memory_space=pltpu.SMEM), vmem, vmem, vmem],
        out_specs=vmem,
        compiler_params=pltpu.CompilerParams(vmem_limit_bytes=VMEM_BYTES),
        cost_estimate=pl.CostEstimate(
            flops=8 * rows * GROUP * width,
            bytes_accessed=2 * (2 * rows + 2 * keys.shape[0]) * width,
            transcendentals=2 * rows * GROUP * width // HD,
        ),
        name="cross_attend",
    )(live, query, keys, values)


def per_device(
    hidden_in,
    query_rows,
    key_rows,
    value_rows,
    w_self_out,
    norm_gain,
    w_cross_q,
    w_cross_k,
    w_cross_v,
    w_cross_out,
    enc_table,
    nb_shard,
    nb_row,
):
    rows, features = hidden_in.shape
    width = query_rows.shape[1]
    heads = width // HD
    n_seq, n_db = lax.axis_size("seq"), lax.axis_size("db")
    seq_index, db_index = lax.axis_index("seq"), lax.axis_index("db")
    scale = 1.0 / math.sqrt(HD)
    share = rows // n_db

    rows_shard, _, depth = enc_table.shape
    piece = rows_shard * NLEN // n_seq
    part = lax.dynamic_slice_in_dim(
        enc_table.reshape(rows_shard * NLEN, depth), seq_index * piece, piece, 0
    )
    part, query_rows, key_rows, value_rows = lax.optimization_barrier(
        (part, query_rows, key_rows, value_rows)
    )
    along_db = lax.all_gather(part, "db", axis=0)
    wanted = jnp.stack((nb_row, nb_shard), axis=-1).astype(jnp.int32)
    before = shift(wanted[-1], "seq", 1, range(n_seq))
    where = jnp.concatenate((before[None], wanted), axis=0).reshape(-1)

    if heads == n_seq:
        attended = self_attention_by_head(query_rows, key_rows, value_rows, scale)
    else:
        attended = self_attention_gathered(query_rows, key_rows, value_rows, scale)

    along_db, attended = lax.optimization_barrier((along_db, attended))
    table = lax.all_gather(along_db, "seq", axis=0).reshape(
        rows_shard, NLEN // piece, n_db, piece, depth
    )

    partial = jnp.dot(attended, w_self_out, preferred_element_type=jnp.float32).astype(jnp.bfloat16)
    attn_share = line_reduce_scatter(partial.reshape(n_db, share, features))
    residual = (
        lax.dynamic_slice_in_dim(hidden_in, db_index * share, share, 0).astype(jnp.float32)
        + attn_share
    )
    mean_square = jnp.mean(residual * residual, axis=-1, keepdims=True)
    normed_share = (
        residual * lax.rsqrt(mean_square + 1e-05) * norm_gain.astype(jnp.float32)
    ).astype(jnp.bfloat16)
    projected = project_encodings(where, table, w_cross_k, w_cross_v)
    normed, (keys, values) = line_all_gather(normed_share, projected)
    normed = normed.reshape(rows, features)
    cross_query = jnp.dot(normed, w_cross_q, preferred_element_type=jnp.float32).astype(
        jnp.bfloat16
    )
    live = (seq_index > 0).astype(jnp.int32).reshape(1)
    mixed = cross_attend(live, cross_query, keys, values, scale)
    out_partial = jnp.dot(mixed, w_cross_out, preferred_element_type=jnp.float32).astype(
        jnp.bfloat16
    )
    return residual + line_reduce_scatter(out_partial.reshape(n_db, share, features))


def solution(mesh):
    placed = (
        P("seq", None),
        P("seq", "db"),
        P("seq", "db"),
        P("seq", "db"),
        P("db", None),
        P(),
        P(None, "db"),
        P(None, "db"),
        P(None, "db"),
        P("db", None),
        P("db", None, None),
        P("seq", None),
        P("seq", None),
    )
    return jax.shard_map(
        per_device, mesh=mesh, in_specs=placed, out_specs=P(("seq", "db"), None), check_vma=False
    )
```

```python
import functools
import math

import jax
import jax.numpy as jnp
from jax import lax
from jax.experimental import pallas as pl
from jax.experimental.pallas import tpu as pltpu
from jax.sharding import PartitionSpec as P

HD = 128
SPAN = 64
NEIGH = 2
NLEN = 128
GROUP = NEIGH * NLEN

NEG_BIG = -1e30
LOG2E = 1.4426950408889634
VMEM_BYTES = 16 * 1024 * 1024


def shift(block, axis, distance, senders):
    size = lax.axis_size(axis)
    route = [(k, k + distance) for k in senders if 0 <= k + distance < size]
    return lax.ppermute(block, axis, route)


def add_rounded(first, second):
    return (first.astype(jnp.float32) + second.astype(jnp.float32)).astype(jnp.bfloat16)


def line_reduce_scatter(blocks):
    size = lax.axis_size("db")
    me = lax.axis_index("db")

    def pick(d):
        return lax.dynamic_index_in_dim(blocks, jnp.clip(d, 0, size - 1), 0, keepdims=False)

    up = down = None
    for step in range(size - 1):
        far = size - 1 - step
        up_block, down_block = pick(me + far), pick(me - far)
        if step:
            up_block, down_block = add_rounded(up_block, up), add_rounded(down_block, down)
        up = shift(up_block, "db", 1, range(step + 1))
        down = shift(down_block, "db", -1, range(size - 1 - step, size))
        up, down = lax.optimization_barrier((up, down))
    total = pick(me).astype(jnp.float32)
    return total + up.astype(jnp.float32) + down.astype(jnp.float32)


def line_all_gather(block, beside):
    size = lax.axis_size("db")
    me = lax.axis_index("db")
    up = down = block
    pieces = []
    for step in range(size - 1):
        up = shift(up, "db", 1, range(step, size))
        down = shift(down, "db", -1, range(0, size - step))
        if step == (size - 1) // 2:
            up, down, beside = lax.optimization_barrier((up, down, beside))
        else:
            up, down = lax.optimization_barrier((up, down))
        pieces.append((step + 1, up, down))
    parts = []
    for owner in range(size):
        chosen = block
        for distance, from_low, from_high in pieces:
            chosen = jnp.where(me - owner == distance, from_low, chosen)
            chosen = jnp.where(owner - me == distance, from_high, chosen)
        parts.append(chosen)
    return jnp.stack(parts), beside


def self_kernel(qkv_ref, out_ref, *, blocks, rows, scale):
    for block in range(blocks):
        query = qkv_ref[block, 0]
        live = (block + 1) * rows
        keys = qkv_ref[0 : block + 1, 1].reshape(live, HD)
        values = qkv_ref[0 : block + 1, 2].reshape(live, HD)
        scores = lax.dot_general(
            query, keys, (((1,), (1,)), ((), ())), preferred_element_type=jnp.float32
        )
        query_pos = block * rows + lax.broadcasted_iota(jnp.int32, (rows, live), 0)
        key_pos = lax.broadcasted_iota(jnp.int32, (rows, live), 1)
        scores = jnp.where(key_pos <= query_pos, scores * (scale * LOG2E), NEG_BIG)
        top = jnp.max(scores, axis=-1, keepdims=True)
        weights = jnp.exp2(scores - top)
        total = jnp.sum(weights, axis=-1, keepdims=True)
        mixed = jnp.dot(weights.astype(jnp.bfloat16), values, preferred_element_type=jnp.float32)
        out_ref[block] = (mixed / total).astype(jnp.bfloat16)


def self_attend_head(qkv, scale):
    blocks, _, rows, _ = qkv.shape
    return pl.pallas_call(
        functools.partial(self_kernel, blocks=blocks, rows=rows, scale=scale),
        out_shape=jax.ShapeDtypeStruct((blocks, rows, HD), jnp.bfloat16),
        in_specs=[pl.BlockSpec(memory_space=pltpu.VMEM)],
        out_specs=pl.BlockSpec(memory_space=pltpu.VMEM),
        compiler_params=pltpu.CompilerParams(vmem_limit_bytes=VMEM_BYTES),
        cost_estimate=pl.CostEstimate(
            flops=2 * blocks * blocks * rows * rows * HD,
            bytes_accessed=8 * blocks * rows * HD,
            transcendentals=blocks * blocks * rows * rows // 2,
        ),
        name="self_attend",
    )(qkv)


def pack_kernel(query_ref, key_ref, value_ref, out_ref):
    for which, ref in enumerate((query_ref, key_ref, value_ref)):
        for head in range(out_ref.shape[0]):
            out_ref[head, which] = ref[:, head * HD : (head + 1) * HD]


def pack_heads(query_rows, key_rows, value_rows):
    rows, width = query_rows.shape
    heads = width // HD
    step = math.gcd(heads, 2)
    return pl.pallas_call(
        pack_kernel,
        grid=(heads // step,),
        out_shape=jax.ShapeDtypeStruct((heads, 3, rows, HD), jnp.bfloat16),
        in_specs=[pl.BlockSpec((rows, step * HD), lambda at: (0, at))] * 3,
        out_specs=pl.BlockSpec((step, 3, rows, HD), lambda at: (at, 0, 0, 0)),
        cost_estimate=pl.CostEstimate(
            flops=0, bytes_accessed=12 * rows * width, transcendentals=0
        ),
        name="pack_heads",
    )(query_rows, key_rows, value_rows)


def self_attention_by_head(query_rows, key_rows, value_rows, scale):
    rows, width = query_rows.shape
    packed = pack_heads(query_rows, key_rows, value_rows)
    held = lax.all_to_all(packed, "seq", 0, 0, tiled=True)
    mixed = self_attend_head(held, scale)
    back = lax.all_to_all(mixed, "seq", 0, 0, tiled=True)
    return back.transpose(1, 0, 2).reshape(rows, width)


def self_attention_gathered(query_rows, key_rows, value_rows, scale):
    rows, width = query_rows.shape
    heads = width // HD
    keys = lax.all_gather(key_rows, "seq", axis=0, tiled=True)
    values = lax.all_gather(value_rows, "seq", axis=0, tiled=True)
    count = keys.shape[0]
    query_pos = lax.axis_index("seq") * rows + jnp.arange(rows, dtype=jnp.int32)
    allowed = jnp.arange(count, dtype=jnp.int32)[None, :] <= query_pos[:, None]
    scores = (
        jnp.einsum(
            "qhd,khd->hqk",
            query_rows.reshape(rows, heads, HD),
            keys.reshape(count, heads, HD),
            preferred_element_type=jnp.float32,
        )
        * scale
    )
    scores = jnp.where(allowed[None], scores, NEG_BIG)
    weights = jnp.exp(scores - jnp.max(scores, axis=-1, keepdims=True))
    total = jnp.sum(weights, axis=-1)
    mixed = jnp.einsum(
        "hqk,khd->hqd",
        weights.astype(jnp.bfloat16),
        values.reshape(count, heads, HD),
        preferred_element_type=jnp.float32,
    )
    return (mixed / total[..., None]).transpose(1, 0, 2).reshape(rows, width).astype(jnp.bfloat16)


def project_kernel(where_ref, first_ref, second_ref, wk_ref, wv_ref, keys_ref, values_ref):
    depth = first_ref.shape[-1]
    rows = jnp.concatenate(
        (first_ref[...].reshape(NLEN, depth), second_ref[...].reshape(NLEN, depth)), axis=0
    )
    keys_ref[...] = jnp.dot(rows, wk_ref[...], preferred_element_type=jnp.float32).astype(
        jnp.bfloat16
    )
    values_ref[...] = jnp.dot(rows, wv_ref[...], preferred_element_type=jnp.float32).astype(
        jnp.bfloat16
    )


def project_encodings(where, table, w_cross_k, w_cross_v):
    groups = where.shape[0] // (2 * NEIGH)
    _, cuts, _, piece, depth = table.shape
    width = w_cross_k.shape[1]

    def entry(neighbour):
        def index(group, where_ref):
            at = 2 * (NEIGH * group + neighbour)
            return (where_ref[at], 0, where_ref[at + 1], 0, 0)

        return pl.BlockSpec((1, cuts, 1, piece, depth), index)

    fixed = pl.BlockSpec((depth, width), lambda group, where_ref: (0, 0))
    made = pl.BlockSpec((GROUP, width), lambda group, where_ref: (group, 0))
    return pl.pallas_call(
        project_kernel,
        out_shape=[jax.ShapeDtypeStruct((groups * GROUP, width), jnp.bfloat16)] * 2,
        grid_spec=pltpu.PrefetchScalarGridSpec(
            num_scalar_prefetch=1,
            grid=(groups,),
            in_specs=[entry(0), entry(1), fixed, fixed],
            out_specs=[made, made],
        ),
        compiler_params=pltpu.CompilerParams(
            vmem_limit_bytes=20 * 1024 * 1024, dimension_semantics=("arbitrary",)
        ),
        cost_estimate=pl.CostEstimate(
            flops=4 * groups * GROUP * depth * width,
            bytes_accessed=2 * (groups * GROUP * (depth + 2 * width) + 2 * depth * width),
            transcendentals=0,
        ),
        name="project_encodings",
    )(where, table, table, w_cross_k, w_cross_v)


def apart_heads(query):
    first = lax.broadcasted_iota(jnp.int32, query.shape, 1) < HD
    nothing = jnp.zeros_like(query)
    return jnp.concatenate(
        (jnp.where(first, query, nothing), jnp.where(first, nothing, query)), axis=0
    )


def together_heads(mixed):
    rows = mixed.shape[0] // 2
    first = lax.broadcasted_iota(jnp.int32, (rows, 2 * HD), 1) < HD
    return jnp.where(first, mixed[:rows], mixed[rows:])


def cross_kernel(live_ref, query_ref, keys_ref, values_ref, out_ref, *, spans, heads, scale):
    tail = 16
    pairs = heads // 2
    row = lax.broadcasted_iota(jnp.int32, (tail, 2 * HD), 0)
    lanes = [slice(2 * pair * HD, 2 * (pair + 1) * HD) for pair in range(pairs)]
    for span in range(spans):
        top = span * SPAN
        here, after = (slice((span + k) * GROUP, (span + k + 1) * GROUP) for k in (0, 1))
        work = [(slice(top, top + SPAN), here, at) for at in lanes]
        work += [(slice(top + SPAN - tail, top + SPAN), after, at) for at in lanes]
        scores = [
            lax.dot_general(
                apart_heads(query_ref[of, at]),
                keys_ref[group, at],
                (((1,), (1,)), ((), ())),
                preferred_element_type=jnp.float32,
            )
            * (scale * LOG2E)
            for of, group, at in work
        ]
        tops = [jnp.max(one, axis=-1, keepdims=True) for one in scores]
        weights = [jnp.exp2(one - top_one) for one, top_one in zip(scores, tops)]
        totals = [jnp.sum(one, axis=-1, keepdims=True) for one in weights]
        mixed = [
            jnp.dot(
                one.astype(jnp.bfloat16), values_ref[group, at], preferred_element_type=jnp.float32
            )
            for one, (_, group, at) in zip(weights, work)
        ]
        mixed = [together_heads(one / total) for one, total in zip(mixed, totals)]
        for pair, at in enumerate(lanes):
            main, last = mixed[pair], mixed[pairs + pair]
            if span == 0:
                main = jnp.where(live_ref[0] > 0, main, 0.0)
            last = jnp.where(row == tail - 1, last, main[SPAN - tail :])
            out_ref[top : top + SPAN - tail, at] = main[: SPAN - tail].astype(jnp.bfloat16)
            out_ref[top + SPAN - tail : top + SPAN, at] = last.astype(jnp.bfloat16)


def cross_attend(live, query, keys, values, scale):
    rows, width = query.shape
    vmem = pl.BlockSpec(memory_space=pltpu.VMEM)
    return pl.pallas_call(
        functools.partial(
            cross_kernel, spans=rows // SPAN, heads=width // HD, scale=scale
        ),
        out_shape=jax.ShapeDtypeStruct((rows, width), jnp.bfloat16),
        in_specs=[pl.BlockSpec(memory_space=pltpu.SMEM), vmem, vmem, vmem],
        out_specs=vmem,
        compiler_params=pltpu.CompilerParams(vmem_limit_bytes=VMEM_BYTES),
        cost_estimate=pl.CostEstimate(
            flops=8 * rows * GROUP * width,
            bytes_accessed=2 * (2 * rows + 2 * keys.shape[0]) * width,
            transcendentals=2 * rows * GROUP * width // HD,
        ),
        name="cross_attend",
    )(live, query, keys, values)


def per_device(
    hidden_in,
    query_rows,
    key_rows,
    value_rows,
    w_self_out,
    norm_gain,
    w_cross_q,
    w_cross_k,
    w_cross_v,
    w_cross_out,
    enc_table,
    nb_shard,
    nb_row,
):
    rows, features = hidden_in.shape
    width = query_rows.shape[1]
    heads = width // HD
    n_seq, n_db = lax.axis_size("seq"), lax.axis_size("db")
    seq_index, db_index = lax.axis_index("seq"), lax.axis_index("db")
    scale = 1.0 / math.sqrt(HD)
    share = rows // n_db

    rows_shard, _, depth = enc_table.shape
    piece = rows_shard * NLEN // n_seq
    part = lax.dynamic_slice_in_dim(
        enc_table.reshape(rows_shard * NLEN, depth), seq_index * piece, piece, 0
    )
    part, query_rows, key_rows, value_rows = lax.optimization_barrier(
        (part, query_rows, key_rows, value_rows)
    )
    along_db = lax.all_gather(part, "db", axis=0)
    wanted = jnp.stack((nb_row, nb_shard), axis=-1).astype(jnp.int32)
    before = shift(wanted[-1], "seq", 1, range(n_seq))
    where = jnp.concatenate((before[None], wanted), axis=0).reshape(-1)

    if heads == n_seq:
        attended = self_attention_by_head(query_rows, key_rows, value_rows, scale)
    else:
        attended = self_attention_gathered(query_rows, key_rows, value_rows, scale)

    along_db, attended = lax.optimization_barrier((along_db, attended))
    table = lax.all_gather(along_db, "seq", axis=0).reshape(
        rows_shard, NLEN // piece, n_db, piece, depth
    )

    partial = jnp.dot(attended, w_self_out, preferred_element_type=jnp.float32).astype(jnp.bfloat16)
    attn_share = line_reduce_scatter(partial.reshape(n_db, share, features))
    residual = (
        lax.dynamic_slice_in_dim(hidden_in, db_index * share, share, 0).astype(jnp.float32)
        + attn_share
    )
    mean_square = jnp.mean(residual * residual, axis=-1, keepdims=True)
    normed_share = (
        residual * lax.rsqrt(mean_square + 1e-05) * norm_gain.astype(jnp.float32)
    ).astype(jnp.bfloat16)
    projected = project_encodings(where, table, w_cross_k, w_cross_v)
    normed, (keys, values) = line_all_gather(normed_share, projected)
    normed = normed.reshape(rows, features)
    cross_query = jnp.dot(normed, w_cross_q, preferred_element_type=jnp.float32).astype(
        jnp.bfloat16
    )
    live = (seq_index > 0).astype(jnp.int32).reshape(1)
    mixed = cross_attend(live, cross_query, keys, values, scale)
    out_partial = jnp.dot(mixed, w_cross_out, preferred_element_type=jnp.float32).astype(
        jnp.bfloat16
    )
    return residual + line_reduce_scatter(out_partial.reshape(n_db, share, features))


def solution(mesh):
    placed = (
        P("seq", None),
        P("seq", "db"),
        P("seq", "db"),
        P("seq", "db"),
        P("db", None),
        P(),
        P(None, "db"),
        P(None, "db"),
        P(None, "db"),
        P("db", None),
        P("db", None, None),
        P("seq", None),
        P("seq", None),
    )
    return jax.shard_map(
        per_device, mesh=mesh, in_specs=placed, out_specs=P(("seq", "db"), None), check_vma=False
    )
```

```python
import functools
import math

import jax
import jax.numpy as jnp
from jax import lax
from jax.experimental import pallas as pl
from jax.experimental.pallas import tpu as pltpu
from jax.sharding import PartitionSpec as P

HD = 128
SPAN = 64
NEIGH = 2
NLEN = 128
GROUP = NEIGH * NLEN

NEG_BIG = -1e30
LOG2E = 1.4426950408889634
VMEM_BYTES = 16 * 1024 * 1024


def shift(block, axis, distance, senders):
    size = lax.axis_size(axis)
    route = [(k, k + distance) for k in senders if 0 <= k + distance < size]
    return lax.ppermute(block, axis, route)


def add_rounded(first, second):
    return (first.astype(jnp.float32) + second.astype(jnp.float32)).astype(jnp.bfloat16)


def pick(blocks, index):
    return lax.dynamic_index_in_dim(
        blocks, jnp.clip(index, 0, blocks.shape[0] - 1), 0, keepdims=False
    )


def reduce_step(blocks, carried, step):
    size = lax.axis_size("db")
    me = lax.axis_index("db")
    far = size - 1 - step
    up_block, down_block = pick(blocks, me + far), pick(blocks, me - far)
    if carried is not None:
        up_block = add_rounded(up_block, carried[0])
        down_block = add_rounded(down_block, carried[1])
    return (
        shift(up_block, "db", 1, range(step + 1)),
        shift(down_block, "db", -1, range(size - 1 - step, size)),
    )


def reduced(blocks, carried):
    total = pick(blocks, lax.axis_index("db")).astype(jnp.float32)
    return total + carried[0].astype(jnp.float32) + carried[1].astype(jnp.float32)


def gather_step(carried, step):
    size = lax.axis_size("db")
    return (
        shift(carried[0], "db", 1, range(step, size)),
        shift(carried[1], "db", -1, range(0, size - step)),
    )


def gather_reduce(normed, blocks, beside, at):
    size = lax.axis_size("db")
    carried_gather, carried_reduce, pieces = (normed, normed), None, []
    for step in range(size):
        if step < size - 1:
            carried_gather = gather_step(carried_gather, step)
        if step:
            carried_reduce = reduce_step(blocks, carried_reduce, step - 1)
        held = (
            carried_gather if step < size - 1 else None,
            carried_reduce,
            blocks if step == 0 else None,
            beside if step == at else None,
        )
        held = lax.optimization_barrier(held)
        if step < size - 1:
            carried_gather = held[0]
            pieces.append(held[0])
        carried_reduce = held[1]
        if step == 0:
            blocks = held[2]
        if step == at:
            beside = held[3]
    return pieces, blocks, carried_reduce, beside


def self_kernel(qkv_ref, out_ref, *, blocks, rows, scale):
    for block in range(blocks):
        query = qkv_ref[block, 0]
        live = (block + 1) * rows
        keys = qkv_ref[0 : block + 1, 1].reshape(live, HD)
        values = qkv_ref[0 : block + 1, 2].reshape(live, HD)
        scores = lax.dot_general(
            query, keys, (((1,), (1,)), ((), ())), preferred_element_type=jnp.float32
        )
        query_pos = block * rows + lax.broadcasted_iota(jnp.int32, (rows, live), 0)
        key_pos = lax.broadcasted_iota(jnp.int32, (rows, live), 1)
        scores = jnp.where(key_pos <= query_pos, scores * (scale * LOG2E), NEG_BIG)
        top = jnp.max(scores, axis=-1, keepdims=True)
        weights = jnp.exp2(scores - top)
        total = jnp.sum(weights, axis=-1, keepdims=True)
        mixed = jnp.dot(weights.astype(jnp.bfloat16), values, preferred_element_type=jnp.float32)
        out_ref[block] = (mixed / total).astype(jnp.bfloat16)


def self_attend_head(qkv, scale):
    blocks, _, rows, _ = qkv.shape
    return pl.pallas_call(
        functools.partial(self_kernel, blocks=blocks, rows=rows, scale=scale),
        out_shape=jax.ShapeDtypeStruct((blocks, rows, HD), jnp.bfloat16),
        in_specs=[pl.BlockSpec(memory_space=pltpu.VMEM)],
        out_specs=pl.BlockSpec(memory_space=pltpu.VMEM),
        compiler_params=pltpu.CompilerParams(vmem_limit_bytes=VMEM_BYTES),
        cost_estimate=pl.CostEstimate(
            flops=2 * blocks * blocks * rows * rows * HD,
            bytes_accessed=8 * blocks * rows * HD,
            transcendentals=blocks * blocks * rows * rows // 2,
        ),
        name="self_attend",
    )(qkv)


def pack_kernel(query_ref, key_ref, value_ref, out_ref):
    for which, ref in enumerate((query_ref, key_ref, value_ref)):
        for head in range(out_ref.shape[0]):
            out_ref[head, which] = ref[:, head * HD : (head + 1) * HD]


def pack_heads(query_rows, key_rows, value_rows):
    rows, width = query_rows.shape
    heads = width // HD
    step = math.gcd(heads, 2)
    return pl.pallas_call(
        pack_kernel,
        grid=(heads // step,),
        out_shape=jax.ShapeDtypeStruct((heads, 3, rows, HD), jnp.bfloat16),
        in_specs=[pl.BlockSpec((rows, step * HD), lambda at: (0, at))] * 3,
        out_specs=pl.BlockSpec((step, 3, rows, HD), lambda at: (at, 0, 0, 0)),
        cost_estimate=pl.CostEstimate(
            flops=0, bytes_accessed=12 * rows * width, transcendentals=0
        ),
        name="pack_heads",
    )(query_rows, key_rows, value_rows)


def self_attention_by_head(query_rows, key_rows, value_rows, scale):
    packed = pack_heads(query_rows, key_rows, value_rows)
    held = lax.all_to_all(packed, "seq", 0, 0, tiled=True)
    mixed = self_attend_head(held, scale)
    return lax.all_to_all(mixed, "seq", 0, 0, tiled=True)


def self_attention_gathered(query_rows, key_rows, value_rows, scale):
    rows, width = query_rows.shape
    heads = width // HD
    keys = lax.all_gather(key_rows, "seq", axis=0, tiled=True)
    values = lax.all_gather(value_rows, "seq", axis=0, tiled=True)
    count = keys.shape[0]
    query_pos = lax.axis_index("seq") * rows + jnp.arange(rows, dtype=jnp.int32)
    allowed = jnp.arange(count, dtype=jnp.int32)[None, :] <= query_pos[:, None]
    scores = (
        jnp.einsum(
            "qhd,khd->hqk",
            query_rows.reshape(rows, heads, HD),
            keys.reshape(count, heads, HD),
            preferred_element_type=jnp.float32,
        )
        * scale
    )
    scores = jnp.where(allowed[None], scores, NEG_BIG)
    weights = jnp.exp(scores - jnp.max(scores, axis=-1, keepdims=True))
    total = jnp.sum(weights, axis=-1)
    mixed = jnp.einsum(
        "hqk,khd->hqd",
        weights.astype(jnp.bfloat16),
        values.reshape(count, heads, HD),
        preferred_element_type=jnp.float32,
    )
    return (mixed / total[..., None]).astype(jnp.bfloat16)


def self_out_kernel(attended_ref, weight_ref, first_ref, second_ref, rows_ref):
    heads, rows, _ = attended_ref.shape
    n_db, half, features = first_ref.shape
    for chunk in range(2):
        for owner in range(n_db):
            source = (2 * owner + chunk) * half
            target = (chunk * n_db + owner) * half
            for head in range(heads):
                rows_ref[target : target + half, head * HD : (head + 1) * HD] = attended_ref[
                    head, source : source + half, :
                ]
    step = math.gcd(features, 512)

    def columns(at, carried):
        here = pl.ds(pl.multiple_of(at * step, step), step)
        product = jnp.dot(rows_ref[...], weight_ref[:, here], preferred_element_type=jnp.float32)
        product = product.astype(jnp.bfloat16)
        for owner in range(n_db):
            first_ref[owner, :, here] = product[owner * half : (owner + 1) * half]
            second_ref[owner, :, here] = product[(n_db + owner) * half : (n_db + owner + 1) * half]
        return carried

    lax.fori_loop(0, features // step, columns, 0)


def self_out(attended, weight, n_db):
    heads, rows, _ = attended.shape
    width, features = weight.shape
    half = rows // n_db // 2
    vmem = pl.BlockSpec(memory_space=pltpu.VMEM)
    return pl.pallas_call(
        self_out_kernel,
        out_shape=[jax.ShapeDtypeStruct((n_db, half, features), jnp.bfloat16)] * 2,
        in_specs=[vmem, vmem],
        out_specs=[vmem, vmem],
        scratch_shapes=[pltpu.VMEM((rows, width), jnp.bfloat16)],
        compiler_params=pltpu.CompilerParams(vmem_limit_bytes=VMEM_BYTES),
        cost_estimate=pl.CostEstimate(
            flops=2 * rows * width * features,
            bytes_accessed=2 * (rows * width + width * features + rows * features),
            transcendentals=0,
        ),
        name="self_out",
    )(attended, weight)


def project_kernel(where_ref, first_ref, second_ref, wk_ref, wv_ref, keys_ref, values_ref):
    depth = first_ref.shape[-1]
    rows = jnp.concatenate(
        (first_ref[...].reshape(NLEN, depth), second_ref[...].reshape(NLEN, depth)), axis=0
    )
    keys_ref[...] = jnp.dot(rows, wk_ref[...], preferred_element_type=jnp.float32).astype(
        jnp.bfloat16
    )
    values_ref[...] = jnp.dot(rows, wv_ref[...], preferred_element_type=jnp.float32).astype(
        jnp.bfloat16
    )


def project_encodings(where, table, w_cross_k, w_cross_v):
    groups = where.shape[0] // (2 * NEIGH)
    _, _, _, piece, depth = table.shape
    cuts = NLEN // piece
    assert cuts in (1, 2)
    width = w_cross_k.shape[1]

    def entry(neighbour):
        def index(group, where_ref):
            at = 2 * (NEIGH * group + neighbour)
            row, shard = where_ref[at], where_ref[at + 1]
            if cuts == 2:
                return (0, row, shard, 0, 0)
            return (lax.rem(row, 2), lax.div(row, 2), shard, 0, 0)

        return pl.BlockSpec((cuts, 1, 1, piece, depth), index)

    fixed = pl.BlockSpec((depth, width), lambda group, where_ref: (0, 0))
    made = pl.BlockSpec((GROUP, width), lambda group, where_ref: (group, 0))
    return pl.pallas_call(
        project_kernel,
        out_shape=[jax.ShapeDtypeStruct((groups * GROUP, width), jnp.bfloat16)] * 2,
        grid_spec=pltpu.PrefetchScalarGridSpec(
            num_scalar_prefetch=1,
            grid=(groups,),
            in_specs=[entry(0), entry(1), fixed, fixed],
            out_specs=[made, made],
        ),
        compiler_params=pltpu.CompilerParams(
            vmem_limit_bytes=20 * 1024 * 1024, dimension_semantics=("arbitrary",)
        ),
        cost_estimate=pl.CostEstimate(
            flops=4 * groups * GROUP * depth * width,
            bytes_accessed=2 * (groups * GROUP * (depth + 2 * width) + 2 * depth * width),
            transcendentals=0,
        ),
        name="project_encodings",
    )(where, table, table, w_cross_k, w_cross_v)


def apart_heads(query):
    first = lax.broadcasted_iota(jnp.int32, query.shape, 1) < HD
    nothing = jnp.zeros_like(query)
    return jnp.concatenate(
        (jnp.where(first, query, nothing), jnp.where(first, nothing, query)), axis=0
    )


def together_heads(mixed):
    rows = mixed.shape[0] // 2
    first = lax.broadcasted_iota(jnp.int32, (rows, 2 * HD), 1) < HD
    return jnp.where(first, mixed[:rows], mixed[rows:])


def cross_kernel(place_ref, *refs, chunk, scale):
    out_ref, rows_ref, mixed_ref = refs[-3:]
    wq_ref, keys_ref, values_ref, wo_ref = refs[-7:-3]
    own_ref, pieces = refs[0], refs[1:-7]
    n_db, half, features = out_ref.shape
    heads = wq_ref.shape[1] // HD
    pairs = heads // 2
    tail = 16
    for me in range(n_db):

        @pl.when(place_ref[0] == me)
        def _(me=me):
            for owner in range(n_db):
                if owner == me:
                    source = own_ref
                elif owner < me:
                    source = pieces[2 * (me - owner - 1)]
                else:
                    source = pieces[2 * (owner - me - 1) + 1]
                rows_ref[owner * half : (owner + 1) * half, :] = source[...]

    row = lax.broadcasted_iota(jnp.int32, (tail, 2 * HD), 0)
    lanes = [slice(2 * pair * HD, 2 * (pair + 1) * HD) for pair in range(pairs)]
    queries = [
        jnp.dot(rows_ref[...], wq_ref[:, at], preferred_element_type=jnp.float32).astype(
            jnp.bfloat16
        )
        for at in lanes
    ]
    for owner in range(n_db):
        top = owner * half
        place = (2 * owner + chunk) * half
        group = place // SPAN
        ends = (place + half) % SPAN == 0
        here, after = (slice((group + k) * GROUP, (group + k + 1) * GROUP) for k in (0, 1))
        work = [(query[top : top + half], here, at) for query, at in zip(queries, lanes)]
        if ends:
            work += [
                (query[top + half - tail : top + half], after, at)
                for query, at in zip(queries, lanes)
            ]
        scores = [
            lax.dot_general(
                apart_heads(query),
                keys_ref[which, at],
                (((1,), (1,)), ((), ())),
                preferred_element_type=jnp.float32,
            )
            * (scale * LOG2E)
            for query, which, at in work
        ]
        tops = [jnp.max(one, axis=-1, keepdims=True) for one in scores]
        weights = [jnp.exp2(one - top_one) for one, top_one in zip(scores, tops)]
        totals = [jnp.sum(one, axis=-1, keepdims=True) for one in weights]
        mixed = [
            jnp.dot(
                one.astype(jnp.bfloat16), values_ref[which, at], preferred_element_type=jnp.float32
            )
            for one, (_, which, at) in zip(weights, work)
        ]
        mixed = [together_heads(one / total) for one, total in zip(mixed, totals)]
        for pair, at in enumerate(lanes):
            main = mixed[pair]
            if group == 0:
                main = jnp.where(place_ref[1] > 0, main, 0.0)
            if ends:
                last = jnp.where(row == tail - 1, mixed[pairs + pair], main[half - tail :])
                if half > tail:
                    mixed_ref[top : top + half - tail, at] = main[: half - tail].astype(
                        jnp.bfloat16
                    )
                mixed_ref[top + half - tail : top + half, at] = last.astype(jnp.bfloat16)
            else:
                mixed_ref[top : top + half, at] = main.astype(jnp.bfloat16)

    step = math.gcd(features, 512)

    def columns(at, carried):
        here = pl.ds(pl.multiple_of(at * step, step), step)
        product = jnp.dot(mixed_ref[...], wo_ref[:, here], preferred_element_type=jnp.float32)
        product = product.astype(jnp.bfloat16)
        for owner in range(n_db):
            out_ref[owner, :, here] = product[owner * half : (owner + 1) * half]
        return carried

    lax.fori_loop(0, features // step, columns, 0)


def cross_chunk(chunk, place, normed, pieces, w_cross_q, keys, values, w_cross_out, n_db, scale):
    half, features = normed.shape
    width = w_cross_q.shape[1]
    rows = n_db * half
    vmem = pl.BlockSpec(memory_space=pltpu.VMEM)
    flat = [one for pair in pieces for one in pair]
    return pl.pallas_call(
        functools.partial(cross_kernel, chunk=chunk, scale=scale),
        out_shape=jax.ShapeDtypeStruct((n_db, half, features), jnp.bfloat16),
        in_specs=[pl.BlockSpec(memory_space=pltpu.SMEM)] + [vmem] * (5 + len(flat)),
        out_specs=vmem,
        scratch_shapes=[
            pltpu.VMEM((rows, features), jnp.bfloat16),
            pltpu.VMEM((rows, width), jnp.bfloat16),
        ],
        compiler_params=pltpu.CompilerParams(vmem_limit_bytes=VMEM_BYTES),
        cost_estimate=pl.CostEstimate(
            flops=4 * rows * width * (features + GROUP),
            bytes_accessed=4 * width * (features + keys.shape[0]) + 4 * rows * features,
            transcendentals=rows * GROUP * width // HD,
        ),
        name="cross_chunk",
    )(place, normed, *flat, w_cross_q, keys, values, w_cross_out)


def per_device(
    hidden_in,
    query_rows,
    key_rows,
    value_rows,
    w_self_out,
    norm_gain,
    w_cross_q,
    w_cross_k,
    w_cross_v,
    w_cross_out,
    enc_table,
    nb_shard,
    nb_row,
):
    rows = hidden_in.shape[0]
    heads = query_rows.shape[1] // HD
    n_seq, n_db = lax.axis_size("seq"), lax.axis_size("db")
    seq_index, db_index = lax.axis_index("seq"), lax.axis_index("db")
    scale = 1.0 / math.sqrt(HD)
    half = rows // n_db // 2

    rows_shard, _, depth = enc_table.shape
    piece = rows_shard * NLEN // n_seq
    part = lax.dynamic_slice_in_dim(
        enc_table.reshape(rows_shard * NLEN, depth), seq_index * piece, piece, 0
    )
    part, query_rows, key_rows, value_rows = lax.optimization_barrier(
        (part, query_rows, key_rows, value_rows)
    )
    along_db = lax.all_gather(part, "db", axis=0)
    cores = [list(range(core, n_seq, 2)) for core in range(2)]
    chips = [[chip, chip + 1] for chip in range(0, n_seq, 2)]
    of_core = lax.all_gather(along_db, "seq", axis=0, axis_index_groups=cores)
    table = lax.all_gather(of_core, "seq", axis=0, axis_index_groups=chips)
    wanted = jnp.stack((nb_row, nb_shard), axis=-1).astype(jnp.int32)
    before = shift(wanted[-1], "seq", 1, range(n_seq))
    where = jnp.concatenate((before[None], wanted), axis=0).reshape(-1)
    place = jnp.stack((db_index, (seq_index > 0).astype(jnp.int32))).astype(jnp.int32)

    if heads == n_seq:
        attended = self_attention_by_head(query_rows, key_rows, value_rows, scale)
    else:
        attended = self_attention_gathered(query_rows, key_rows, value_rows, scale)
    attended, where = lax.optimization_barrier((attended, where))

    gain = norm_gain.astype(jnp.float32)

    def finish_norm(chunk, blocks, carried):
        own = lax.dynamic_slice_in_dim(hidden_in, (2 * db_index + chunk) * half, half, 0)
        residual = own.astype(jnp.float32) + reduced(blocks, carried)
        mean_square = jnp.mean(residual * residual, axis=-1, keepdims=True)
        return residual, (residual * lax.rsqrt(mean_square + 1e-05) * gain).astype(jnp.bfloat16)

    def cross(chunk, normed, pieces, keys, values):
        return cross_chunk(
            chunk, place, normed, pieces, w_cross_q, keys, values, w_cross_out, n_db, scale
        )

    first, second = self_out(attended, w_self_out, n_db)
    carried = None
    for step in range(n_db - 1):
        carried = lax.optimization_barrier(reduce_step(first, carried, step))
    residual_first, normed_first = finish_norm(0, first, carried)

    projected = project_encodings(where, table, w_cross_k, w_cross_v)
    pieces, second, carried, (keys, values) = gather_reduce(
        normed_first, second, projected, n_db - 2
    )
    out_first = cross(0, normed_first, pieces, keys, values)
    residual_second, normed_second = finish_norm(1, second, carried)

    pieces, out_first, carried, _ = gather_reduce(normed_second, out_first, None, 0)
    out_second = cross(1, normed_second, pieces, keys, values)
    block_first = residual_first + reduced(out_first, carried)

    carried = None
    for step in range(n_db - 1):
        carried = lax.optimization_barrier(reduce_step(out_second, carried, step))
    block_second = residual_second + reduced(out_second, carried)
    return jnp.concatenate((block_first, block_second), axis=0)


def solution(mesh):
    placed = (
        P("seq", None),
        P("seq", "db"),
        P("seq", "db"),
        P("seq", "db"),
        P("db", None),
        P(),
        P(None, "db"),
        P(None, "db"),
        P(None, "db"),
        P("db", None),
        P("db", None, None),
        P("seq", None),
        P("seq", None),
    )
    return jax.shard_map(
        per_device, mesh=mesh, in_specs=placed, out_specs=P(("seq", "db"), None), check_vma=False
    )
```

```python
import functools
import math

import jax
import jax.numpy as jnp
from jax import lax
from jax.experimental import pallas as pl
from jax.experimental.pallas import tpu as pltpu
from jax.sharding import PartitionSpec as P

HD = 128
SPAN = 64
NEIGH = 2
NLEN = 128
GROUP = NEIGH * NLEN

NEG_BIG = -1e30
LOG2E = 1.4426950408889634
VMEM_BYTES = 48 * 1024 * 1024


def shift(block, axis, distance, senders):
    size = lax.axis_size(axis)
    route = [(k, k + distance) for k in senders if 0 <= k + distance < size]
    return lax.ppermute(block, axis, route)


def add_rounded(first, second):
    return (first.astype(jnp.float32) + second.astype(jnp.float32)).astype(jnp.bfloat16)


def pick(blocks, index):
    return lax.dynamic_index_in_dim(
        blocks, jnp.clip(index, 0, blocks.shape[0] - 1), 0, keepdims=False
    )


def reduce_step(blocks, carried, step):
    size = lax.axis_size("db")
    me = lax.axis_index("db")
    far = size - 1 - step
    up_block, down_block = pick(blocks, me + far), pick(blocks, me - far)
    if carried is not None:
        up_block = add_rounded(up_block, carried[0])
        down_block = add_rounded(down_block, carried[1])
    return (
        shift(up_block, "db", 1, range(step + 1)),
        shift(down_block, "db", -1, range(size - 1 - step, size)),
    )


def reduced(blocks, carried):
    total = pick(blocks, lax.axis_index("db")).astype(jnp.float32)
    return total + carried[0].astype(jnp.float32) + carried[1].astype(jnp.float32)


def gather_step(carried, step):
    size = lax.axis_size("db")
    return (
        shift(carried[0], "db", 1, range(step, size)),
        shift(carried[1], "db", -1, range(0, size - step)),
    )


def reduce_scatter(blocks):
    carried = None
    for step in range(lax.axis_size("db") - 1):
        carried = lax.optimization_barrier(reduce_step(blocks, carried, step))
    return reduced(blocks, carried)


def gather(block, beside):
    size = lax.axis_size("db")
    carried, pieces = (block, block), []
    for step in range(size - 1):
        carried = gather_step(carried, step)
        if step == (size - 1) // 2:
            carried, beside = lax.optimization_barrier((carried, beside))
        else:
            carried = lax.optimization_barrier(carried)
        pieces.append(carried)
    return pieces, beside


def self_kernel(qkv_ref, out_ref, *, blocks, rows, scale):
    for block in range(blocks):
        query = qkv_ref[block, 0]
        live = (block + 1) * rows
        keys = qkv_ref[0 : block + 1, 1].reshape(live, HD)
        values = qkv_ref[0 : block + 1, 2].reshape(live, HD)
        scores = lax.dot_general(
            query, keys, (((1,), (1,)), ((), ())), preferred_element_type=jnp.float32
        )
        query_pos = block * rows + lax.broadcasted_iota(jnp.int32, (rows, live), 0)
        key_pos = lax.broadcasted_iota(jnp.int32, (rows, live), 1)
        scores = jnp.where(key_pos <= query_pos, scores * (scale * LOG2E), NEG_BIG)
        top = jnp.max(scores, axis=-1, keepdims=True)
        weights = jnp.exp2(scores - top)
        total = jnp.sum(weights, axis=-1, keepdims=True)
        mixed = jnp.dot(weights.astype(jnp.bfloat16), values, preferred_element_type=jnp.float32)
        out_ref[block] = (mixed / total).astype(jnp.bfloat16)


def self_attend_head(qkv, scale):
    blocks, _, rows, _ = qkv.shape
    return pl.pallas_call(
        functools.partial(self_kernel, blocks=blocks, rows=rows, scale=scale),
        out_shape=jax.ShapeDtypeStruct((blocks, rows, HD), jnp.bfloat16),
        in_specs=[pl.BlockSpec(memory_space=pltpu.VMEM)],
        out_specs=pl.BlockSpec(memory_space=pltpu.VMEM),
        compiler_params=pltpu.CompilerParams(vmem_limit_bytes=VMEM_BYTES),
        cost_estimate=pl.CostEstimate(
            flops=2 * blocks * blocks * rows * rows * HD,
            bytes_accessed=8 * blocks * rows * HD,
            transcendentals=blocks * blocks * rows * rows // 2,
        ),
        name="self_attend",
    )(qkv)


def span_before(wanted):
    return shift(wanted[-1], "seq", 1, range(lax.axis_size("seq")))


def pack_kernel(query_ref, key_ref, value_ref, out_ref):
    for which, ref in enumerate((query_ref, key_ref, value_ref)):
        for head in range(out_ref.shape[0]):
            out_ref[head, which] = ref[:, head * HD : (head + 1) * HD]


def pack_heads(query_rows, key_rows, value_rows):
    rows, width = query_rows.shape
    heads = width // HD
    step = math.gcd(heads, 2)
    return pl.pallas_call(
        pack_kernel,
        grid=(heads // step,),
        out_shape=jax.ShapeDtypeStruct((heads, 3, rows, HD), jnp.bfloat16),
        in_specs=[pl.BlockSpec((rows, step * HD), lambda at: (0, at))] * 3,
        out_specs=pl.BlockSpec((step, 3, rows, HD), lambda at: (at, 0, 0, 0)),
        cost_estimate=pl.CostEstimate(
            flops=0, bytes_accessed=12 * rows * width, transcendentals=0
        ),
        name="pack_heads",
    )(query_rows, key_rows, value_rows)


def self_attention_by_head(query_rows, key_rows, value_rows, wanted, scale):
    packed, wanted = lax.optimization_barrier((pack_heads(query_rows, key_rows, value_rows), wanted))
    held, before = lax.optimization_barrier(
        (lax.all_to_all(packed, "seq", 0, 0, tiled=True), span_before(wanted))
    )
    mixed = self_attend_head(held, scale)
    return lax.all_to_all(mixed, "seq", 0, 0, tiled=True), before


def self_attention_gathered(query_rows, key_rows, value_rows, scale):
    rows, width = query_rows.shape
    heads = width // HD
    keys = lax.all_gather(key_rows, "seq", axis=0, tiled=True)
    values = lax.all_gather(value_rows, "seq", axis=0, tiled=True)
    count = keys.shape[0]
    query_pos = lax.axis_index("seq") * rows + jnp.arange(rows, dtype=jnp.int32)
    allowed = jnp.arange(count, dtype=jnp.int32)[None, :] <= query_pos[:, None]
    scores = (
        jnp.einsum(
            "qhd,khd->hqk",
            query_rows.reshape(rows, heads, HD),
            keys.reshape(count, heads, HD),
            preferred_element_type=jnp.float32,
        )
        * scale
    )
    scores = jnp.where(allowed[None], scores, NEG_BIG)
    weights = jnp.exp(scores - jnp.max(scores, axis=-1, keepdims=True))
    total = jnp.sum(weights, axis=-1)
    mixed = jnp.einsum(
        "hqk,khd->hqd",
        weights.astype(jnp.bfloat16),
        values.reshape(count, heads, HD),
        preferred_element_type=jnp.float32,
    )
    return (mixed / total[..., None]).astype(jnp.bfloat16)


def self_out_kernel(attended_ref, weight_ref, out_ref, rows_ref):
    @pl.when(pl.program_id(0) == 0)
    def _():
        for head in range(attended_ref.shape[0]):
            rows_ref[:, head * HD : (head + 1) * HD] = attended_ref[head]

    product = jnp.dot(rows_ref[...], weight_ref[...], preferred_element_type=jnp.float32)
    out_ref[...] = product.astype(jnp.bfloat16)


def self_out(attended, weight):
    heads, rows, _ = attended.shape
    width, features = weight.shape
    step = math.gcd(features, 512)
    return pl.pallas_call(
        self_out_kernel,
        grid=(features // step,),
        out_shape=jax.ShapeDtypeStruct((rows, features), jnp.bfloat16),
        in_specs=[
            pl.BlockSpec((heads, rows, HD), lambda at: (0, 0, 0)),
            pl.BlockSpec((width, step), lambda at: (0, at)),
        ],
        out_specs=pl.BlockSpec((rows, step), lambda at: (0, at)),
        scratch_shapes=[pltpu.VMEM((rows, width), jnp.bfloat16)],
        compiler_params=pltpu.CompilerParams(vmem_limit_bytes=VMEM_BYTES),
        cost_estimate=pl.CostEstimate(
            flops=2 * rows * width * features,
            bytes_accessed=2 * (rows * width + width * features + rows * features),
            transcendentals=0,
        ),
        name="self_out",
    )(attended, weight)


def project_kernel(where_ref, first_ref, second_ref, wk_ref, wv_ref, keys_ref, values_ref):
    depth = first_ref.shape[-1]
    rows = jnp.concatenate(
        (first_ref[...].reshape(NLEN, depth), second_ref[...].reshape(NLEN, depth)), axis=0
    )
    keys_ref[...] = jnp.dot(rows, wk_ref[...], preferred_element_type=jnp.float32).astype(
        jnp.bfloat16
    )
    values_ref[...] = jnp.dot(rows, wv_ref[...], preferred_element_type=jnp.float32).astype(
        jnp.bfloat16
    )


def project_encodings(where, table, w_cross_k, w_cross_v):
    groups = where.shape[0] // (2 * NEIGH)
    _, cuts, _, piece, depth = table.shape
    width = w_cross_k.shape[1]

    def entry(neighbour):
        def index(group, where_ref):
            at = 2 * (NEIGH * group + neighbour)
            return (where_ref[at], 0, where_ref[at + 1], 0, 0)

        return pl.BlockSpec((1, cuts, 1, piece, depth), index)

    fixed = pl.BlockSpec((depth, width), lambda group, where_ref: (0, 0))
    made = pl.BlockSpec((GROUP, width), lambda group, where_ref: (group, 0))
    return pl.pallas_call(
        project_kernel,
        out_shape=[jax.ShapeDtypeStruct((groups * GROUP, width), jnp.bfloat16)] * 2,
        grid_spec=pltpu.PrefetchScalarGridSpec(
            num_scalar_prefetch=1,
            grid=(groups,),
            in_specs=[entry(0), entry(1), fixed, fixed],
            out_specs=[made, made],
        ),
        compiler_params=pltpu.CompilerParams(
            vmem_limit_bytes=VMEM_BYTES, dimension_semantics=("arbitrary",)
        ),
        cost_estimate=pl.CostEstimate(
            flops=4 * groups * GROUP * depth * width,
            bytes_accessed=2 * (groups * GROUP * (depth + 2 * width) + 2 * depth * width),
            transcendentals=0,
        ),
        name="project_encodings",
    )(where, table, table, w_cross_k, w_cross_v)


def apart_heads(query):
    first = lax.broadcasted_iota(jnp.int32, query.shape, 1) < HD
    nothing = jnp.zeros_like(query)
    return jnp.concatenate(
        (jnp.where(first, query, nothing), jnp.where(first, nothing, query)), axis=0
    )


def together_heads(mixed):
    rows = mixed.shape[0] // 2
    first = lax.broadcasted_iota(jnp.int32, (rows, 2 * HD), 1) < HD
    return jnp.where(first, mixed[:rows], mixed[rows:])


def cross_kernel(place_ref, own_ref, *refs, scale):
    wq_hbm, keys_hbm, values_hbm, wo_hbm, out_ref = refs[-13:-8]
    wq_ref, keys_ref, values_ref, wo_ref, rows_ref, query_ref, mixed_ref, sems = refs[-8:]
    pieces = refs[:-13]
    share, features = own_ref.shape
    width = wq_ref.shape[1]
    n_db = out_ref.shape[0]
    pairs = width // HD // 2
    tail = 16
    cut = features // 4
    low = width // 4
    wq_copies = [
        pltpu.make_async_copy(
            wq_hbm.at[pl.ds(k * cut, cut)], wq_ref.at[pl.ds(k * cut, cut)], sems.at[k]
        )
        for k in range(4)
    ]
    other_copies = [
        pltpu.make_async_copy(keys_hbm, keys_ref, sems.at[4]),
        pltpu.make_async_copy(values_hbm, values_ref, sems.at[5]),
    ] + [
        pltpu.make_async_copy(
            wo_hbm.at[pl.ds(k * low, low)], wo_ref.at[pl.ds(k * low, low)], sems.at[6 + k]
        )
        for k in range(4)
    ]
    for copy in wq_copies + other_copies:
        copy.start()
    for me in range(n_db):

        @pl.when(place_ref[0] == me)
        def _(me=me):
            for owner in range(n_db):
                if owner == me:
                    source = own_ref
                elif owner < me:
                    source = pieces[2 * (me - owner - 1)]
                else:
                    source = pieces[2 * (owner - me - 1) + 1]
                rows_ref[owner * share : (owner + 1) * share, :] = source[...]

    lanes = [slice(2 * pair * HD, 2 * (pair + 1) * HD) for pair in range(pairs)]
    for k, copy in enumerate(wq_copies):
        copy.wait()
        inner = slice(k * cut, (k + 1) * cut)
        for at in lanes:
            part = jnp.dot(
                rows_ref[:, inner], wq_ref[inner, at], preferred_element_type=jnp.float32
            )
            query_ref[:, at] = part if k == 0 else query_ref[:, at] + part
    for copy in other_copies[:2]:
        copy.wait()
    row = lax.broadcasted_iota(jnp.int32, (tail, 2 * HD), 0)
    spans = n_db * share // SPAN
    for span in range(spans):
        top = span * SPAN
        here, after = (slice((span + k) * GROUP, (span + k + 1) * GROUP) for k in (0, 1))
        work = [(slice(top, top + SPAN), here, at) for at in lanes]
        work += [(slice(top + SPAN - tail, top + SPAN), after, at) for at in lanes]
        scores = [
            lax.dot_general(
                apart_heads(query_ref[of, at].astype(jnp.bfloat16)),
                keys_ref[which, at],
                (((1,), (1,)), ((), ())),
                preferred_element_type=jnp.float32,
            )
            * (scale * LOG2E)
            for of, which, at in work
        ]
        tops = [jnp.max(one, axis=-1, keepdims=True) for one in scores]
        weights = [jnp.exp2(one - top_one) for one, top_one in zip(scores, tops)]
        totals = [jnp.sum(one, axis=-1, keepdims=True) for one in weights]
        mixed = [
            jnp.dot(
                one.astype(jnp.bfloat16), values_ref[which, at], preferred_element_type=jnp.float32
            )
            for one, (_, which, at) in zip(weights, work)
        ]
        mixed = [together_heads(one / total) for one, total in zip(mixed, totals)]
        for pair, at in enumerate(lanes):
            main, last = mixed[pair], mixed[pairs + pair]
            if span == 0:
                main = jnp.where(place_ref[1] > 0, main, 0.0)
            last = jnp.where(row == tail - 1, last, main[SPAN - tail :])
            mixed_ref[top : top + SPAN - tail, at] = main[: SPAN - tail].astype(jnp.bfloat16)
            mixed_ref[top + SPAN - tail : top + SPAN, at] = last.astype(jnp.bfloat16)
    for copy in other_copies[2:]:
        copy.wait()
    step = math.gcd(features, 512)

    def columns(at, carried):
        here = pl.ds(pl.multiple_of(at * step, step), step)
        product = jnp.dot(mixed_ref[...], wo_ref[:, here], preferred_element_type=jnp.float32)
        product = product.astype(jnp.bfloat16)
        for owner in range(n_db):
            out_ref[owner, :, here] = product[owner * share : (owner + 1) * share]
        return carried

    lax.fori_loop(0, features // step, columns, 0)


def cross_block(place, normed, pieces, w_cross_q, keys, values, w_cross_out, n_db, scale):
    share, features = normed.shape
    width = w_cross_q.shape[1]
    rows = n_db * share
    vmem = pl.BlockSpec(memory_space=pltpu.VMEM)
    anywhere = pl.BlockSpec(memory_space=pl.ANY)
    flat = [one for pair in pieces for one in pair]
    return pl.pallas_call(
        functools.partial(cross_kernel, scale=scale),
        out_shape=jax.ShapeDtypeStruct((n_db, share, features), jnp.bfloat16),
        in_specs=[pl.BlockSpec(memory_space=pltpu.SMEM)]
        + [vmem] * (1 + len(flat))
        + [anywhere] * 4,
        out_specs=vmem,
        scratch_shapes=[
            pltpu.VMEM((features, width), jnp.bfloat16),
            pltpu.VMEM(keys.shape, jnp.bfloat16),
            pltpu.VMEM(values.shape, jnp.bfloat16),
            pltpu.VMEM((width, features), jnp.bfloat16),
            pltpu.VMEM((rows, features), jnp.bfloat16),
            pltpu.VMEM((rows, width), jnp.float32),
            pltpu.VMEM((rows, width), jnp.bfloat16),
            pltpu.SemaphoreType.DMA((10,)),
        ],
        compiler_params=pltpu.CompilerParams(vmem_limit_bytes=VMEM_BYTES),
        cost_estimate=pl.CostEstimate(
            flops=4 * rows * width * (features + GROUP),
            bytes_accessed=4 * width * (features + keys.shape[0]) + 4 * rows * features,
            transcendentals=rows * GROUP * width // HD,
        ),
        name="cross_block",
    )(place, normed, *flat, w_cross_q, keys, values, w_cross_out)


def per_device(
    hidden_in,
    query_rows,
    key_rows,
    value_rows,
    w_self_out,
    norm_gain,
    w_cross_q,
    w_cross_k,
    w_cross_v,
    w_cross_out,
    enc_table,
    nb_shard,
    nb_row,
):
    rows, features = hidden_in.shape
    heads = query_rows.shape[1] // HD
    n_seq, n_db = lax.axis_size("seq"), lax.axis_size("db")
    seq_index, db_index = lax.axis_index("seq"), lax.axis_index("db")
    scale = 1.0 / math.sqrt(HD)
    share = rows // n_db

    rows_shard, _, depth = enc_table.shape
    piece = rows_shard * NLEN // n_seq
    part = lax.dynamic_slice_in_dim(
        enc_table.reshape(rows_shard * NLEN, depth), seq_index * piece, piece, 0
    )
    part, query_rows, key_rows, value_rows = lax.optimization_barrier(
        (part, query_rows, key_rows, value_rows)
    )
    along_db = lax.all_gather(part, "db", axis=0)
    wanted = jnp.stack((nb_row, nb_shard), axis=-1).astype(jnp.int32)
    place = jnp.stack((db_index, (seq_index > 0).astype(jnp.int32))).astype(jnp.int32)

    if heads == n_seq:
        attended, before = self_attention_by_head(query_rows, key_rows, value_rows, wanted, scale)
    else:
        attended = self_attention_gathered(query_rows, key_rows, value_rows, scale)
        before = span_before(wanted)
    where = jnp.concatenate((before[None], wanted), axis=0).reshape(-1)

    along_db, attended = lax.optimization_barrier((along_db, attended))
    table = lax.all_gather(along_db, "seq", axis=0).reshape(
        rows_shard, NLEN // piece, n_db, piece, depth
    )

    partial = self_out(attended, w_self_out).reshape(n_db, share, features)
    own = lax.dynamic_slice_in_dim(hidden_in, db_index * share, share, 0)
    residual = own.astype(jnp.float32) + reduce_scatter(partial)
    mean_square = jnp.mean(residual * residual, axis=-1, keepdims=True)
    normed = (
        residual * lax.rsqrt(mean_square + 1e-05) * norm_gain.astype(jnp.float32)
    ).astype(jnp.bfloat16)
    projected = project_encodings(where, table, w_cross_k, w_cross_v)
    pieces, (keys, values) = gather(normed, projected)
    out_partial = cross_block(
        place, normed, pieces, w_cross_q, keys, values, w_cross_out, n_db, scale
    )
    return residual + reduce_scatter(out_partial)


def solution(mesh):
    placed = (
        P("seq", None),
        P("seq", "db"),
        P("seq", "db"),
        P("seq", "db"),
        P("db", None),
        P(),
        P(None, "db"),
        P(None, "db"),
        P(None, "db"),
        P("db", None),
        P("db", None, None),
        P("seq", None),
        P("seq", None),
    )
    return jax.shard_map(
        per_device, mesh=mesh, in_specs=placed, out_specs=P(("seq", "db"), None), check_vma=False
    )
```

```python
import functools
import math

import jax
import jax.numpy as jnp
from jax import lax
from jax.experimental import pallas as pl
from jax.experimental.pallas import tpu as pltpu
from jax.sharding import PartitionSpec as P

HD = 128
SPAN = 64
NEIGH = 2
NLEN = 128
GROUP = NEIGH * NLEN

NEG_BIG = -1e30
LOG2E = 1.4426950408889634
VMEM_BYTES = 14 * 1024 * 1024


def shift(block, axis, distance, senders):
    size = lax.axis_size(axis)
    route = [(k, k + distance) for k in senders if 0 <= k + distance < size]
    return lax.ppermute(block, axis, route)


def add_rounded(first, second):
    return (first.astype(jnp.float32) + second.astype(jnp.float32)).astype(jnp.bfloat16)


def pick(blocks, index):
    return lax.dynamic_index_in_dim(
        blocks, jnp.clip(index, 0, blocks.shape[0] - 1), 0, keepdims=False
    )


def reduce_step(blocks, carried, step):
    size = lax.axis_size("db")
    me = lax.axis_index("db")
    far = size - 1 - step
    up_block, down_block = pick(blocks, me + far), pick(blocks, me - far)
    if carried is not None:
        up_block = add_rounded(up_block, carried[0])
        down_block = add_rounded(down_block, carried[1])
    return (
        shift(up_block, "db", 1, range(step + 1)),
        shift(down_block, "db", -1, range(size - 1 - step, size)),
    )


def reduced(blocks, carried):
    total = pick(blocks, lax.axis_index("db")).astype(jnp.float32)
    return total + carried[0].astype(jnp.float32) + carried[1].astype(jnp.float32)


def reduce_scatter(blocks):
    carried = None
    for step in range(lax.axis_size("db") - 1):
        carried = lax.optimization_barrier(reduce_step(blocks, carried, step))
    return reduced(blocks, carried)


def plane_swap(block, masks):
    return lax.ppermute(block, "seq", [(i, i ^ masks[i & 1]) for i in range(8)])


def plane_pieces(mine, near):
    swap = plane_swap
    four = (mine, near, swap(mine, (4, 2)), swap(near, (4, 2)))
    four = lax.optimization_barrier(four)
    return four + tuple(swap(one, (1, 1)) for one in four)


def plane_slot(owner, me):
    apart = owner ^ me
    core, x, y = apart & 1, (apart >> 1) & 1, apart >> 2
    return 4 * core + jnp.where((owner & 1) == 0, x + 2 * y, y + 2 * x)


def self_kernel(qkv_ref, weight_hbm, out_ref, weight_ref, sem, *, blocks, rows, scale):
    bring = pltpu.make_async_copy(weight_hbm, weight_ref, sem)
    bring.start()
    for block in range(blocks):
        query = qkv_ref[block, 0]
        live = (block + 1) * rows
        keys = qkv_ref[0 : block + 1, 1].reshape(live, HD)
        values = qkv_ref[0 : block + 1, 2].reshape(live, HD)
        scores = lax.dot_general(
            query, keys, (((1,), (1,)), ((), ())), preferred_element_type=jnp.float32
        )
        query_pos = block * rows + lax.broadcasted_iota(jnp.int32, (rows, live), 0)
        key_pos = lax.broadcasted_iota(jnp.int32, (rows, live), 1)
        scores = jnp.where(key_pos <= query_pos, scores * (scale * LOG2E), NEG_BIG)
        top = jnp.max(scores, axis=-1, keepdims=True)
        weights = jnp.exp2(scores - top)
        total = jnp.sum(weights, axis=-1, keepdims=True)
        mixed = jnp.dot(weights.astype(jnp.bfloat16), values, preferred_element_type=jnp.float32)
        out_ref[block] = (mixed / total).astype(jnp.bfloat16)
    bring.wait()


def self_attend_head(qkv, weight, scale):
    blocks, _, rows, _ = qkv.shape
    vmem = pl.BlockSpec(memory_space=pltpu.VMEM)
    return pl.pallas_call(
        functools.partial(self_kernel, blocks=blocks, rows=rows, scale=scale),
        out_shape=[
            jax.ShapeDtypeStruct((blocks, rows, HD), jnp.bfloat16),
            jax.ShapeDtypeStruct(weight.shape, weight.dtype),
        ],
        in_specs=[vmem, pl.BlockSpec(memory_space=pl.ANY)],
        out_specs=[vmem, vmem],
        scratch_shapes=[pltpu.SemaphoreType.DMA],
        compiler_params=pltpu.CompilerParams(vmem_limit_bytes=VMEM_BYTES),
        cost_estimate=pl.CostEstimate(
            flops=2 * blocks * blocks * rows * rows * HD,
            bytes_accessed=8 * blocks * rows * HD + 2 * weight.size,
            transcendentals=blocks * blocks * rows * rows // 2,
        ),
        name="self_attend",
    )(qkv, weight)


def span_before(wanted):
    return shift(wanted[-1], "seq", 1, range(lax.axis_size("seq")))


def pack_kernel(query_ref, key_ref, value_ref, out_ref):
    for which, ref in enumerate((query_ref, key_ref, value_ref)):
        for head in range(out_ref.shape[0]):
            out_ref[head, which] = ref[:, head * HD : (head + 1) * HD]


def pack_heads(query_rows, key_rows, value_rows):
    rows, width = query_rows.shape
    heads = width // HD
    step = math.gcd(heads, 2)
    return pl.pallas_call(
        pack_kernel,
        grid=(heads // step,),
        out_shape=jax.ShapeDtypeStruct((heads, 3, rows, HD), jnp.bfloat16),
        in_specs=[pl.BlockSpec((rows, step * HD), lambda at: (0, at))] * 3,
        out_specs=pl.BlockSpec((step, 3, rows, HD), lambda at: (at, 0, 0, 0)),
        cost_estimate=pl.CostEstimate(
            flops=0, bytes_accessed=12 * rows * width, transcendentals=0
        ),
        name="pack_heads",
    )(query_rows, key_rows, value_rows)


def self_attention_by_head(query_rows, key_rows, value_rows, wanted, weight, scale):
    packed, wanted = lax.optimization_barrier((pack_heads(query_rows, key_rows, value_rows), wanted))
    held, before = lax.optimization_barrier(
        (lax.all_to_all(packed, "seq", 0, 0, tiled=True), span_before(wanted))
    )
    mixed, weight = self_attend_head(held, weight, scale)
    return lax.all_to_all(mixed, "seq", 0, 0, tiled=True), before, weight


def self_attention_gathered(query_rows, key_rows, value_rows, scale):
    rows, width = query_rows.shape
    heads = width // HD
    keys = lax.all_gather(key_rows, "seq", axis=0, tiled=True)
    values = lax.all_gather(value_rows, "seq", axis=0, tiled=True)
    count = keys.shape[0]
    query_pos = lax.axis_index("seq") * rows + jnp.arange(rows, dtype=jnp.int32)
    allowed = jnp.arange(count, dtype=jnp.int32)[None, :] <= query_pos[:, None]
    scores = (
        jnp.einsum(
            "qhd,khd->hqk",
            query_rows.reshape(rows, heads, HD),
            keys.reshape(count, heads, HD),
            preferred_element_type=jnp.float32,
        )
        * scale
    )
    scores = jnp.where(allowed[None], scores, NEG_BIG)
    weights = jnp.exp(scores - jnp.max(scores, axis=-1, keepdims=True))
    total = jnp.sum(weights, axis=-1)
    mixed = jnp.einsum(
        "hqk,khd->hqd",
        weights.astype(jnp.bfloat16),
        values.reshape(count, heads, HD),
        preferred_element_type=jnp.float32,
    )
    return (mixed / total[..., None]).astype(jnp.bfloat16)


def self_out_kernel(attended_ref, weight_ref, out_ref, rows_ref):
    for head in range(attended_ref.shape[0]):
        rows_ref[:, head * HD : (head + 1) * HD] = attended_ref[head]
    features = out_ref.shape[1]
    step = math.gcd(features, 512)

    def columns(at, carried):
        here = pl.ds(pl.multiple_of(at * step, step), step)
        product = jnp.dot(rows_ref[...], weight_ref[:, here], preferred_element_type=jnp.float32)
        out_ref[:, here] = product.astype(jnp.bfloat16)
        return carried

    lax.fori_loop(0, features // step, columns, 0)


def self_out(attended, weight):
    heads, rows, _ = attended.shape
    width, features = weight.shape
    vmem = pl.BlockSpec(memory_space=pltpu.VMEM)
    return pl.pallas_call(
        self_out_kernel,
        out_shape=jax.ShapeDtypeStruct((rows, features), jnp.bfloat16),
        in_specs=[vmem, vmem],
        out_specs=vmem,
        scratch_shapes=[pltpu.VMEM((rows, width), jnp.bfloat16)],
        compiler_params=pltpu.CompilerParams(vmem_limit_bytes=VMEM_BYTES),
        cost_estimate=pl.CostEstimate(
            flops=2 * rows * width * features,
            bytes_accessed=2 * (rows * width + width * features + rows * features),
            transcendentals=0,
        ),
        name="self_out",
    )(attended, weight)


def project_kernel(where_ref, *refs, cuts):
    wk_hbm, wv_hbm, wq_hbm, wo_hbm, keys_ref, values_ref, wq_ref, wo_ref = refs[-12:-4]
    rows_ref, wk_ref, wv_ref, sems = refs[-4:]
    tables = refs[:-12]
    entries = keys_ref.shape[0] // NLEN
    piece = NLEN // cuts
    bring = [
        pltpu.make_async_copy(source, target, sems.at[entries * cuts + at])
        for at, (source, target) in enumerate(
            ((wk_hbm, wk_ref), (wv_hbm, wv_ref), (wq_hbm, wq_ref), (wo_hbm, wo_ref))
        )
    ]
    for copy in bring[:2]:
        copy.start()

    def entry_copy(entry, cut, table, first, shard):
        return pltpu.make_async_copy(
            table.at[first + cut, shard],
            rows_ref.at[pl.ds(entry * NLEN + cut * piece, piece)],
            sems.at[entry * cuts + cut],
        )

    for entry in range(entries):
        for slot, table in enumerate(tables):

            @pl.when(where_ref[3 * entry] == slot)
            def _(entry=entry, table=table):
                for cut in range(cuts):
                    entry_copy(
                        entry, cut, table, where_ref[3 * entry + 1], where_ref[3 * entry + 2]
                    ).start()

    for copy in bring[2:]:
        copy.start()
    for copy in bring[:2]:
        copy.wait()
    width = keys_ref.shape[1]
    step = math.gcd(width, 512)
    for group in range(entries // NEIGH):
        for entry in range(NEIGH * group, NEIGH * (group + 1)):
            for cut in range(cuts):
                entry_copy(entry, cut, tables[0], 0, 0).wait()
        here = slice(group * GROUP, (group + 1) * GROUP)
        for at in range(0, width, step):
            lanes = slice(at, at + step)
            for weight, made in ((wk_ref, keys_ref), (wv_ref, values_ref)):
                made[here, lanes] = jnp.dot(
                    rows_ref[here, :], weight[:, lanes], preferred_element_type=jnp.float32
                ).astype(jnp.bfloat16)
    for copy in bring[2:]:
        copy.wait()


def project_encodings(where, tables, w_cross_k, w_cross_v, w_cross_q, w_cross_out):
    entries = where.shape[0] // 3
    piece, depth = tables[0].shape[2:]
    cuts = NLEN // piece
    width = w_cross_k.shape[1]
    vmem = pl.BlockSpec(memory_space=pltpu.VMEM)
    anywhere = pl.BlockSpec(memory_space=pl.ANY)
    made = jax.ShapeDtypeStruct((entries * NLEN, width), jnp.bfloat16)
    return pl.pallas_call(
        functools.partial(project_kernel, cuts=cuts),
        out_shape=[made, made]
        + [jax.ShapeDtypeStruct(one.shape, one.dtype) for one in (w_cross_q, w_cross_out)],
        in_specs=[pl.BlockSpec(memory_space=pltpu.SMEM)] + [anywhere] * (len(tables) + 4),
        out_specs=[vmem] * 4,
        scratch_shapes=[
            pltpu.VMEM((entries * NLEN, depth), jnp.bfloat16),
            pltpu.VMEM(w_cross_k.shape, jnp.bfloat16),
            pltpu.VMEM(w_cross_v.shape, jnp.bfloat16),
            pltpu.SemaphoreType.DMA((entries * cuts + 4,)),
        ],
        compiler_params=pltpu.CompilerParams(vmem_limit_bytes=VMEM_BYTES),
        cost_estimate=pl.CostEstimate(
            flops=entries * NLEN * depth,
            bytes_accessed=2 * entries * NLEN * depth,
            transcendentals=0,
        ),
        name="project_encodings",
    )(where, *tables, w_cross_k, w_cross_v, w_cross_q, w_cross_out)


def apart_heads(query):
    first = lax.broadcasted_iota(jnp.int32, query.shape, 1) < HD
    nothing = jnp.zeros_like(query)
    return jnp.concatenate(
        (jnp.where(first, query, nothing), jnp.where(first, nothing, query)), axis=0
    )


def together_heads(mixed):
    rows = mixed.shape[0] // 2
    first = lax.broadcasted_iota(jnp.int32, (rows, 2 * HD), 1) < HD
    return jnp.where(first, mixed[:rows], mixed[rows:])


def cross_kernel(
    place_ref,
    hidden_ref,
    total_ref,
    gain_ref,
    wq_ref,
    keys_ref,
    values_ref,
    wo_ref,
    out_ref,
    residual_ref,
    rows_ref,
    query_ref,
    mixed_ref,
    *,
    scale,
):
    rows, features = hidden_ref.shape
    n_db, share, _ = out_ref.shape
    pairs = wq_ref.shape[1] // HD // 2
    tail = 16
    block = math.gcd(rows, 32)

    def norm(at, carried):
        here = pl.ds(pl.multiple_of(at * block, block), block)
        residual = hidden_ref[here, :].astype(jnp.float32) + total_ref[here, :].astype(jnp.float32)
        mean_square = jnp.mean(residual * residual, axis=-1, keepdims=True)
        rows_ref[here, :] = (
            residual * lax.rsqrt(mean_square + 1e-05) * gain_ref[...].astype(jnp.float32)
        ).astype(jnp.bfloat16)
        return carried

    lax.fori_loop(0, rows // block, norm, 0)
    own = pl.ds(pl.multiple_of(place_ref[0] * share, share), share)
    residual_ref[...] = hidden_ref[own, :].astype(jnp.float32) + total_ref[own, :].astype(
        jnp.float32
    )
    lanes = [slice(2 * pair * HD, 2 * (pair + 1) * HD) for pair in range(pairs)]
    for at in lanes:
        query_ref[:, at] = jnp.dot(
            rows_ref[...], wq_ref[:, at], preferred_element_type=jnp.float32
        ).astype(jnp.bfloat16)
    row = lax.broadcasted_iota(jnp.int32, (tail, 2 * HD), 0)
    spans = rows // SPAN
    for span in range(spans):
        top = span * SPAN
        here, after = (slice((span + k) * GROUP, (span + k + 1) * GROUP) for k in (0, 1))
        work = [(slice(top, top + SPAN), here, at) for at in lanes]
        work += [(slice(top + SPAN - tail, top + SPAN), after, at) for at in lanes]
        scores = [
            lax.dot_general(
                apart_heads(query_ref[of, at]),
                keys_ref[which, at],
                (((1,), (1,)), ((), ())),
                preferred_element_type=jnp.float32,
            )
            * (scale * LOG2E)
            for of, which, at in work
        ]
        tops = [jnp.max(one, axis=-1, keepdims=True) for one in scores]
        weights = [jnp.exp2(one - top_one) for one, top_one in zip(scores, tops)]
        totals = [jnp.sum(one, axis=-1, keepdims=True) for one in weights]
        mixed = [
            jnp.dot(
                one.astype(jnp.bfloat16), values_ref[which, at], preferred_element_type=jnp.float32
            )
            for one, (_, which, at) in zip(weights, work)
        ]
        mixed = [together_heads(one / total) for one, total in zip(mixed, totals)]
        for pair, at in enumerate(lanes):
            main, last = mixed[pair], mixed[pairs + pair]
            if span == 0:
                main = jnp.where(place_ref[1] > 0, main, 0.0)
            last = jnp.where(row == tail - 1, last, main[SPAN - tail :])
            mixed_ref[top : top + SPAN - tail, at] = main[: SPAN - tail].astype(jnp.bfloat16)
            mixed_ref[top + SPAN - tail : top + SPAN, at] = last.astype(jnp.bfloat16)
    step = math.gcd(features, 512)

    def columns(at, carried):
        here = pl.ds(pl.multiple_of(at * step, step), step)
        product = jnp.dot(mixed_ref[...], wo_ref[:, here], preferred_element_type=jnp.float32)
        product = product.astype(jnp.bfloat16)
        for owner in range(n_db):
            out_ref[owner, :, here] = product[owner * share : (owner + 1) * share]
        return carried

    lax.fori_loop(0, features // step, columns, 0)


def cross_block(place, hidden, total, gain, w_cross_q, keys, values, w_cross_out, n_db, scale):
    rows, features = hidden.shape
    share = rows // n_db
    width = w_cross_q.shape[1]
    vmem = pl.BlockSpec(memory_space=pltpu.VMEM)
    return pl.pallas_call(
        functools.partial(cross_kernel, scale=scale),
        out_shape=[
            jax.ShapeDtypeStruct((n_db, share, features), jnp.bfloat16),
            jax.ShapeDtypeStruct((share, features), jnp.float32),
        ],
        in_specs=[pl.BlockSpec(memory_space=pltpu.SMEM)] + [vmem] * 7,
        out_specs=[vmem, vmem],
        scratch_shapes=[
            pltpu.VMEM((rows, features), jnp.bfloat16),
            pltpu.VMEM((rows, width), jnp.bfloat16),
            pltpu.VMEM((rows, width), jnp.bfloat16),
        ],
        compiler_params=pltpu.CompilerParams(vmem_limit_bytes=VMEM_BYTES),
        cost_estimate=pl.CostEstimate(
            flops=4 * rows * width * (features + GROUP),
            bytes_accessed=4 * width * (features + keys.shape[0]) + 8 * rows * features,
            transcendentals=rows * GROUP * width // HD,
        ),
        name="cross_block",
    )(place, hidden, total, gain, w_cross_q, keys, values, w_cross_out)


def per_device(
    hidden_in,
    query_rows,
    key_rows,
    value_rows,
    w_self_out,
    norm_gain,
    w_cross_q,
    w_cross_k,
    w_cross_v,
    w_cross_out,
    enc_table,
    nb_shard,
    nb_row,
):
    rows, features = hidden_in.shape
    heads = query_rows.shape[1] // HD
    n_seq, n_db = lax.axis_size("seq"), lax.axis_size("db")
    seq_index, db_index = lax.axis_index("seq"), lax.axis_index("db")
    scale = 1.0 / math.sqrt(HD)

    rows_shard, _, depth = enc_table.shape
    piece = rows_shard * NLEN // n_seq
    part = lax.dynamic_slice_in_dim(
        enc_table.reshape(rows_shard * NLEN, depth), seq_index * piece, piece, 0
    )
    part, query_rows, key_rows, value_rows = lax.optimization_barrier(
        (part, query_rows, key_rows, value_rows)
    )
    along_db = lax.all_gather(part, "db", axis=0)
    wanted = jnp.stack((nb_row, nb_shard), axis=-1).astype(jnp.int32)
    place = jnp.stack((db_index, (seq_index > 0).astype(jnp.int32))).astype(jnp.int32)

    by_head = heads == n_seq
    if by_head:
        attended, before, w_self_out = self_attention_by_head(
            query_rows, key_rows, value_rows, wanted, w_self_out, scale
        )
    else:
        attended = self_attention_gathered(query_rows, key_rows, value_rows, scale)
        before = span_before(wanted)

    in_plane = n_seq == 8 and piece == NLEN
    along_db, attended = lax.optimization_barrier((along_db, attended))
    partial = self_out(attended, w_self_out)
    if in_plane:
        along_db = (along_db, plane_swap(along_db, (2, 4)))
    along_db, partial = lax.optimization_barrier((along_db, partial))
    total = lax.psum(partial, "db")

    nearest = jnp.concatenate((before[None], wanted), axis=0)
    row, shard = nearest[..., 0], nearest[..., 1]
    if in_plane:
        tables = tuple(one[None] for one in plane_pieces(*along_db))
        where = jnp.stack((plane_slot(row, seq_index), jnp.zeros_like(row), shard), axis=-1)
    else:
        tables = (lax.all_gather(along_db, "seq", axis=0),)
        where = jnp.stack((jnp.zeros_like(row), row * (NLEN // piece), shard), axis=-1)
    projected = project_encodings(
        where.astype(jnp.int32).reshape(-1), tables, w_cross_k, w_cross_v, w_cross_q, w_cross_out
    )
    total, (keys, values, w_cross_q, w_cross_out) = lax.optimization_barrier((total, projected))
    out_partial, residual = cross_block(
        place,
        hidden_in,
        total,
        norm_gain.reshape(1, features),
        w_cross_q,
        keys,
        values,
        w_cross_out,
        n_db,
        scale,
    )
    return residual + reduce_scatter(out_partial)


def solution(mesh):
    placed = (
        P("seq", None),
        P("seq", "db"),
        P("seq", "db"),
        P("seq", "db"),
        P("db", None),
        P(),
        P(None, "db"),
        P(None, "db"),
        P(None, "db"),
        P("db", None),
        P("db", None, None),
        P("seq", None),
        P("seq", None),
    )
    return jax.shard_map(
        per_device, mesh=mesh, in_specs=placed, out_specs=P(("seq", "db"), None), check_vma=False
    )
```

```python
import functools
import math

import jax
import jax.numpy as jnp
from jax import lax
from jax.experimental import pallas as pl
from jax.experimental.pallas import tpu as pltpu
from jax.sharding import PartitionSpec as P

HD = 128
SPAN = 64
NEIGH = 2
NLEN = 128
GROUP = NEIGH * NLEN

NEG_BIG = -1e30
LOG2E = 1.4426950408889634
VMEM_BYTES = 48 * 1024 * 1024
MIDDLE_BYTES = 36 * 1024 * 1024
BLOCK_BYTES = 14 * 1024 * 1024
SMALL_BYTES = 4 * 1024 * 1024


def shift(block, axis, distance, senders):
    size = lax.axis_size(axis)
    route = [(k, k + distance) for k in senders if 0 <= k + distance < size]
    return lax.ppermute(block, axis, route)


def far_blocks(blocks_ref, me, far):
    last = blocks_ref.shape[0] - 1
    return jnp.minimum(me + far, last), jnp.maximum(me - far, 0)


def add_kernel(info_ref, blocks_ref, up_ref, down_ref, up_out_ref, down_out_ref, *, far):
    above, below = far_blocks(blocks_ref, info_ref[0], far)
    rows = 16

    def add(at, carried):
        here = pl.ds(pl.multiple_of(at * rows, rows), rows)
        for index, ref, out_ref in ((above, up_ref, up_out_ref), (below, down_ref, down_out_ref)):
            out_ref[here, :] = (
                blocks_ref[index, here, :].astype(jnp.float32) + ref[here, :].astype(jnp.float32)
            ).astype(jnp.bfloat16)
        return carried

    lax.fori_loop(0, up_ref.shape[0] // rows, add, 0)


def add_step(info, blocks, up, down, far):
    vmem = pl.BlockSpec(memory_space=pltpu.VMEM)
    one = jax.ShapeDtypeStruct(up.shape, up.dtype)
    return pl.pallas_call(
        functools.partial(add_kernel, far=far),
        out_shape=[one, one],
        in_specs=[pl.BlockSpec(memory_space=pltpu.SMEM), vmem, vmem, vmem],
        out_specs=[vmem, vmem],
        compiler_params=pltpu.CompilerParams(vmem_limit_bytes=SMALL_BYTES),
        cost_estimate=pl.CostEstimate(
            flops=2 * up.size, bytes_accessed=12 * up.size, transcendentals=0
        ),
        name="add_step",
    )(info, blocks, up, down)


def reduce_scatter(info, blocks, up, down):
    size = lax.axis_size("db")
    for step in range(size - 1):
        if step:
            up, down = add_step(info, blocks, up, down, size - 1 - step)
        up = shift(up, "db", 1, range(step + 1))
        down = shift(down, "db", -1, range(size - 1 - step, size))
        up, down = lax.optimization_barrier((up, down))
    return up, down


def gather_step(carried, step):
    size = lax.axis_size("db")
    return (
        shift(carried[0], "db", 1, range(step, size)),
        shift(carried[1], "db", -1, range(0, size - step)),
    )


def gather(block, beside):
    size = lax.axis_size("db")
    carried, pieces = (block, block), []
    for step in range(size - 1):
        carried = gather_step(carried, step)
        if step == (size - 1) // 2:
            carried, beside = lax.optimization_barrier((carried, beside))
        else:
            carried = lax.optimization_barrier(carried)
        pieces.append(carried)
    return pieces, beside


def self_kernel(qkv_ref, out_ref, *, blocks, rows, scale):
    for block in range(blocks):
        query = qkv_ref[block, 0]
        live = (block + 1) * rows
        keys = qkv_ref[0 : block + 1, 1].reshape(live, HD)
        values = qkv_ref[0 : block + 1, 2].reshape(live, HD)
        scores = lax.dot_general(
            query, keys, (((1,), (1,)), ((), ())), preferred_element_type=jnp.float32
        )
        query_pos = block * rows + lax.broadcasted_iota(jnp.int32, (rows, live), 0)
        key_pos = lax.broadcasted_iota(jnp.int32, (rows, live), 1)
        scores = jnp.where(key_pos <= query_pos, scores * (scale * LOG2E), NEG_BIG)
        top = jnp.max(scores, axis=-1, keepdims=True)
        weights = jnp.exp2(scores - top)
        total = jnp.sum(weights, axis=-1, keepdims=True)
        mixed = jnp.dot(weights.astype(jnp.bfloat16), values, preferred_element_type=jnp.float32)
        out_ref[block] = (mixed / total).astype(jnp.bfloat16)


def self_attend_head(qkv, scale):
    blocks, _, rows, _ = qkv.shape
    return pl.pallas_call(
        functools.partial(self_kernel, blocks=blocks, rows=rows, scale=scale),
        out_shape=jax.ShapeDtypeStruct((blocks, rows, HD), jnp.bfloat16),
        in_specs=[pl.BlockSpec(memory_space=pltpu.VMEM)],
        out_specs=pl.BlockSpec(memory_space=pltpu.VMEM),
        compiler_params=pltpu.CompilerParams(vmem_limit_bytes=VMEM_BYTES),
        cost_estimate=pl.CostEstimate(
            flops=2 * blocks * blocks * rows * rows * HD,
            bytes_accessed=8 * blocks * rows * HD,
            transcendentals=blocks * blocks * rows * rows // 2,
        ),
        name="self_attend",
    )(qkv)


def span_before(wanted):
    return shift(wanted[-1], "seq", 1, range(lax.axis_size("seq")))


def pack_kernel(index_ref, query_ref, key_ref, value_ref, part_ref, out_ref, part_out_ref):
    for which, ref in enumerate((query_ref, key_ref, value_ref)):
        for head in range(out_ref.shape[0]):
            out_ref[head, which] = ref[:, head * HD : (head + 1) * HD]
    part_out_ref[...] = part_ref[...]


def pack_heads(index, query_rows, key_rows, value_rows, encodings, piece):
    rows, width = query_rows.shape
    heads = width // HD
    depth = encodings.shape[1]
    steps = 4
    block, part = rows // steps, piece // steps
    row_block = pl.BlockSpec((block, width), lambda at, index_ref: (at, 0))
    return pl.pallas_call(
        pack_kernel,
        out_shape=[
            jax.ShapeDtypeStruct((heads, 3, rows, HD), jnp.bfloat16),
            jax.ShapeDtypeStruct((piece, depth), jnp.bfloat16),
        ],
        grid_spec=pltpu.PrefetchScalarGridSpec(
            num_scalar_prefetch=1,
            grid=(steps,),
            in_specs=[row_block] * 3
            + [pl.BlockSpec((part, depth), lambda at, index_ref: (index_ref[0] * steps + at, 0))],
            out_specs=[
                pl.BlockSpec((heads, 3, block, HD), lambda at, index_ref: (0, 0, at, 0)),
                pl.BlockSpec((part, depth), lambda at, index_ref: (at, 0)),
            ],
        ),
        compiler_params=pltpu.CompilerParams(
            vmem_limit_bytes=VMEM_BYTES, dimension_semantics=("arbitrary",)
        ),
        cost_estimate=pl.CostEstimate(
            flops=0, bytes_accessed=12 * rows * width, transcendentals=0
        ),
        name="pack_heads",
    )(index, query_rows, key_rows, value_rows, encodings)


def self_attention_gathered(query_rows, key_rows, value_rows, scale):
    rows, width = query_rows.shape
    heads = width // HD
    keys = lax.all_gather(key_rows, "seq", axis=0, tiled=True)
    values = lax.all_gather(value_rows, "seq", axis=0, tiled=True)
    count = keys.shape[0]
    query_pos = lax.axis_index("seq") * rows + jnp.arange(rows, dtype=jnp.int32)
    allowed = jnp.arange(count, dtype=jnp.int32)[None, :] <= query_pos[:, None]
    scores = (
        jnp.einsum(
            "qhd,khd->hqk",
            query_rows.reshape(rows, heads, HD),
            keys.reshape(count, heads, HD),
            preferred_element_type=jnp.float32,
        )
        * scale
    )
    scores = jnp.where(allowed[None], scores, NEG_BIG)
    weights = jnp.exp(scores - jnp.max(scores, axis=-1, keepdims=True))
    total = jnp.sum(weights, axis=-1)
    mixed = jnp.einsum(
        "hqk,khd->hqd",
        weights.astype(jnp.bfloat16),
        values.reshape(count, heads, HD),
        preferred_element_type=jnp.float32,
    )
    return (mixed / total[..., None]).astype(jnp.bfloat16)


def self_out_kernel(
    info_ref, attended_ref, weight_hbm, out_ref, up_ref, down_ref, rows_ref, weight_ref, sum_ref, sems
):
    heads, rows, _ = attended_ref.shape
    n_db, share, features = out_ref.shape
    width = weight_hbm.shape[0]
    cuts = 4
    depth = width // cuts
    copies = [
        pltpu.make_async_copy(
            weight_hbm.at[pl.ds(k * depth, depth)], weight_ref.at[pl.ds(k * depth, depth)], sems.at[k]
        )
        for k in range(cuts)
    ]
    for copy in copies:
        copy.start()
    for head in range(heads):
        rows_ref[:, head * HD : (head + 1) * HD] = attended_ref[head]
    step = math.gcd(features, 512)

    def columns(at, carried, begin, end):
        here = pl.ds(pl.multiple_of(at * step, step), step)
        inner = slice(begin * depth, end * depth)
        product = jnp.dot(
            rows_ref[:, inner], weight_ref[inner, here], preferred_element_type=jnp.float32
        )
        if begin == 0:
            sum_ref[:, here] = product
            return carried
        product = (product + sum_ref[:, here]).astype(jnp.bfloat16)
        for owner in range(n_db):
            out_ref[owner, :, here] = product[owner * share : (owner + 1) * share]
        return carried

    for begin, end in ((0, cuts // 2), (cuts // 2, cuts)):
        for copy in copies[begin:end]:
            copy.wait()
        lax.fori_loop(
            0, features // step, functools.partial(columns, begin=begin, end=end), 0
        )
    above, below = far_blocks(out_ref, info_ref[0], n_db - 1)
    up_ref[...] = out_ref[above]
    down_ref[...] = out_ref[below]


def self_out(info, attended, weight, n_db):
    heads, rows, _ = attended.shape
    width, features = weight.shape
    share = rows // n_db
    vmem = pl.BlockSpec(memory_space=pltpu.VMEM)
    one = jax.ShapeDtypeStruct((share, features), jnp.bfloat16)
    return pl.pallas_call(
        self_out_kernel,
        out_shape=[jax.ShapeDtypeStruct((n_db, share, features), jnp.bfloat16), one, one],
        in_specs=[
            pl.BlockSpec(memory_space=pltpu.SMEM), vmem, pl.BlockSpec(memory_space=pl.ANY)
        ],
        out_specs=[vmem] * 3,
        scratch_shapes=[
            pltpu.VMEM((rows, width), jnp.bfloat16),
            pltpu.VMEM((width, features), jnp.bfloat16),
            pltpu.VMEM((rows, features), jnp.float32),
            pltpu.SemaphoreType.DMA((4,)),
        ],
        compiler_params=pltpu.CompilerParams(vmem_limit_bytes=VMEM_BYTES),
        cost_estimate=pl.CostEstimate(
            flops=2 * rows * width * features,
            bytes_accessed=2 * (rows * width + width * features + rows * features),
            transcendentals=0,
        ),
        name="self_out",
    )(info, attended, weight)


def norm_kernel(
    info_ref, blocks_ref, up_ref, down_ref, gain_ref, hidden_hbm, residual_ref, normed_ref, own_ref, sem
):
    me = info_ref[0]
    share = up_ref.shape[0]
    bring = pltpu.make_async_copy(
        hidden_hbm.at[pl.ds(pl.multiple_of(me * share, share), share)], own_ref, sem
    )
    bring.start()
    bring.wait()
    rows = 16

    def norm(at, carried):
        here = pl.ds(pl.multiple_of(at * rows, rows), rows)
        residual = own_ref[here, :].astype(jnp.float32) + blocks_ref[me, here, :].astype(jnp.float32)
        residual = residual + up_ref[here, :].astype(jnp.float32)
        residual = residual + down_ref[here, :].astype(jnp.float32)
        residual_ref[here, :] = residual
        mean_square = jnp.mean(residual * residual, axis=-1, keepdims=True)
        normed_ref[here, :] = (
            residual * lax.rsqrt(mean_square + 1e-05) * gain_ref[...].astype(jnp.float32)
        ).astype(jnp.bfloat16)
        return carried

    lax.fori_loop(0, share // rows, norm, 0)


def norm_share(info, blocks, up, down, gain, hidden):
    share, features = up.shape
    vmem = pl.BlockSpec(memory_space=pltpu.VMEM)
    return pl.pallas_call(
        norm_kernel,
        out_shape=[
            jax.ShapeDtypeStruct((share, features), jnp.float32),
            jax.ShapeDtypeStruct((share, features), jnp.bfloat16),
        ],
        in_specs=[pl.BlockSpec(memory_space=pltpu.SMEM)]
        + [vmem] * 4
        + [pl.BlockSpec(memory_space=pl.ANY)],
        out_specs=[vmem, vmem],
        scratch_shapes=[pltpu.VMEM((share, features), jnp.bfloat16), pltpu.SemaphoreType.DMA],
        compiler_params=pltpu.CompilerParams(vmem_limit_bytes=SMALL_BYTES),
        cost_estimate=pl.CostEstimate(
            flops=8 * up.size, bytes_accessed=16 * up.size, transcendentals=0
        ),
        name="norm_share",
    )(info, blocks, up, down, gain, hidden)


def project_kernel(where_ref, *refs, cuts):
    wk_hbm, wv_hbm, wq_hbm, wo_hbm, keys_ref, values_ref, wq_ref, wo_ref = refs[-12:-4]
    rows_ref, wk_ref, wv_ref, sems = refs[-4:]
    (table,) = refs[:-12]
    entries = keys_ref.shape[0] // NLEN
    piece = NLEN // cuts
    bring = [
        pltpu.make_async_copy(source, target, sems.at[entries * cuts + at])
        for at, (source, target) in enumerate(
            ((wk_hbm, wk_ref), (wv_hbm, wv_ref), (wq_hbm, wq_ref), (wo_hbm, wo_ref))
        )
    ]
    for copy in bring[:2]:
        copy.start()

    def entry_copy(entry, cut):
        row, shard = where_ref[2 + 2 * entry], where_ref[3 + 2 * entry]
        return pltpu.make_async_copy(
            table.at[row * cuts + cut, shard],
            rows_ref.at[pl.ds(entry * NLEN + cut * piece, piece)],
            sems.at[entry * cuts + cut],
        )

    for entry in range(entries):
        for cut in range(cuts):
            entry_copy(entry, cut).start()

    for copy in bring[2:]:
        copy.start()
    for copy in bring[:2]:
        copy.wait()
    width = keys_ref.shape[1]
    step = math.gcd(width, 512)
    for group in range(entries // NEIGH):
        for entry in range(NEIGH * group, NEIGH * (group + 1)):
            for cut in range(cuts):
                entry_copy(entry, cut).wait()
        here = slice(group * GROUP, (group + 1) * GROUP)
        for at in range(0, width, step):
            lanes = slice(at, at + step)
            for weight, made in ((wk_ref, keys_ref), (wv_ref, values_ref)):
                made[here, lanes] = jnp.dot(
                    rows_ref[here, :], weight[:, lanes], preferred_element_type=jnp.float32
                ).astype(jnp.bfloat16)
    for copy in bring[2:]:
        copy.wait()


def project_encodings(info, table, w_cross_k, w_cross_v, w_cross_q, w_cross_out):
    entries = (info.shape[0] - 2) // 2
    piece, depth = table.shape[2:]
    cuts = NLEN // piece
    width = w_cross_k.shape[1]
    vmem = pl.BlockSpec(memory_space=pltpu.VMEM)
    anywhere = pl.BlockSpec(memory_space=pl.ANY)
    made = jax.ShapeDtypeStruct((entries * NLEN, width), jnp.bfloat16)
    return pl.pallas_call(
        functools.partial(project_kernel, cuts=cuts),
        out_shape=[made, made]
        + [jax.ShapeDtypeStruct(one.shape, one.dtype) for one in (w_cross_q, w_cross_out)],
        in_specs=[pl.BlockSpec(memory_space=pltpu.SMEM)] + [anywhere] * 5,
        out_specs=[vmem] * 4,
        scratch_shapes=[
            pltpu.VMEM((entries * NLEN, depth), jnp.bfloat16),
            pltpu.VMEM(w_cross_k.shape, jnp.bfloat16),
            pltpu.VMEM(w_cross_v.shape, jnp.bfloat16),
            pltpu.SemaphoreType.DMA((entries * cuts + 4,)),
        ],
        compiler_params=pltpu.CompilerParams(vmem_limit_bytes=MIDDLE_BYTES),
        cost_estimate=pl.CostEstimate(
            flops=4 * entries * NLEN * depth * width,
            bytes_accessed=2 * (entries * NLEN * depth + 2 * depth * width + 2 * w_cross_q.size),
            transcendentals=0,
        ),
        name="project_encodings",
    )(info, table, w_cross_k, w_cross_v, w_cross_q, w_cross_out)


def apart_heads(query):
    first = lax.broadcasted_iota(jnp.int32, query.shape, 1) < HD
    nothing = jnp.zeros_like(query)
    return jnp.concatenate(
        (jnp.where(first, query, nothing), jnp.where(first, nothing, query)), axis=0
    )


def together_heads(mixed):
    rows = mixed.shape[0] // 2
    first = lax.broadcasted_iota(jnp.int32, (rows, 2 * HD), 1) < HD
    return jnp.where(first, mixed[:rows], mixed[rows:])


def cross_kernel(info_ref, own_ref, *refs, scale):
    wq_ref, keys_ref, values_ref, wo_ref, out_ref, up_ref, down_ref = refs[-10:-3]
    rows_ref, query_ref, mixed_ref = refs[-3:]
    pieces = refs[:-10]
    share, features = own_ref.shape
    width = wq_ref.shape[1]
    n_db = out_ref.shape[0]
    pairs = width // HD // 2
    tail = 16
    for me in range(n_db):

        @pl.when(info_ref[0] == me)
        def _(me=me):
            for owner in range(n_db):
                if owner == me:
                    source = own_ref
                elif owner < me:
                    source = pieces[2 * (me - owner - 1)]
                else:
                    source = pieces[2 * (owner - me - 1) + 1]
                rows_ref[owner * share : (owner + 1) * share, :] = source[...]

    lanes = [slice(2 * pair * HD, 2 * (pair + 1) * HD) for pair in range(pairs)]
    for at in lanes:
        query_ref[:, at] = jnp.dot(
            rows_ref[...], wq_ref[:, at], preferred_element_type=jnp.float32
        ).astype(jnp.bfloat16)
    row = lax.broadcasted_iota(jnp.int32, (tail, 2 * HD), 0)
    spans = n_db * share // SPAN
    for span in range(spans):
        top = span * SPAN
        here, after = (slice((span + k) * GROUP, (span + k + 1) * GROUP) for k in (0, 1))
        work = [(slice(top, top + SPAN), here, at) for at in lanes]
        work += [(slice(top + SPAN - tail, top + SPAN), after, at) for at in lanes]
        scores = [
            lax.dot_general(
                apart_heads(query_ref[of, at]),
                keys_ref[which, at],
                (((1,), (1,)), ((), ())),
                preferred_element_type=jnp.float32,
            )
            * (scale * LOG2E)
            for of, which, at in work
        ]
        tops = [jnp.max(one, axis=-1, keepdims=True) for one in scores]
        weights = [jnp.exp2(one - top_one) for one, top_one in zip(scores, tops)]
        totals = [jnp.sum(one, axis=-1, keepdims=True) for one in weights]
        mixed = [
            jnp.dot(
                one.astype(jnp.bfloat16), values_ref[which, at], preferred_element_type=jnp.float32
            )
            for one, (_, which, at) in zip(weights, work)
        ]
        mixed = [together_heads(one / total) for one, total in zip(mixed, totals)]
        for pair, at in enumerate(lanes):
            main, last = mixed[pair], mixed[pairs + pair]
            if span == 0:
                main = jnp.where(info_ref[1] > 0, main, 0.0)
            last = jnp.where(row == tail - 1, last, main[SPAN - tail :])
            mixed_ref[top : top + SPAN - tail, at] = main[: SPAN - tail].astype(jnp.bfloat16)
            mixed_ref[top + SPAN - tail : top + SPAN, at] = last.astype(jnp.bfloat16)
    step = math.gcd(features, 512)

    def columns(at, carried):
        here = pl.ds(pl.multiple_of(at * step, step), step)
        product = jnp.dot(mixed_ref[...], wo_ref[:, here], preferred_element_type=jnp.float32)
        product = product.astype(jnp.bfloat16)
        for owner in range(n_db):
            out_ref[owner, :, here] = product[owner * share : (owner + 1) * share]
        return carried

    lax.fori_loop(0, features // step, columns, 0)
    above, below = far_blocks(out_ref, info_ref[0], n_db - 1)
    up_ref[...] = out_ref[above]
    down_ref[...] = out_ref[below]


def cross_block(info, normed, pieces, w_cross_q, keys, values, w_cross_out, n_db, scale):
    share, features = normed.shape
    width = w_cross_q.shape[1]
    rows = n_db * share
    vmem = pl.BlockSpec(memory_space=pltpu.VMEM)
    one = jax.ShapeDtypeStruct((share, features), jnp.bfloat16)
    flat = [one for pair in pieces for one in pair]
    return pl.pallas_call(
        functools.partial(cross_kernel, scale=scale),
        out_shape=[jax.ShapeDtypeStruct((n_db, share, features), jnp.bfloat16), one, one],
        in_specs=[pl.BlockSpec(memory_space=pltpu.SMEM)] + [vmem] * (5 + len(flat)),
        out_specs=[vmem] * 3,
        scratch_shapes=[
            pltpu.VMEM((rows, features), jnp.bfloat16),
            pltpu.VMEM((rows, width), jnp.bfloat16),
            pltpu.VMEM((rows, width), jnp.bfloat16),
        ],
        compiler_params=pltpu.CompilerParams(vmem_limit_bytes=BLOCK_BYTES),
        cost_estimate=pl.CostEstimate(
            flops=4 * rows * width * (features + GROUP),
            bytes_accessed=4 * width * (features + keys.shape[0]) + 4 * rows * features,
            transcendentals=rows * GROUP * width // HD,
        ),
        name="cross_block",
    )(info, normed, *flat, w_cross_q, keys, values, w_cross_out)


def per_device(
    hidden_in,
    query_rows,
    key_rows,
    value_rows,
    w_self_out,
    norm_gain,
    w_cross_q,
    w_cross_k,
    w_cross_v,
    w_cross_out,
    enc_table,
    nb_shard,
    nb_row,
):
    features = hidden_in.shape[1]
    heads = query_rows.shape[1] // HD
    n_seq, n_db = lax.axis_size("seq"), lax.axis_size("db")
    seq_index, db_index = lax.axis_index("seq"), lax.axis_index("db")
    scale = 1.0 / math.sqrt(HD)

    rows_shard, _, depth = enc_table.shape
    encodings = enc_table.reshape(rows_shard * NLEN, depth)
    piece = rows_shard * NLEN // n_seq
    packed, part = pack_heads(
        seq_index.reshape(1).astype(jnp.int32), query_rows, key_rows, value_rows, encodings, piece
    )
    along_db = lax.all_gather(part, "db", axis=0)

    packed, nb_row, nb_shard = lax.optimization_barrier((packed, nb_row, nb_shard))
    wanted = jnp.stack((nb_row, nb_shard), axis=-1).astype(jnp.int32)
    place = jnp.stack((db_index, (seq_index > 0).astype(jnp.int32))).astype(jnp.int32)
    info = jnp.concatenate((place, span_before(wanted).reshape(-1), wanted.reshape(-1)))
    if heads == n_seq:
        held = lax.all_to_all(packed, "seq", 0, 0, tiled=True)
        held, info = lax.optimization_barrier((held, info))
        attended = lax.all_to_all(self_attend_head(held, scale), "seq", 0, 0, tiled=True)
    else:
        attended = self_attention_gathered(query_rows, key_rows, value_rows, scale)

    along_db, attended = lax.optimization_barrier((along_db, attended))
    table = lax.all_gather(along_db, "seq", axis=0)

    partial, up, down = self_out(info, attended, w_self_out, n_db)
    up, down = reduce_scatter(info, partial, up, down)
    residual, normed = norm_share(
        info, partial, up, down, norm_gain.reshape(1, features), hidden_in
    )
    projected = project_encodings(info, table, w_cross_k, w_cross_v, w_cross_q, w_cross_out)
    pieces, (keys, values, w_cross_q, w_cross_out) = gather(normed, projected)
    partial, up, down = cross_block(
        info, normed, pieces, w_cross_q, keys, values, w_cross_out, n_db, scale
    )
    up, down = reduce_scatter(info, partial, up, down)
    own = lax.dynamic_index_in_dim(partial, db_index, 0, keepdims=False).astype(jnp.float32)
    return residual + own + up.astype(jnp.float32) + down.astype(jnp.float32)


def solution(mesh):
    placed = (
        P("seq", None),
        P("seq", "db"),
        P("seq", "db"),
        P("seq", "db"),
        P("db", None),
        P(),
        P(None, "db"),
        P(None, "db"),
        P(None, "db"),
        P("db", None),
        P("db", None, None),
        P("seq", None),
        P("seq", None),
    )
    return jax.shard_map(
        per_device, mesh=mesh, in_specs=placed, out_specs=P(("seq", "db"), None), check_vma=False
    )
```

```python
import functools
import math

import jax
import jax.numpy as jnp
from jax import lax
from jax.experimental import pallas as pl
from jax.experimental.pallas import tpu as pltpu
from jax.sharding import PartitionSpec as P

HD = 128
SPAN = 64
NEIGH = 2
NLEN = 128
GROUP = NEIGH * NLEN

NEG_BIG = -1e30
LOG2E = 1.4426950408889634
VMEM_BYTES = 48 * 1024 * 1024
LARGE_BYTES = 58 * 1024 * 1024
SMALL_BYTES = 4 * 1024 * 1024


def shift(block, axis, distance, senders):
    size = lax.axis_size(axis)
    route = [(k, k + distance) for k in senders if 0 <= k + distance < size]
    return lax.ppermute(block, axis, route)


def line_shift(block, lead, up_from, down_from):
    n_seq, size = lax.axis_size("seq"), lax.axis_size("db")
    route = []
    for row in range(n_seq):
        up = row % 2 == lead
        for k in up_from if up else down_from:
            other = k + 1 if up else k - 1
            if 0 <= other < size:
                route.append((row * size + k, row * size + other))
    return lax.ppermute(block, ("seq", "db"), route)


def far_block(blocks_ref, info_ref, lead, far):
    way = 1 - 2 * (info_ref[2] ^ lead)
    return jnp.clip(info_ref[0] + way * far, 0, blocks_ref.shape[0] - 1)


def add_kernel(info_ref, blocks_ref, sum_ref, out_ref, *, lead, far):
    index = far_block(blocks_ref, info_ref, lead, far)
    rows = 16

    def add(at, carried):
        here = pl.ds(pl.multiple_of(at * rows, rows), rows)
        out_ref[here, :] = (
            blocks_ref[index, here, :].astype(jnp.float32) + sum_ref[here, :].astype(jnp.float32)
        ).astype(jnp.bfloat16)
        return carried

    lax.fori_loop(0, sum_ref.shape[0] // rows, add, 0)


def add_step(info, blocks, arrived, lead, far):
    vmem = pl.BlockSpec(memory_space=pltpu.VMEM)
    return pl.pallas_call(
        functools.partial(add_kernel, lead=lead, far=far),
        out_shape=jax.ShapeDtypeStruct(arrived.shape, arrived.dtype),
        in_specs=[pl.BlockSpec(memory_space=pltpu.SMEM), vmem, vmem],
        out_specs=vmem,
        compiler_params=pltpu.CompilerParams(vmem_limit_bytes=SMALL_BYTES),
        cost_estimate=pl.CostEstimate(
            flops=arrived.size, bytes_accessed=6 * arrived.size, transcendentals=0
        ),
        name="add_step",
    )(info, blocks, arrived)


def reduce_scatter(info, blocks, first, second):
    size = lax.axis_size("db")
    for step in range(size - 1):
        senders = (range(step + 1), range(size - 1 - step, size))
        if step:
            first = add_step(info, blocks, first, 0, size - 1 - step)
            first, held = lax.optimization_barrier((first, held))
        first_sent = first
        first = line_shift(first, 0, *senders)
        if step:
            second = add_step(info, blocks, second, 1, size - 1 - step)
        second, first_sent = lax.optimization_barrier((second, first_sent))
        held = second
        second = line_shift(second, 1, *senders)
    return first, second


def gather(block, beside):
    size = lax.axis_size("db")
    first, second, pieces = block, block, []
    for step in range(size - 1):
        senders = (range(step, size), range(0, size - step))
        if step == size // 2:
            first, held, beside = lax.optimization_barrier((first, held, beside))
        elif step:
            first, held = lax.optimization_barrier((first, held))
        first_sent = first
        first = line_shift(first, 0, *senders)
        second, first_sent = lax.optimization_barrier((second, first_sent))
        held = second
        second = line_shift(second, 1, *senders)
        pieces.append((first, second))
    return pieces, beside


def self_kernel(qkv_ref, out_ref, *, blocks, rows, scale):
    for block in range(blocks):
        query = qkv_ref[block, 0]
        live = (block + 1) * rows
        keys = qkv_ref[0 : block + 1, 1].reshape(live, HD)
        values = qkv_ref[0 : block + 1, 2].reshape(live, HD)
        scores = lax.dot_general(
            query, keys, (((1,), (1,)), ((), ())), preferred_element_type=jnp.float32
        )
        query_pos = block * rows + lax.broadcasted_iota(jnp.int32, (rows, live), 0)
        key_pos = lax.broadcasted_iota(jnp.int32, (rows, live), 1)
        scores = jnp.where(key_pos <= query_pos, scores * (scale * LOG2E), NEG_BIG)
        top = jnp.max(scores, axis=-1, keepdims=True)
        weights = jnp.exp2(scores - top)
        total = jnp.sum(weights, axis=-1, keepdims=True)
        mixed = jnp.dot(weights.astype(jnp.bfloat16), values, preferred_element_type=jnp.float32)
        out_ref[block] = (mixed / total).astype(jnp.bfloat16)


def self_attend_head(qkv, scale):
    blocks, _, rows, _ = qkv.shape
    return pl.pallas_call(
        functools.partial(self_kernel, blocks=blocks, rows=rows, scale=scale),
        out_shape=jax.ShapeDtypeStruct((blocks, rows, HD), jnp.bfloat16),
        in_specs=[pl.BlockSpec(memory_space=pltpu.VMEM)],
        out_specs=pl.BlockSpec(memory_space=pltpu.VMEM),
        compiler_params=pltpu.CompilerParams(vmem_limit_bytes=VMEM_BYTES),
        cost_estimate=pl.CostEstimate(
            flops=2 * blocks * blocks * rows * rows * HD,
            bytes_accessed=8 * blocks * rows * HD,
            transcendentals=blocks * blocks * rows * rows // 2,
        ),
        name="self_attend",
    )(qkv)


def span_before(wanted):
    return shift(wanted[-1], "seq", 1, range(lax.axis_size("seq")))


def pack_kernel(index_ref, query_ref, key_ref, value_ref, part_ref, out_ref, part_out_ref):
    for which, ref in enumerate((query_ref, key_ref, value_ref)):
        for head in range(out_ref.shape[0]):
            out_ref[head, which] = ref[:, head * HD : (head + 1) * HD]
    part_out_ref[...] = part_ref[...]


def pack_heads(index, query_rows, key_rows, value_rows, encodings, piece):
    rows, width = query_rows.shape
    heads = width // HD
    depth = encodings.shape[1]
    steps = 4
    block, part = rows // steps, piece // steps
    row_block = pl.BlockSpec((block, width), lambda at, index_ref: (at, 0))
    return pl.pallas_call(
        pack_kernel,
        out_shape=[
            jax.ShapeDtypeStruct((heads, 3, rows, HD), jnp.bfloat16),
            jax.ShapeDtypeStruct((piece, depth), jnp.bfloat16),
        ],
        grid_spec=pltpu.PrefetchScalarGridSpec(
            num_scalar_prefetch=1,
            grid=(steps,),
            in_specs=[row_block] * 3
            + [pl.BlockSpec((part, depth), lambda at, index_ref: (index_ref[0] * steps + at, 0))],
            out_specs=[
                pl.BlockSpec((heads, 3, block, HD), lambda at, index_ref: (0, 0, at, 0)),
                pl.BlockSpec((part, depth), lambda at, index_ref: (at, 0)),
            ],
        ),
        compiler_params=pltpu.CompilerParams(
            vmem_limit_bytes=LARGE_BYTES, dimension_semantics=("arbitrary",)
        ),
        cost_estimate=pl.CostEstimate(
            flops=0, bytes_accessed=12 * rows * width, transcendentals=0
        ),
        name="pack_heads",
    )(index, query_rows, key_rows, value_rows, encodings)


def self_attention_gathered(query_rows, key_rows, value_rows, scale):
    rows, width = query_rows.shape
    heads = width // HD
    keys = lax.all_gather(key_rows, "seq", axis=0, tiled=True)
    values = lax.all_gather(value_rows, "seq", axis=0, tiled=True)
    count = keys.shape[0]
    query_pos = lax.axis_index("seq") * rows + jnp.arange(rows, dtype=jnp.int32)
    allowed = jnp.arange(count, dtype=jnp.int32)[None, :] <= query_pos[:, None]
    scores = (
        jnp.einsum(
            "qhd,khd->hqk",
            query_rows.reshape(rows, heads, HD),
            keys.reshape(count, heads, HD),
            preferred_element_type=jnp.float32,
        )
        * scale
    )
    scores = jnp.where(allowed[None], scores, NEG_BIG)
    weights = jnp.exp(scores - jnp.max(scores, axis=-1, keepdims=True))
    total = jnp.sum(weights, axis=-1)
    mixed = jnp.einsum(
        "hqk,khd->hqd",
        weights.astype(jnp.bfloat16),
        values.reshape(count, heads, HD),
        preferred_element_type=jnp.float32,
    )
    return (mixed / total[..., None]).astype(jnp.bfloat16)


def self_out_kernel(
    info_ref, attended_ref, weight_hbm, out_ref, first_ref, second_ref, rows_ref, weight_ref, sum_ref, sems
):
    heads, rows, _ = attended_ref.shape
    n_db, share, features = out_ref.shape
    width = weight_hbm.shape[0]
    cuts = 4
    depth = width // cuts
    copies = [
        pltpu.make_async_copy(
            weight_hbm.at[pl.ds(k * depth, depth)], weight_ref.at[pl.ds(k * depth, depth)], sems.at[k]
        )
        for k in range(cuts)
    ]
    for copy in copies:
        copy.start()
    for head in range(heads):
        rows_ref[:, head * HD : (head + 1) * HD] = attended_ref[head]
    step = math.gcd(features, 512)

    def columns(at, carried, begin, end):
        here = pl.ds(pl.multiple_of(at * step, step), step)
        inner = slice(begin * depth, end * depth)
        product = jnp.dot(
            rows_ref[:, inner], weight_ref[inner, here], preferred_element_type=jnp.float32
        )
        if begin == 0:
            sum_ref[:, here] = product
            return carried
        product = (product + sum_ref[:, here]).astype(jnp.bfloat16)
        for owner in range(n_db):
            out_ref[owner, :, here] = product[owner * share : (owner + 1) * share]
        return carried

    for begin, end in ((0, cuts // 2), (cuts // 2, cuts)):
        for copy in copies[begin:end]:
            copy.wait()
        lax.fori_loop(
            0, features // step, functools.partial(columns, begin=begin, end=end), 0, unroll=4
        )
    first_ref[...] = out_ref[far_block(out_ref, info_ref, 0, n_db - 1)]
    second_ref[...] = out_ref[far_block(out_ref, info_ref, 1, n_db - 1)]


def self_out(info, attended, weight, n_db):
    heads, rows, _ = attended.shape
    width, features = weight.shape
    share = rows // n_db
    vmem = pl.BlockSpec(memory_space=pltpu.VMEM)
    one = jax.ShapeDtypeStruct((share, features), jnp.bfloat16)
    return pl.pallas_call(
        self_out_kernel,
        out_shape=[jax.ShapeDtypeStruct((n_db, share, features), jnp.bfloat16), one, one],
        in_specs=[
            pl.BlockSpec(memory_space=pltpu.SMEM), vmem, pl.BlockSpec(memory_space=pl.ANY)
        ],
        out_specs=[vmem] * 3,
        scratch_shapes=[
            pltpu.VMEM((rows, width), jnp.bfloat16),
            pltpu.VMEM((width, features), jnp.bfloat16),
            pltpu.VMEM((rows, features), jnp.float32),
            pltpu.SemaphoreType.DMA((4,)),
        ],
        compiler_params=pltpu.CompilerParams(vmem_limit_bytes=VMEM_BYTES),
        cost_estimate=pl.CostEstimate(
            flops=2 * rows * width * features,
            bytes_accessed=2 * (rows * width + width * features + rows * features),
            transcendentals=0,
        ),
        name="self_out",
    )(info, attended, weight)


def norm_kernel(
    info_ref, blocks_ref, up_ref, down_ref, gain_ref, hidden_hbm, residual_ref, normed_ref, own_ref, sem
):
    me = info_ref[0]
    share = up_ref.shape[0]
    bring = pltpu.make_async_copy(
        hidden_hbm.at[pl.ds(pl.multiple_of(me * share, share), share)], own_ref, sem
    )
    bring.start()
    bring.wait()
    rows = 16

    def norm(at, carried):
        here = pl.ds(pl.multiple_of(at * rows, rows), rows)
        residual = own_ref[here, :].astype(jnp.float32) + blocks_ref[me, here, :].astype(jnp.float32)
        residual = residual + up_ref[here, :].astype(jnp.float32)
        residual = residual + down_ref[here, :].astype(jnp.float32)
        residual_ref[here, :] = residual
        mean_square = jnp.mean(residual * residual, axis=-1, keepdims=True)
        normed_ref[here, :] = (
            residual * lax.rsqrt(mean_square + 1e-05) * gain_ref[...].astype(jnp.float32)
        ).astype(jnp.bfloat16)
        return carried

    lax.fori_loop(0, share // rows, norm, 0)


def norm_share(info, blocks, up, down, gain, hidden):
    share, features = up.shape
    vmem = pl.BlockSpec(memory_space=pltpu.VMEM)
    return pl.pallas_call(
        norm_kernel,
        out_shape=[
            jax.ShapeDtypeStruct((share, features), jnp.float32),
            jax.ShapeDtypeStruct((share, features), jnp.bfloat16),
        ],
        in_specs=[pl.BlockSpec(memory_space=pltpu.SMEM)]
        + [vmem] * 4
        + [pl.BlockSpec(memory_space=pl.ANY)],
        out_specs=[vmem, vmem],
        scratch_shapes=[pltpu.VMEM((share, features), jnp.bfloat16), pltpu.SemaphoreType.DMA],
        compiler_params=pltpu.CompilerParams(vmem_limit_bytes=SMALL_BYTES),
        cost_estimate=pl.CostEstimate(
            flops=8 * up.size, bytes_accessed=16 * up.size, transcendentals=0
        ),
        name="norm_share",
    )(info, blocks, up, down, gain, hidden)


def project_kernel(where_ref, first_ref, second_ref, wk_ref, wv_ref, keys_ref, values_ref):
    depth = first_ref.shape[-1]
    rows = jnp.concatenate(
        (first_ref[...].reshape(NLEN, depth), second_ref[...].reshape(NLEN, depth)), axis=0
    )
    keys_ref[...] = jnp.dot(rows, wk_ref[...], preferred_element_type=jnp.float32).astype(
        jnp.bfloat16
    )
    values_ref[...] = jnp.dot(rows, wv_ref[...], preferred_element_type=jnp.float32).astype(
        jnp.bfloat16
    )


def project_encodings(where, table, w_cross_k, w_cross_v):
    groups = (where.shape[0] - 3) // (2 * NEIGH)
    _, cuts, _, piece, depth = table.shape
    width = w_cross_k.shape[1]

    def entry(neighbour):
        def index(group, where_ref):
            at = 3 + 2 * (NEIGH * group + neighbour)
            return (where_ref[at], 0, where_ref[at + 1], 0, 0)

        return pl.BlockSpec((1, cuts, 1, piece, depth), index)

    fixed = pl.BlockSpec((depth, width), lambda group, where_ref: (0, 0))
    made = pl.BlockSpec((GROUP, width), lambda group, where_ref: (group, 0))
    return pl.pallas_call(
        project_kernel,
        out_shape=[jax.ShapeDtypeStruct((groups * GROUP, width), jnp.bfloat16)] * 2,
        grid_spec=pltpu.PrefetchScalarGridSpec(
            num_scalar_prefetch=1,
            grid=(groups,),
            in_specs=[entry(0), entry(1), fixed, fixed],
            out_specs=[made, made],
        ),
        compiler_params=pltpu.CompilerParams(
            vmem_limit_bytes=LARGE_BYTES, dimension_semantics=("arbitrary",)
        ),
        cost_estimate=pl.CostEstimate(
            flops=4 * groups * GROUP * depth * width,
            bytes_accessed=2 * (groups * GROUP * (depth + 2 * width) + 2 * depth * width),
            transcendentals=0,
        ),
        name="project_encodings",
    )(where, table, table, w_cross_k, w_cross_v)


def apart_heads(query):
    first = lax.broadcasted_iota(jnp.int32, query.shape, 1) < HD
    nothing = jnp.zeros_like(query)
    return jnp.concatenate(
        (jnp.where(first, query, nothing), jnp.where(first, nothing, query)), axis=0
    )


def together_heads(mixed):
    rows = mixed.shape[0] // 2
    first = lax.broadcasted_iota(jnp.int32, (rows, 2 * HD), 1) < HD
    return jnp.where(first, mixed[:rows], mixed[rows:])


def cross_kernel(info_ref, own_ref, *refs, scale):
    wq_hbm, keys_hbm, values_hbm, wo_hbm, out_ref, first_ref, second_ref = refs[-15:-8]
    wq_ref, keys_ref, values_ref, wo_ref, rows_ref, query_ref, mixed_ref, sems = refs[-8:]
    pieces = refs[:-15]
    share, features = own_ref.shape
    width = wq_ref.shape[1]
    n_db = out_ref.shape[0]
    pairs = width // HD // 2
    tail = 16
    cut = features // 4
    low = width // 4
    wq_copies = [
        pltpu.make_async_copy(
            wq_hbm.at[pl.ds(k * cut, cut)], wq_ref.at[pl.ds(k * cut, cut)], sems.at[k]
        )
        for k in range(4)
    ]
    other_copies = [
        pltpu.make_async_copy(keys_hbm, keys_ref, sems.at[4]),
        pltpu.make_async_copy(values_hbm, values_ref, sems.at[5]),
    ] + [
        pltpu.make_async_copy(
            wo_hbm.at[pl.ds(k * low, low)], wo_ref.at[pl.ds(k * low, low)], sems.at[6 + k]
        )
        for k in range(4)
    ]
    for copy in wq_copies + other_copies:
        copy.start()
    me = info_ref[0]

    def place(source, owner):
        @pl.when((owner >= 0) & (owner < n_db))
        def _():
            at = pl.multiple_of(jnp.clip(owner, 0, n_db - 1) * share, share)
            rows_ref[pl.ds(at, share), :] = source[...]

    place(own_ref, me)
    for at, source in enumerate(pieces):
        way = 1 - 2 * (info_ref[2] ^ (at % 2))
        place(source, me - way * (at // 2 + 1))
    lanes = [slice(2 * pair * HD, 2 * (pair + 1) * HD) for pair in range(pairs)]
    for k, copy in enumerate(wq_copies):
        copy.wait()
        inner = slice(k * cut, (k + 1) * cut)
        for at in lanes:
            part = jnp.dot(
                rows_ref[:, inner], wq_ref[inner, at], preferred_element_type=jnp.float32
            )
            query_ref[:, at] = part if k == 0 else query_ref[:, at] + part
    for copy in other_copies[:2]:
        copy.wait()
    row = lax.broadcasted_iota(jnp.int32, (tail, 2 * HD), 0)
    spans = n_db * share // SPAN
    for span in range(spans):
        top = span * SPAN
        here, after = (slice((span + k) * GROUP, (span + k + 1) * GROUP) for k in (0, 1))
        work = [(slice(top, top + SPAN), here, at) for at in lanes]
        work += [(slice(top + SPAN - tail, top + SPAN), after, at) for at in lanes]
        scores = [
            lax.dot_general(
                apart_heads(query_ref[of, at].astype(jnp.bfloat16)),
                keys_ref[which, at],
                (((1,), (1,)), ((), ())),
                preferred_element_type=jnp.float32,
            )
            * (scale * LOG2E)
            for of, which, at in work
        ]
        tops = [jnp.max(one, axis=-1, keepdims=True) for one in scores]
        weights = [jnp.exp2(one - top_one) for one, top_one in zip(scores, tops)]
        totals = [jnp.sum(one, axis=-1, keepdims=True) for one in weights]
        mixed = [
            jnp.dot(
                one.astype(jnp.bfloat16), values_ref[which, at], preferred_element_type=jnp.float32
            )
            for one, (_, which, at) in zip(weights, work)
        ]
        mixed = [together_heads(one / total) for one, total in zip(mixed, totals)]
        for pair, at in enumerate(lanes):
            main, last = mixed[pair], mixed[pairs + pair]
            if span == 0:
                main = jnp.where(info_ref[1] > 0, main, 0.0)
            last = jnp.where(row == tail - 1, last, main[SPAN - tail :])
            mixed_ref[top : top + SPAN - tail, at] = main[: SPAN - tail].astype(jnp.bfloat16)
            mixed_ref[top + SPAN - tail : top + SPAN, at] = last.astype(jnp.bfloat16)
    for copy in other_copies[2:]:
        copy.wait()
    step = math.gcd(features, 512)

    def columns(at, carried):
        here = pl.ds(pl.multiple_of(at * step, step), step)
        product = jnp.dot(mixed_ref[...], wo_ref[:, here], preferred_element_type=jnp.float32)
        product = product.astype(jnp.bfloat16)
        for owner in range(n_db):
            out_ref[owner, :, here] = product[owner * share : (owner + 1) * share]
        return carried

    lax.fori_loop(0, features // step, columns, 0, unroll=4)
    first_ref[...] = out_ref[far_block(out_ref, info_ref, 0, n_db - 1)]
    second_ref[...] = out_ref[far_block(out_ref, info_ref, 1, n_db - 1)]


def cross_block(info, normed, pieces, w_cross_q, keys, values, w_cross_out, n_db, scale):
    share, features = normed.shape
    width = w_cross_q.shape[1]
    rows = n_db * share
    vmem = pl.BlockSpec(memory_space=pltpu.VMEM)
    anywhere = pl.BlockSpec(memory_space=pl.ANY)
    one = jax.ShapeDtypeStruct((share, features), jnp.bfloat16)
    flat = [one for pair in pieces for one in pair]
    return pl.pallas_call(
        functools.partial(cross_kernel, scale=scale),
        out_shape=[jax.ShapeDtypeStruct((n_db, share, features), jnp.bfloat16), one, one],
        in_specs=[pl.BlockSpec(memory_space=pltpu.SMEM)]
        + [vmem] * (1 + len(flat))
        + [anywhere] * 4,
        out_specs=[vmem] * 3,
        scratch_shapes=[
            pltpu.VMEM((features, width), jnp.bfloat16),
            pltpu.VMEM(keys.shape, jnp.bfloat16),
            pltpu.VMEM(values.shape, jnp.bfloat16),
            pltpu.VMEM((width, features), jnp.bfloat16),
            pltpu.VMEM((rows, features), jnp.bfloat16),
            pltpu.VMEM((rows, width), jnp.float32),
            pltpu.VMEM((rows, width), jnp.bfloat16),
            pltpu.SemaphoreType.DMA((10,)),
        ],
        compiler_params=pltpu.CompilerParams(vmem_limit_bytes=VMEM_BYTES),
        cost_estimate=pl.CostEstimate(
            flops=4 * rows * width * (features + GROUP),
            bytes_accessed=4 * width * (features + keys.shape[0]) + 4 * rows * features,
            transcendentals=rows * GROUP * width // HD,
        ),
        name="cross_block",
    )(info, normed, *flat, w_cross_q, keys, values, w_cross_out)


def per_device(
    hidden_in,
    query_rows,
    key_rows,
    value_rows,
    w_self_out,
    norm_gain,
    w_cross_q,
    w_cross_k,
    w_cross_v,
    w_cross_out,
    enc_table,
    nb_shard,
    nb_row,
):
    features = hidden_in.shape[1]
    heads = query_rows.shape[1] // HD
    n_seq, n_db = lax.axis_size("seq"), lax.axis_size("db")
    seq_index, db_index = lax.axis_index("seq"), lax.axis_index("db")
    scale = 1.0 / math.sqrt(HD)

    rows_shard, _, depth = enc_table.shape
    encodings = enc_table.reshape(rows_shard * NLEN, depth)
    piece = rows_shard * NLEN // n_seq
    packed, part = pack_heads(
        seq_index.reshape(1).astype(jnp.int32), query_rows, key_rows, value_rows, encodings, piece
    )
    along_db = lax.all_gather(part, "db", axis=0)

    packed, nb_row, nb_shard = lax.optimization_barrier((packed, nb_row, nb_shard))
    wanted = jnp.stack((nb_row, nb_shard), axis=-1).astype(jnp.int32)
    place = jnp.stack((db_index, (seq_index > 0).astype(jnp.int32), seq_index % 2)).astype(jnp.int32)
    info = jnp.concatenate((place, span_before(wanted).reshape(-1), wanted.reshape(-1)))
    if heads == n_seq:
        held = lax.all_to_all(packed, "seq", 0, 0, tiled=True)
        held, info = lax.optimization_barrier((held, info))
        attended = lax.all_to_all(self_attend_head(held, scale), "seq", 0, 0, tiled=True)
    else:
        attended = self_attention_gathered(query_rows, key_rows, value_rows, scale)

    along_db, attended = lax.optimization_barrier((along_db, attended))
    table = lax.all_gather(along_db, "seq", axis=0).reshape(
        rows_shard, NLEN // piece, n_db, piece, depth
    )

    partial, up, down = self_out(info, attended, w_self_out, n_db)
    up, down = reduce_scatter(info, partial, up, down)
    residual, normed = norm_share(
        info, partial, up, down, norm_gain.reshape(1, features), hidden_in
    )
    projected = project_encodings(info, table, w_cross_k, w_cross_v)
    pieces, (keys, values) = gather(normed, projected)
    partial, up, down = cross_block(
        info, normed, pieces, w_cross_q, keys, values, w_cross_out, n_db, scale
    )
    up, down = reduce_scatter(info, partial, up, down)
    own = lax.dynamic_index_in_dim(partial, db_index, 0, keepdims=False).astype(jnp.float32)
    return residual + own + up.astype(jnp.float32) + down.astype(jnp.float32)


def solution(mesh):
    placed = (
        P("seq", None),
        P("seq", "db"),
        P("seq", "db"),
        P("seq", "db"),
        P("db", None),
        P(),
        P(None, "db"),
        P(None, "db"),
        P(None, "db"),
        P("db", None),
        P("db", None, None),
        P("seq", None),
        P("seq", None),
    )
    return jax.shard_map(
        per_device, mesh=mesh, in_specs=placed, out_specs=P(("seq", "db"), None), check_vma=False
    )
```

```python
import functools
import math

import jax
import jax.numpy as jnp
from jax import lax
from jax.experimental import pallas as pl
from jax.experimental.pallas import tpu as pltpu
from jax.sharding import PartitionSpec as P

HD = 128
SPAN = 64
NEIGH = 2
NLEN = 128
GROUP = NEIGH * NLEN

NEG_BIG = -1e30
LOG2E = 1.4426950408889634
VMEM_BYTES = 48 * 1024 * 1024
LARGE_BYTES = 58 * 1024 * 1024
SMALL_BYTES = 4 * 1024 * 1024


def shift(block, axis, distance, senders):
    size = lax.axis_size(axis)
    route = [(k, k + distance) for k in senders if 0 <= k + distance < size]
    return lax.ppermute(block, axis, route)


def line_shift(block, lead, up_from, down_from):
    n_seq, size = lax.axis_size("seq"), lax.axis_size("db")
    route = []
    for row in range(n_seq):
        up = lead == 0
        for k in up_from if up else down_from:
            other = k + 1 if up else k - 1
            if 0 <= other < size:
                route.append((row * size + k, row * size + other))
    return lax.ppermute(block, ("seq", "db"), route)


def far_block(blocks_ref, info_ref, lead, far):
    way = 1 - 2 * lead
    return jnp.clip(info_ref[0] + way * far, 0, blocks_ref.shape[0] - 1)


def add_kernel(info_ref, blocks_ref, up_ref, down_ref, up_out_ref, down_out_ref, *, far):
    rows = 16

    def add(at, carried):
        here = pl.ds(pl.multiple_of(at * rows, rows), rows)
        for lead, ref, out_ref in ((0, up_ref, up_out_ref), (1, down_ref, down_out_ref)):
            index = far_block(blocks_ref, info_ref, lead, far)
            out_ref[here, :] = (
                blocks_ref[index, here, :].astype(jnp.float32) + ref[here, :].astype(jnp.float32)
            ).astype(jnp.bfloat16)
        return carried

    lax.fori_loop(0, up_ref.shape[0] // rows, add, 0)


def add_step(info, blocks, up, down, far):
    vmem = pl.BlockSpec(memory_space=pltpu.VMEM)
    one = jax.ShapeDtypeStruct(up.shape, up.dtype)
    return pl.pallas_call(
        functools.partial(add_kernel, far=far),
        out_shape=[one, one],
        in_specs=[pl.BlockSpec(memory_space=pltpu.SMEM), vmem, vmem, vmem],
        out_specs=[vmem, vmem],
        compiler_params=pltpu.CompilerParams(vmem_limit_bytes=SMALL_BYTES),
        cost_estimate=pl.CostEstimate(
            flops=2 * up.size, bytes_accessed=12 * up.size, transcendentals=0
        ),
        name="add_step",
    )(info, blocks, up, down)


def reduce_scatter(info, blocks, up, down):
    size = lax.axis_size("db")
    for step in range(size - 1):
        senders = (range(step + 1), range(size - 1 - step, size))
        if step:
            up, down = add_step(info, blocks, up, down, size - 1 - step)
        down = line_shift(down, 1, *senders)
        up = line_shift(up, 0, *senders)
        down, up = lax.optimization_barrier((down, up))
    return up, down


def gather(block, beside):
    size = lax.axis_size("db")
    up, down, pieces = block, block, []
    for step in range(size - 1):
        senders = (range(step, size), range(0, size - step))
        down = line_shift(down, 1, *senders)
        up = line_shift(up, 0, *senders)
        at = step + len(beside) - (size - 1)
        if at >= 0:
            up, down, beside[at] = lax.optimization_barrier((up, down, beside[at]))
        else:
            up, down = lax.optimization_barrier((up, down))
        pieces.append((up, down))
    return pieces, beside


def self_kernel(qkv_ref, out_ref, *, blocks, rows, scale):
    for block in range(blocks):
        query = qkv_ref[block, 0]
        live = (block + 1) * rows
        keys = qkv_ref[0 : block + 1, 1].reshape(live, HD)
        values = qkv_ref[0 : block + 1, 2].reshape(live, HD)
        scores = lax.dot_general(
            query, keys, (((1,), (1,)), ((), ())), preferred_element_type=jnp.float32
        )
        query_pos = block * rows + lax.broadcasted_iota(jnp.int32, (rows, live), 0)
        key_pos = lax.broadcasted_iota(jnp.int32, (rows, live), 1)
        scores = jnp.where(key_pos <= query_pos, scores * (scale * LOG2E), NEG_BIG)
        top = jnp.max(scores, axis=-1, keepdims=True)
        weights = jnp.exp2(scores - top)
        total = jnp.sum(weights, axis=-1, keepdims=True)
        mixed = jnp.dot(weights.astype(jnp.bfloat16), values, preferred_element_type=jnp.float32)
        out_ref[block] = (mixed / total).astype(jnp.bfloat16)


def self_attend_head(qkv, scale):
    blocks, _, rows, _ = qkv.shape
    return pl.pallas_call(
        functools.partial(self_kernel, blocks=blocks, rows=rows, scale=scale),
        out_shape=jax.ShapeDtypeStruct((blocks, rows, HD), jnp.bfloat16),
        in_specs=[pl.BlockSpec(memory_space=pltpu.VMEM)],
        out_specs=pl.BlockSpec(memory_space=pltpu.VMEM),
        compiler_params=pltpu.CompilerParams(vmem_limit_bytes=VMEM_BYTES),
        cost_estimate=pl.CostEstimate(
            flops=2 * blocks * blocks * rows * rows * HD,
            bytes_accessed=8 * blocks * rows * HD,
            transcendentals=blocks * blocks * rows * rows // 2,
        ),
        name="self_attend",
    )(qkv)


def span_before(wanted):
    return shift(wanted[-1], "seq", 1, range(lax.axis_size("seq")))


def pack_kernel(index_ref, query_ref, key_ref, value_ref, part_ref, out_ref, part_out_ref):
    for which, ref in enumerate((query_ref, key_ref, value_ref)):
        for head in range(out_ref.shape[0]):
            out_ref[head, which] = ref[:, head * HD : (head + 1) * HD]
    part_out_ref[...] = part_ref[...]


def pack_heads(index, query_rows, key_rows, value_rows, encodings, piece):
    rows, width = query_rows.shape
    heads = width // HD
    depth = encodings.shape[1]
    steps = 4
    block, part = rows // steps, piece // steps
    row_block = pl.BlockSpec((block, width), lambda at, index_ref: (at, 0))
    return pl.pallas_call(
        pack_kernel,
        out_shape=[
            jax.ShapeDtypeStruct((heads, 3, rows, HD), jnp.bfloat16),
            jax.ShapeDtypeStruct((piece, depth), jnp.bfloat16),
        ],
        grid_spec=pltpu.PrefetchScalarGridSpec(
            num_scalar_prefetch=1,
            grid=(steps,),
            in_specs=[row_block] * 3
            + [pl.BlockSpec((part, depth), lambda at, index_ref: (index_ref[0] * steps + at, 0))],
            out_specs=[
                pl.BlockSpec((heads, 3, block, HD), lambda at, index_ref: (0, 0, at, 0)),
                pl.BlockSpec((part, depth), lambda at, index_ref: (at, 0)),
            ],
        ),
        compiler_params=pltpu.CompilerParams(
            vmem_limit_bytes=LARGE_BYTES, dimension_semantics=("arbitrary",)
        ),
        cost_estimate=pl.CostEstimate(
            flops=0, bytes_accessed=12 * rows * width, transcendentals=0
        ),
        name="pack_heads",
    )(index, query_rows, key_rows, value_rows, encodings)


def self_attention_gathered(query_rows, key_rows, value_rows, scale):
    rows, width = query_rows.shape
    heads = width // HD
    keys = lax.all_gather(key_rows, "seq", axis=0, tiled=True)
    values = lax.all_gather(value_rows, "seq", axis=0, tiled=True)
    count = keys.shape[0]
    query_pos = lax.axis_index("seq") * rows + jnp.arange(rows, dtype=jnp.int32)
    allowed = jnp.arange(count, dtype=jnp.int32)[None, :] <= query_pos[:, None]
    scores = (
        jnp.einsum(
            "qhd,khd->hqk",
            query_rows.reshape(rows, heads, HD),
            keys.reshape(count, heads, HD),
            preferred_element_type=jnp.float32,
        )
        * scale
    )
    scores = jnp.where(allowed[None], scores, NEG_BIG)
    weights = jnp.exp(scores - jnp.max(scores, axis=-1, keepdims=True))
    total = jnp.sum(weights, axis=-1)
    mixed = jnp.einsum(
        "hqk,khd->hqd",
        weights.astype(jnp.bfloat16),
        values.reshape(count, heads, HD),
        preferred_element_type=jnp.float32,
    )
    return (mixed / total[..., None]).astype(jnp.bfloat16)


def self_out_kernel(
    info_ref, attended_ref, weight_hbm, out_ref, first_ref, second_ref, rows_ref, weight_ref, sum_ref, sems
):
    heads, rows, _ = attended_ref.shape
    n_db, share, features = out_ref.shape
    width = weight_hbm.shape[0]
    cuts = 4
    depth = width // cuts
    copies = [
        pltpu.make_async_copy(
            weight_hbm.at[pl.ds(k * depth, depth)], weight_ref.at[pl.ds(k * depth, depth)], sems.at[k]
        )
        for k in range(cuts)
    ]
    for copy in copies:
        copy.start()
    for head in range(heads):
        rows_ref[:, head * HD : (head + 1) * HD] = attended_ref[head]
    step = math.gcd(features, 512)

    def columns(at, carried, begin, end):
        here = pl.ds(pl.multiple_of(at * step, step), step)
        inner = slice(begin * depth, end * depth)
        product = jnp.dot(
            rows_ref[:, inner], weight_ref[inner, here], preferred_element_type=jnp.float32
        )
        if begin == 0:
            sum_ref[:, here] = product
            return carried
        product = (product + sum_ref[:, here]).astype(jnp.bfloat16)
        for owner in range(n_db):
            out_ref[owner, :, here] = product[owner * share : (owner + 1) * share]
        return carried

    for begin, end in ((0, cuts // 2), (cuts // 2, cuts)):
        for copy in copies[begin:end]:
            copy.wait()
        lax.fori_loop(
            0, features // step, functools.partial(columns, begin=begin, end=end), 0, unroll=4
        )
    first_ref[...] = out_ref[far_block(out_ref, info_ref, 0, n_db - 1)]
    second_ref[...] = out_ref[far_block(out_ref, info_ref, 1, n_db - 1)]


def self_out(info, attended, weight, n_db):
    heads, rows, _ = attended.shape
    width, features = weight.shape
    share = rows // n_db
    vmem = pl.BlockSpec(memory_space=pltpu.VMEM)
    one = jax.ShapeDtypeStruct((share, features), jnp.bfloat16)
    return pl.pallas_call(
        self_out_kernel,
        out_shape=[jax.ShapeDtypeStruct((n_db, share, features), jnp.bfloat16), one, one],
        in_specs=[
            pl.BlockSpec(memory_space=pltpu.SMEM), vmem, pl.BlockSpec(memory_space=pl.ANY)
        ],
        out_specs=[vmem] * 3,
        scratch_shapes=[
            pltpu.VMEM((rows, width), jnp.bfloat16),
            pltpu.VMEM((width, features), jnp.bfloat16),
            pltpu.VMEM((rows, features), jnp.float32),
            pltpu.SemaphoreType.DMA((4,)),
        ],
        compiler_params=pltpu.CompilerParams(vmem_limit_bytes=VMEM_BYTES),
        cost_estimate=pl.CostEstimate(
            flops=2 * rows * width * features,
            bytes_accessed=2 * (rows * width + width * features + rows * features),
            transcendentals=0,
        ),
        name="self_out",
    )(info, attended, weight)


def norm_kernel(
    info_ref, blocks_ref, up_ref, down_ref, gain_ref, hidden_hbm, residual_ref, normed_ref, own_ref, sem
):
    me = info_ref[0]
    share = up_ref.shape[0]
    bring = pltpu.make_async_copy(
        hidden_hbm.at[pl.ds(pl.multiple_of(me * share, share), share)], own_ref, sem
    )
    bring.start()
    bring.wait()
    rows = 16

    def norm(at, carried):
        here = pl.ds(pl.multiple_of(at * rows, rows), rows)
        residual = own_ref[here, :].astype(jnp.float32) + blocks_ref[me, here, :].astype(jnp.float32)
        residual = residual + up_ref[here, :].astype(jnp.float32)
        residual = residual + down_ref[here, :].astype(jnp.float32)
        residual_ref[here, :] = residual
        mean_square = jnp.mean(residual * residual, axis=-1, keepdims=True)
        normed_ref[here, :] = (
            residual * lax.rsqrt(mean_square + 1e-05) * gain_ref[...].astype(jnp.float32)
        ).astype(jnp.bfloat16)
        return carried

    lax.fori_loop(0, share // rows, norm, 0)


def norm_share(info, blocks, up, down, gain, hidden):
    share, features = up.shape
    vmem = pl.BlockSpec(memory_space=pltpu.VMEM)
    return pl.pallas_call(
        norm_kernel,
        out_shape=[
            jax.ShapeDtypeStruct((share, features), jnp.float32),
            jax.ShapeDtypeStruct((share, features), jnp.bfloat16),
        ],
        in_specs=[pl.BlockSpec(memory_space=pltpu.SMEM)]
        + [vmem] * 4
        + [pl.BlockSpec(memory_space=pl.ANY)],
        out_specs=[vmem, vmem],
        scratch_shapes=[pltpu.VMEM((share, features), jnp.bfloat16), pltpu.SemaphoreType.DMA],
        compiler_params=pltpu.CompilerParams(vmem_limit_bytes=SMALL_BYTES),
        cost_estimate=pl.CostEstimate(
            flops=8 * up.size, bytes_accessed=16 * up.size, transcendentals=0
        ),
        name="norm_share",
    )(info, blocks, up, down, gain, hidden)


def project_kernel(where_ref, first_ref, second_ref, weight_ref, made_ref):
    depth = first_ref.shape[-1]
    rows = jnp.concatenate(
        (first_ref[...].reshape(NLEN, depth), second_ref[...].reshape(NLEN, depth)), axis=0
    )
    made_ref[...] = jnp.dot(rows, weight_ref[...], preferred_element_type=jnp.float32).astype(
        jnp.bfloat16
    )


def project_encodings(where, table, weight):
    groups = (where.shape[0] - 2) // (2 * NEIGH)
    _, cuts, _, piece, depth = table.shape
    width = weight.shape[1]

    def entry(neighbour):
        def index(group, where_ref):
            at = 2 + 2 * (NEIGH * group + neighbour)
            return (where_ref[at], 0, where_ref[at + 1], 0, 0)

        return pl.BlockSpec((1, cuts, 1, piece, depth), index)

    return pl.pallas_call(
        project_kernel,
        out_shape=jax.ShapeDtypeStruct((groups * GROUP, width), jnp.bfloat16),
        grid_spec=pltpu.PrefetchScalarGridSpec(
            num_scalar_prefetch=1,
            grid=(groups,),
            in_specs=[
                entry(0),
                entry(1),
                pl.BlockSpec((depth, width), lambda group, where_ref: (0, 0)),
            ],
            out_specs=pl.BlockSpec((GROUP, width), lambda group, where_ref: (group, 0)),
        ),
        compiler_params=pltpu.CompilerParams(
            vmem_limit_bytes=LARGE_BYTES, dimension_semantics=("arbitrary",)
        ),
        cost_estimate=pl.CostEstimate(
            flops=2 * groups * GROUP * depth * width,
            bytes_accessed=2 * (groups * GROUP * (depth + width) + depth * width),
            transcendentals=0,
        ),
        name="project_encodings",
    )(where, table, table, weight)


def apart_heads(query):
    first = lax.broadcasted_iota(jnp.int32, query.shape, 1) < HD
    nothing = jnp.zeros_like(query)
    return jnp.concatenate(
        (jnp.where(first, query, nothing), jnp.where(first, nothing, query)), axis=0
    )


def together_heads(mixed):
    rows = mixed.shape[0] // 2
    first = lax.broadcasted_iota(jnp.int32, (rows, 2 * HD), 1) < HD
    return jnp.where(first, mixed[:rows], mixed[rows:])


def cross_kernel(info_ref, own_ref, *refs, scale):
    wq_hbm, keys_hbm, values_hbm, wo_hbm, out_ref, first_ref, second_ref = refs[-15:-8]
    wq_ref, keys_ref, values_ref, wo_ref, rows_ref, query_ref, mixed_ref, sems = refs[-8:]
    pieces = refs[:-15]
    share, features = own_ref.shape
    width = wq_ref.shape[1]
    n_db = out_ref.shape[0]
    pairs = width // HD // 2
    tail = 16
    cut = features // 4
    low = width // 4
    wq_copies = [
        pltpu.make_async_copy(
            wq_hbm.at[pl.ds(k * cut, cut)], wq_ref.at[pl.ds(k * cut, cut)], sems.at[k]
        )
        for k in range(4)
    ]
    other_copies = [
        pltpu.make_async_copy(keys_hbm, keys_ref, sems.at[4]),
        pltpu.make_async_copy(values_hbm, values_ref, sems.at[5]),
    ] + [
        pltpu.make_async_copy(
            wo_hbm.at[pl.ds(k * low, low)], wo_ref.at[pl.ds(k * low, low)], sems.at[6 + k]
        )
        for k in range(4)
    ]
    for copy in wq_copies + other_copies:
        copy.start()
    me = info_ref[0]

    def place(source, owner):
        @pl.when((owner >= 0) & (owner < n_db))
        def _():
            at = pl.multiple_of(jnp.clip(owner, 0, n_db - 1) * share, share)
            rows_ref[pl.ds(at, share), :] = source[...]

    place(own_ref, me)
    for at, source in enumerate(pieces):
        way = 1 - 2 * (at % 2)
        place(source, me - way * (at // 2 + 1))
    lanes = [slice(2 * pair * HD, 2 * (pair + 1) * HD) for pair in range(pairs)]
    for k, copy in enumerate(wq_copies):
        copy.wait()
        inner = slice(k * cut, (k + 1) * cut)
        for at in lanes:
            part = jnp.dot(
                rows_ref[:, inner], wq_ref[inner, at], preferred_element_type=jnp.float32
            )
            query_ref[:, at] = part if k == 0 else query_ref[:, at] + part
    for copy in other_copies[:2]:
        copy.wait()
    row = lax.broadcasted_iota(jnp.int32, (tail, 2 * HD), 0)
    spans = n_db * share // SPAN
    for span in range(spans):
        top = span * SPAN
        here, after = (slice((span + k) * GROUP, (span + k + 1) * GROUP) for k in (0, 1))
        work = [(slice(top, top + SPAN), here, at) for at in lanes]
        work += [(slice(top + SPAN - tail, top + SPAN), after, at) for at in lanes]
        scores = [
            lax.dot_general(
                apart_heads(query_ref[of, at].astype(jnp.bfloat16)),
                keys_ref[which, at],
                (((1,), (1,)), ((), ())),
                preferred_element_type=jnp.float32,
            )
            * (scale * LOG2E)
            for of, which, at in work
        ]
        tops = [jnp.max(one, axis=-1, keepdims=True) for one in scores]
        weights = [jnp.exp2(one - top_one) for one, top_one in zip(scores, tops)]
        totals = [jnp.sum(one, axis=-1, keepdims=True) for one in weights]
        mixed = [
            jnp.dot(
                one.astype(jnp.bfloat16), values_ref[which, at], preferred_element_type=jnp.float32
            )
            for one, (_, which, at) in zip(weights, work)
        ]
        mixed = [together_heads(one / total) for one, total in zip(mixed, totals)]
        for pair, at in enumerate(lanes):
            main, last = mixed[pair], mixed[pairs + pair]
            if span == 0:
                main = jnp.where(info_ref[1] > 0, main, 0.0)
            last = jnp.where(row == tail - 1, last, main[SPAN - tail :])
            mixed_ref[top : top + SPAN - tail, at] = main[: SPAN - tail].astype(jnp.bfloat16)
            mixed_ref[top + SPAN - tail : top + SPAN, at] = last.astype(jnp.bfloat16)
    for copy in other_copies[2:]:
        copy.wait()
    step = math.gcd(features, 512)

    def columns(at, carried):
        here = pl.ds(pl.multiple_of(at * step, step), step)
        product = jnp.dot(mixed_ref[...], wo_ref[:, here], preferred_element_type=jnp.float32)
        product = product.astype(jnp.bfloat16)
        for owner in range(n_db):
            out_ref[owner, :, here] = product[owner * share : (owner + 1) * share]
        return carried

    lax.fori_loop(0, features // step, columns, 0, unroll=4)
    first_ref[...] = out_ref[far_block(out_ref, info_ref, 0, n_db - 1)]
    second_ref[...] = out_ref[far_block(out_ref, info_ref, 1, n_db - 1)]


def cross_block(info, normed, pieces, w_cross_q, keys, values, w_cross_out, n_db, scale):
    share, features = normed.shape
    width = w_cross_q.shape[1]
    rows = n_db * share
    vmem = pl.BlockSpec(memory_space=pltpu.VMEM)
    anywhere = pl.BlockSpec(memory_space=pl.ANY)
    one = jax.ShapeDtypeStruct((share, features), jnp.bfloat16)
    flat = [one for pair in pieces for one in pair]
    return pl.pallas_call(
        functools.partial(cross_kernel, scale=scale),
        out_shape=[jax.ShapeDtypeStruct((n_db, share, features), jnp.bfloat16), one, one],
        in_specs=[pl.BlockSpec(memory_space=pltpu.SMEM)]
        + [vmem] * (1 + len(flat))
        + [anywhere] * 4,
        out_specs=[vmem] * 3,
        scratch_shapes=[
            pltpu.VMEM((features, width), jnp.bfloat16),
            pltpu.VMEM(keys.shape, jnp.bfloat16),
            pltpu.VMEM(values.shape, jnp.bfloat16),
            pltpu.VMEM((width, features), jnp.bfloat16),
            pltpu.VMEM((rows, features), jnp.bfloat16),
            pltpu.VMEM((rows, width), jnp.float32),
            pltpu.VMEM((rows, width), jnp.bfloat16),
            pltpu.SemaphoreType.DMA((10,)),
        ],
        compiler_params=pltpu.CompilerParams(vmem_limit_bytes=VMEM_BYTES),
        cost_estimate=pl.CostEstimate(
            flops=4 * rows * width * (features + GROUP),
            bytes_accessed=4 * width * (features + keys.shape[0]) + 4 * rows * features,
            transcendentals=rows * GROUP * width // HD,
        ),
        name="cross_block",
    )(info, normed, *flat, w_cross_q, keys, values, w_cross_out)


def per_device(
    hidden_in,
    query_rows,
    key_rows,
    value_rows,
    w_self_out,
    norm_gain,
    w_cross_q,
    w_cross_k,
    w_cross_v,
    w_cross_out,
    enc_table,
    nb_shard,
    nb_row,
):
    features = hidden_in.shape[1]
    heads = query_rows.shape[1] // HD
    n_seq, n_db = lax.axis_size("seq"), lax.axis_size("db")
    seq_index, db_index = lax.axis_index("seq"), lax.axis_index("db")
    scale = 1.0 / math.sqrt(HD)

    rows_shard, _, depth = enc_table.shape
    encodings = enc_table.reshape(rows_shard * NLEN, depth)
    piece = rows_shard * NLEN // n_seq
    packed, part = pack_heads(
        seq_index.reshape(1).astype(jnp.int32), query_rows, key_rows, value_rows, encodings, piece
    )
    along_db = lax.all_gather(part, "db", axis=0)

    packed, nb_row, nb_shard = lax.optimization_barrier((packed, nb_row, nb_shard))
    wanted = jnp.stack((nb_row, nb_shard), axis=-1).astype(jnp.int32)
    place = jnp.stack((db_index, (seq_index > 0).astype(jnp.int32))).astype(jnp.int32)
    info = jnp.concatenate((place, span_before(wanted).reshape(-1), wanted.reshape(-1)))
    if heads == n_seq:
        held = lax.all_to_all(packed, "seq", 0, 0, tiled=True)
        held, info = lax.optimization_barrier((held, info))
        attended = lax.all_to_all(self_attend_head(held, scale), "seq", 0, 0, tiled=True)
    else:
        attended = self_attention_gathered(query_rows, key_rows, value_rows, scale)

    along_db, attended = lax.optimization_barrier((along_db, attended))
    table = lax.all_gather(along_db, "seq", axis=0).reshape(
        rows_shard, NLEN // piece, n_db, piece, depth
    )

    partial, up, down = self_out(info, attended, w_self_out, n_db)
    up, down = reduce_scatter(info, partial, up, down)
    residual, normed = norm_share(
        info, partial, up, down, norm_gain.reshape(1, features), hidden_in
    )
    projected = [project_encodings(info, table, weight) for weight in (w_cross_k, w_cross_v)]
    pieces, (keys, values) = gather(normed, projected)
    partial, up, down = cross_block(
        info, normed, pieces, w_cross_q, keys, values, w_cross_out, n_db, scale
    )
    up, down = reduce_scatter(info, partial, up, down)
    own = lax.dynamic_index_in_dim(partial, db_index, 0, keepdims=False).astype(jnp.float32)
    return residual + own + up.astype(jnp.float32) + down.astype(jnp.float32)


def solution(mesh):
    placed = (
        P("seq", None),
        P("seq", "db"),
        P("seq", "db"),
        P("seq", "db"),
        P("db", None),
        P(),
        P(None, "db"),
        P(None, "db"),
        P(None, "db"),
        P("db", None),
        P("db", None, None),
        P("seq", None),
        P("seq", None),
    )
    return jax.shard_map(
        per_device, mesh=mesh, in_specs=placed, out_specs=P(("seq", "db"), None), check_vma=False
    )
```

```python
import functools
import math

import jax
import jax.numpy as jnp
from jax import lax
from jax.experimental import pallas as pl
from jax.experimental.pallas import tpu as pltpu
from jax.sharding import PartitionSpec as P

HD = 128
SPAN = 64
NEIGH = 2
NLEN = 128
GROUP = NEIGH * NLEN

NEG_BIG = -1e30
LOG2E = 1.4426950408889634
VMEM_BYTES = 48 * 1024 * 1024
LARGE_BYTES = 58 * 1024 * 1024
SMALL_BYTES = 4 * 1024 * 1024


def shift(block, axis, distance, senders):
    size = lax.axis_size(axis)
    route = [(k, k + distance) for k in senders if 0 <= k + distance < size]
    return lax.ppermute(block, axis, route)


def line_shift(block, lead, up_from, down_from):
    n_seq, size = lax.axis_size("seq"), lax.axis_size("db")
    route = []
    for row in range(n_seq):
        up = lead == 0
        for k in up_from if up else down_from:
            other = k + 1 if up else k - 1
            if 0 <= other < size:
                route.append((row * size + k, row * size + other))
    return lax.ppermute(block, ("seq", "db"), route)


def far_block(blocks_ref, info_ref, lead, far):
    way = 1 - 2 * lead
    return jnp.clip(info_ref[0] + way * far, 0, blocks_ref.shape[0] - 1)


def add_kernel(info_ref, blocks_ref, up_ref, down_ref, up_out_ref, down_out_ref, *, far):
    rows = 16

    def add(at, carried):
        here = pl.ds(pl.multiple_of(at * rows, rows), rows)
        for lead, ref, out_ref in ((0, up_ref, up_out_ref), (1, down_ref, down_out_ref)):
            index = far_block(blocks_ref, info_ref, lead, far)
            out_ref[here, :] = (
                blocks_ref[index, here, :].astype(jnp.float32) + ref[here, :].astype(jnp.float32)
            ).astype(jnp.bfloat16)
        return carried

    lax.fori_loop(0, up_ref.shape[0] // rows, add, 0)


def add_step(info, blocks, up, down, far):
    vmem = pl.BlockSpec(memory_space=pltpu.VMEM)
    one = jax.ShapeDtypeStruct(up.shape, up.dtype)
    return pl.pallas_call(
        functools.partial(add_kernel, far=far),
        out_shape=[one, one],
        in_specs=[pl.BlockSpec(memory_space=pltpu.SMEM), vmem, vmem, vmem],
        out_specs=[vmem, vmem],
        compiler_params=pltpu.CompilerParams(vmem_limit_bytes=SMALL_BYTES),
        cost_estimate=pl.CostEstimate(
            flops=2 * up.size, bytes_accessed=12 * up.size, transcendentals=0
        ),
        name="add_step",
    )(info, blocks, up, down)


def reduce_scatter(info, blocks, up, down):
    size = lax.axis_size("db")
    for step in range(size - 1):
        senders = (range(step + 1), range(size - 1 - step, size))
        if step:
            up, down = add_step(info, blocks, up, down, size - 1 - step)
        down = line_shift(down, 1, *senders)
        up = line_shift(up, 0, *senders)
        down, up = lax.optimization_barrier((down, up))
    return up, down


def plane_swap(block, mask):
    return lax.ppermute(block, "seq", [(i, i ^ mask) for i in range(8)])


def plane_pieces(own):
    same = lax.optimization_barrier((own,) + tuple(plane_swap(own, mask) for mask in (2, 4, 6)))
    return same + tuple(plane_swap(one, 1) for one in same)


def plane_slot(owner, me):
    apart = owner ^ me
    return (apart >> 1) + 4 * (apart & 1)


def self_kernel(qkv_ref, out_ref, *, blocks, rows, scale):
    for block in range(blocks):
        query = qkv_ref[block, 0]
        live = (block + 1) * rows
        keys = qkv_ref[0 : block + 1, 1].reshape(live, HD)
        values = qkv_ref[0 : block + 1, 2].reshape(live, HD)
        scores = lax.dot_general(
            query, keys, (((1,), (1,)), ((), ())), preferred_element_type=jnp.float32
        )
        query_pos = block * rows + lax.broadcasted_iota(jnp.int32, (rows, live), 0)
        key_pos = lax.broadcasted_iota(jnp.int32, (rows, live), 1)
        scores = jnp.where(key_pos <= query_pos, scores * (scale * LOG2E), NEG_BIG)
        top = jnp.max(scores, axis=-1, keepdims=True)
        weights = jnp.exp2(scores - top)
        total = jnp.sum(weights, axis=-1, keepdims=True)
        mixed = jnp.dot(weights.astype(jnp.bfloat16), values, preferred_element_type=jnp.float32)
        out_ref[block] = (mixed / total).astype(jnp.bfloat16)


def self_attend_head(qkv, scale):
    blocks, _, rows, _ = qkv.shape
    return pl.pallas_call(
        functools.partial(self_kernel, blocks=blocks, rows=rows, scale=scale),
        out_shape=jax.ShapeDtypeStruct((blocks, rows, HD), jnp.bfloat16),
        in_specs=[pl.BlockSpec(memory_space=pltpu.VMEM)],
        out_specs=pl.BlockSpec(memory_space=pltpu.VMEM),
        compiler_params=pltpu.CompilerParams(vmem_limit_bytes=VMEM_BYTES),
        cost_estimate=pl.CostEstimate(
            flops=2 * blocks * blocks * rows * rows * HD,
            bytes_accessed=8 * blocks * rows * HD,
            transcendentals=blocks * blocks * rows * rows // 2,
        ),
        name="self_attend",
    )(qkv)


def span_before(wanted):
    return shift(wanted[-1], "seq", 1, range(lax.axis_size("seq")))


def pack_kernel(index_ref, query_ref, key_ref, value_ref, part_ref, out_ref, part_out_ref):
    for which, ref in enumerate((query_ref, key_ref, value_ref)):
        for head in range(out_ref.shape[0]):
            out_ref[head, which] = ref[:, head * HD : (head + 1) * HD]
    part_out_ref[...] = part_ref[...]


def pack_heads(index, query_rows, key_rows, value_rows, encodings, piece):
    rows, width = query_rows.shape
    heads = width // HD
    depth = encodings.shape[1]
    steps = 4
    block, part = rows // steps, piece // steps
    row_block = pl.BlockSpec((block, width), lambda at, index_ref: (at, 0))
    return pl.pallas_call(
        pack_kernel,
        out_shape=[
            jax.ShapeDtypeStruct((heads, 3, rows, HD), jnp.bfloat16),
            jax.ShapeDtypeStruct((piece, depth), jnp.bfloat16),
        ],
        grid_spec=pltpu.PrefetchScalarGridSpec(
            num_scalar_prefetch=1,
            grid=(steps,),
            in_specs=[row_block] * 3
            + [pl.BlockSpec((part, depth), lambda at, index_ref: (index_ref[0] * steps + at, 0))],
            out_specs=[
                pl.BlockSpec((heads, 3, block, HD), lambda at, index_ref: (0, 0, at, 0)),
                pl.BlockSpec((part, depth), lambda at, index_ref: (at, 0)),
            ],
        ),
        compiler_params=pltpu.CompilerParams(
            vmem_limit_bytes=LARGE_BYTES, dimension_semantics=("arbitrary",)
        ),
        cost_estimate=pl.CostEstimate(
            flops=0, bytes_accessed=12 * rows * width, transcendentals=0
        ),
        name="pack_heads",
    )(index, query_rows, key_rows, value_rows, encodings)


def self_attention_gathered(query_rows, key_rows, value_rows, scale):
    rows, width = query_rows.shape
    heads = width // HD
    keys = lax.all_gather(key_rows, "seq", axis=0, tiled=True)
    values = lax.all_gather(value_rows, "seq", axis=0, tiled=True)
    count = keys.shape[0]
    query_pos = lax.axis_index("seq") * rows + jnp.arange(rows, dtype=jnp.int32)
    allowed = jnp.arange(count, dtype=jnp.int32)[None, :] <= query_pos[:, None]
    scores = (
        jnp.einsum(
            "qhd,khd->hqk",
            query_rows.reshape(rows, heads, HD),
            keys.reshape(count, heads, HD),
            preferred_element_type=jnp.float32,
        )
        * scale
    )
    scores = jnp.where(allowed[None], scores, NEG_BIG)
    weights = jnp.exp(scores - jnp.max(scores, axis=-1, keepdims=True))
    total = jnp.sum(weights, axis=-1)
    mixed = jnp.einsum(
        "hqk,khd->hqd",
        weights.astype(jnp.bfloat16),
        values.reshape(count, heads, HD),
        preferred_element_type=jnp.float32,
    )
    return (mixed / total[..., None]).astype(jnp.bfloat16)


def self_out_kernel(
    attended_ref, weight_hbm, out_ref, rows_ref, weight_ref, sum_ref, sems
):
    heads, rows, _ = attended_ref.shape
    features = out_ref.shape[1]
    width = weight_hbm.shape[0]
    cuts = 4
    depth = width // cuts
    copies = [
        pltpu.make_async_copy(
            weight_hbm.at[pl.ds(k * depth, depth)], weight_ref.at[pl.ds(k * depth, depth)], sems.at[k]
        )
        for k in range(cuts)
    ]
    for copy in copies:
        copy.start()
    for head in range(heads):
        rows_ref[:, head * HD : (head + 1) * HD] = attended_ref[head]
    step = math.gcd(features, 512)

    def columns(at, carried, begin, end):
        here = pl.ds(pl.multiple_of(at * step, step), step)
        inner = slice(begin * depth, end * depth)
        product = jnp.dot(
            rows_ref[:, inner], weight_ref[inner, here], preferred_element_type=jnp.float32
        )
        if begin == 0:
            sum_ref[:, here] = product
            return carried
        out_ref[:, here] = (product + sum_ref[:, here]).astype(jnp.bfloat16)
        return carried

    for begin, end in ((0, cuts // 2), (cuts // 2, cuts)):
        for copy in copies[begin:end]:
            copy.wait()
        lax.fori_loop(
            0, features // step, functools.partial(columns, begin=begin, end=end), 0, unroll=4
        )


def self_out(attended, weight):
    heads, rows, _ = attended.shape
    width, features = weight.shape
    vmem = pl.BlockSpec(memory_space=pltpu.VMEM)
    return pl.pallas_call(
        self_out_kernel,
        out_shape=jax.ShapeDtypeStruct((rows, features), jnp.bfloat16),
        in_specs=[vmem, pl.BlockSpec(memory_space=pl.ANY)],
        out_specs=vmem,
        scratch_shapes=[
            pltpu.VMEM((rows, width), jnp.bfloat16),
            pltpu.VMEM((width, features), jnp.bfloat16),
            pltpu.VMEM((rows, features), jnp.float32),
            pltpu.SemaphoreType.DMA((4,)),
        ],
        compiler_params=pltpu.CompilerParams(vmem_limit_bytes=VMEM_BYTES),
        cost_estimate=pl.CostEstimate(
            flops=2 * rows * width * features,
            bytes_accessed=2 * (rows * width + width * features + rows * features),
            transcendentals=0,
        ),
        name="self_out",
    )(attended, weight)


def project_kernel(where_ref, *refs, cuts):
    wk_hbm, wv_hbm, keys_ref, values_ref = refs[-8:-4]
    rows_ref, wk_ref, wv_ref, sems = refs[-4:]
    tables = refs[:-8]
    entries = keys_ref.shape[0] // NLEN
    piece = NLEN // cuts
    bring = [
        pltpu.make_async_copy(source, target, sems.at[entries * cuts + at])
        for at, (source, target) in enumerate(
            ((wk_hbm, wk_ref), (wv_hbm, wv_ref))
        )
    ]
    for copy in bring:
        copy.start()

    def entry_copy(entry, cut, table, first, shard):
        return pltpu.make_async_copy(
            table.at[first + cut, shard],
            rows_ref.at[pl.ds(entry * NLEN + cut * piece, piece)],
            sems.at[entry * cuts + cut],
        )

    for entry in range(entries):
        for slot, table in enumerate(tables):

            @pl.when(where_ref[2 + 3 * entry] == slot)
            def _(entry=entry, table=table):
                for cut in range(cuts):
                    entry_copy(
                        entry, cut, table, where_ref[3 + 3 * entry], where_ref[4 + 3 * entry]
                    ).start()

    for copy in bring:
        copy.wait()
    width = keys_ref.shape[1]
    step = math.gcd(width, 512)
    for group in range(entries // NEIGH):
        for entry in range(NEIGH * group, NEIGH * (group + 1)):
            for cut in range(cuts):
                entry_copy(entry, cut, tables[0], 0, 0).wait()
        here = slice(group * GROUP, (group + 1) * GROUP)
        for at in range(0, width, step):
            lanes = slice(at, at + step)
            for weight, made in ((wk_ref, keys_ref), (wv_ref, values_ref)):
                made[here, lanes] = jnp.dot(
                    rows_ref[here, :], weight[:, lanes], preferred_element_type=jnp.float32
                ).astype(jnp.bfloat16)


def project_encodings(where, tables, w_cross_k, w_cross_v):
    entries = (where.shape[0] - 2) // 3
    piece, depth = tables[0].shape[2:]
    cuts = NLEN // piece
    width = w_cross_k.shape[1]
    vmem = pl.BlockSpec(memory_space=pltpu.VMEM)
    anywhere = pl.BlockSpec(memory_space=pl.ANY)
    made = jax.ShapeDtypeStruct((entries * NLEN, width), jnp.bfloat16)
    return pl.pallas_call(
        functools.partial(project_kernel, cuts=cuts),
        out_shape=[made, made],
        in_specs=[pl.BlockSpec(memory_space=pltpu.SMEM)] + [anywhere] * (len(tables) + 2),
        out_specs=[vmem] * 2,
        scratch_shapes=[
            pltpu.VMEM((entries * NLEN, depth), jnp.bfloat16),
            pltpu.VMEM(w_cross_k.shape, jnp.bfloat16),
            pltpu.VMEM(w_cross_v.shape, jnp.bfloat16),
            pltpu.SemaphoreType.DMA((entries * cuts + 2,)),
        ],
        compiler_params=pltpu.CompilerParams(vmem_limit_bytes=VMEM_BYTES),
        cost_estimate=pl.CostEstimate(
            flops=entries * NLEN * depth,
            bytes_accessed=2 * entries * NLEN * depth,
            transcendentals=0,
        ),
        name="project_encodings",
    )(where, *tables, w_cross_k, w_cross_v)


def apart_heads(query):
    first = lax.broadcasted_iota(jnp.int32, query.shape, 1) < HD
    nothing = jnp.zeros_like(query)
    return jnp.concatenate(
        (jnp.where(first, query, nothing), jnp.where(first, nothing, query)), axis=0
    )


def together_heads(mixed):
    rows = mixed.shape[0] // 2
    first = lax.broadcasted_iota(jnp.int32, (rows, 2 * HD), 1) < HD
    return jnp.where(first, mixed[:rows], mixed[rows:])


def cross_kernel(
    info_ref,
    hidden_ref,
    total_ref,
    gain_ref,
    wq_hbm,
    keys_hbm,
    values_hbm,
    wo_hbm,
    out_ref,
    residual_ref,
    first_ref,
    second_ref,
    wq_ref,
    keys_ref,
    values_ref,
    wo_ref,
    rows_ref,
    query_ref,
    mixed_ref,
    sems,
    *,
    scale,
):
    rows, features = hidden_ref.shape
    n_db, share, _ = out_ref.shape
    width = wq_ref.shape[1]
    pairs = width // HD // 2
    tail = 16
    cut = features // 4
    low = width // 4
    wq_copies = [
        pltpu.make_async_copy(
            wq_hbm.at[pl.ds(k * cut, cut)], wq_ref.at[pl.ds(k * cut, cut)], sems.at[k]
        )
        for k in range(4)
    ]
    other_copies = [
        pltpu.make_async_copy(keys_hbm, keys_ref, sems.at[4]),
        pltpu.make_async_copy(values_hbm, values_ref, sems.at[5]),
    ] + [
        pltpu.make_async_copy(
            wo_hbm.at[pl.ds(k * low, low)], wo_ref.at[pl.ds(k * low, low)], sems.at[6 + k]
        )
        for k in range(4)
    ]
    for copy in wq_copies + other_copies:
        copy.start()
    block = math.gcd(rows, 32)

    def norm(at, carried):
        here = pl.ds(pl.multiple_of(at * block, block), block)
        residual = hidden_ref[here, :].astype(jnp.float32) + total_ref[here, :].astype(jnp.float32)
        mean_square = jnp.mean(residual * residual, axis=-1, keepdims=True)
        rows_ref[here, :] = (
            residual * lax.rsqrt(mean_square + 1e-05) * gain_ref[...].astype(jnp.float32)
        ).astype(jnp.bfloat16)
        return carried

    lax.fori_loop(0, rows // block, norm, 0)
    own = pl.ds(pl.multiple_of(info_ref[0] * share, share), share)
    residual_ref[...] = hidden_ref[own, :].astype(jnp.float32) + total_ref[own, :].astype(
        jnp.float32
    )
    lanes = [slice(2 * pair * HD, 2 * (pair + 1) * HD) for pair in range(pairs)]
    for k, copy in enumerate(wq_copies):
        copy.wait()
        inner = slice(k * cut, (k + 1) * cut)
        for at in lanes:
            part = jnp.dot(
                rows_ref[:, inner], wq_ref[inner, at], preferred_element_type=jnp.float32
            )
            query_ref[:, at] = part if k == 0 else query_ref[:, at] + part
    for copy in other_copies[:2]:
        copy.wait()
    row = lax.broadcasted_iota(jnp.int32, (tail, 2 * HD), 0)
    spans = rows // SPAN
    for span in range(spans):
        top = span * SPAN
        here, after = (slice((span + k) * GROUP, (span + k + 1) * GROUP) for k in (0, 1))
        work = [(slice(top, top + SPAN), here, at) for at in lanes]
        work += [(slice(top + SPAN - tail, top + SPAN), after, at) for at in lanes]
        scores = [
            lax.dot_general(
                apart_heads(query_ref[of, at].astype(jnp.bfloat16)),
                keys_ref[which, at],
                (((1,), (1,)), ((), ())),
                preferred_element_type=jnp.float32,
            )
            * (scale * LOG2E)
            for of, which, at in work
        ]
        tops = [jnp.max(one, axis=-1, keepdims=True) for one in scores]
        weights = [jnp.exp2(one - top_one) for one, top_one in zip(scores, tops)]
        totals = [jnp.sum(one, axis=-1, keepdims=True) for one in weights]
        mixed = [
            jnp.dot(
                one.astype(jnp.bfloat16), values_ref[which, at], preferred_element_type=jnp.float32
            )
            for one, (_, which, at) in zip(weights, work)
        ]
        mixed = [together_heads(one / total) for one, total in zip(mixed, totals)]
        for pair, at in enumerate(lanes):
            main, last = mixed[pair], mixed[pairs + pair]
            if span == 0:
                main = jnp.where(info_ref[1] > 0, main, 0.0)
            last = jnp.where(row == tail - 1, last, main[SPAN - tail :])
            mixed_ref[top : top + SPAN - tail, at] = main[: SPAN - tail].astype(jnp.bfloat16)
            mixed_ref[top + SPAN - tail : top + SPAN, at] = last.astype(jnp.bfloat16)
    for copy in other_copies[2:]:
        copy.wait()
    step = math.gcd(features, 512)

    def columns(at, carried):
        here = pl.ds(pl.multiple_of(at * step, step), step)
        product = jnp.dot(mixed_ref[...], wo_ref[:, here], preferred_element_type=jnp.float32)
        product = product.astype(jnp.bfloat16)
        for owner in range(n_db):
            out_ref[owner, :, here] = product[owner * share : (owner + 1) * share]
        return carried

    lax.fori_loop(0, features // step, columns, 0, unroll=4)
    first_ref[...] = out_ref[far_block(out_ref, info_ref, 0, n_db - 1)]
    second_ref[...] = out_ref[far_block(out_ref, info_ref, 1, n_db - 1)]


def cross_block(info, hidden, total, gain, w_cross_q, keys, values, w_cross_out, n_db, scale):
    rows, features = hidden.shape
    share = rows // n_db
    width = w_cross_q.shape[1]
    vmem = pl.BlockSpec(memory_space=pltpu.VMEM)
    anywhere = pl.BlockSpec(memory_space=pl.ANY)
    one = jax.ShapeDtypeStruct((share, features), jnp.bfloat16)
    return pl.pallas_call(
        functools.partial(cross_kernel, scale=scale),
        out_shape=[
            jax.ShapeDtypeStruct((n_db, share, features), jnp.bfloat16),
            jax.ShapeDtypeStruct((share, features), jnp.float32),
            one,
            one,
        ],
        in_specs=[pl.BlockSpec(memory_space=pltpu.SMEM)] + [vmem] * 3 + [anywhere] * 4,
        out_specs=[vmem] * 4,
        scratch_shapes=[
            pltpu.VMEM((features, width), jnp.bfloat16),
            pltpu.VMEM(keys.shape, jnp.bfloat16),
            pltpu.VMEM(values.shape, jnp.bfloat16),
            pltpu.VMEM((width, features), jnp.bfloat16),
            pltpu.VMEM((rows, features), jnp.bfloat16),
            pltpu.VMEM((rows, width), jnp.float32),
            pltpu.VMEM((rows, width), jnp.bfloat16),
            pltpu.SemaphoreType.DMA((10,)),
        ],
        compiler_params=pltpu.CompilerParams(vmem_limit_bytes=VMEM_BYTES),
        cost_estimate=pl.CostEstimate(
            flops=4 * rows * width * (features + GROUP),
            bytes_accessed=4 * width * (features + keys.shape[0]) + 8 * rows * features,
            transcendentals=rows * GROUP * width // HD,
        ),
        name="cross_block",
    )(info, hidden, total, gain, w_cross_q, keys, values, w_cross_out)


def per_device(
    hidden_in,
    query_rows,
    key_rows,
    value_rows,
    w_self_out,
    norm_gain,
    w_cross_q,
    w_cross_k,
    w_cross_v,
    w_cross_out,
    enc_table,
    nb_shard,
    nb_row,
):
    features = hidden_in.shape[1]
    heads = query_rows.shape[1] // HD
    n_seq, n_db = lax.axis_size("seq"), lax.axis_size("db")
    seq_index, db_index = lax.axis_index("seq"), lax.axis_index("db")
    scale = 1.0 / math.sqrt(HD)

    rows_shard, _, depth = enc_table.shape
    encodings = enc_table.reshape(rows_shard * NLEN, depth)
    piece = rows_shard * NLEN // n_seq
    packed, part = pack_heads(
        seq_index.reshape(1).astype(jnp.int32), query_rows, key_rows, value_rows, encodings, piece
    )
    along_db = lax.all_gather(part, "db", axis=0)

    packed, nb_row, nb_shard = lax.optimization_barrier((packed, nb_row, nb_shard))
    wanted = jnp.stack((nb_row, nb_shard), axis=-1).astype(jnp.int32)
    place = jnp.stack((db_index, (seq_index > 0).astype(jnp.int32))).astype(jnp.int32)
    nearest = jnp.concatenate((span_before(wanted)[None], wanted), axis=0)
    row, shard = nearest[..., 0], nearest[..., 1]
    in_plane = n_seq == 8 and piece == NLEN
    if in_plane:
        where = jnp.stack((plane_slot(row, seq_index), jnp.zeros_like(row), shard), axis=-1)
    else:
        where = jnp.stack((jnp.zeros_like(row), row * (NLEN // piece), shard), axis=-1)
    info = jnp.concatenate((place, where.reshape(-1))).astype(jnp.int32)
    if heads == n_seq:
        held = lax.all_to_all(packed, "seq", 0, 0, tiled=True)
        held, info = lax.optimization_barrier((held, info))
        attended = lax.all_to_all(self_attend_head(held, scale), "seq", 0, 0, tiled=True)
    else:
        attended = self_attention_gathered(query_rows, key_rows, value_rows, scale)

    along_db, attended = lax.optimization_barrier((along_db, attended))
    partial = self_out(attended, w_self_out)
    along_db, partial = lax.optimization_barrier((along_db, partial))
    total = lax.psum(partial, "db")
    if in_plane:
        tables = tuple(one[None] for one in plane_pieces(along_db))
    else:
        tables = (lax.all_gather(along_db, "seq", axis=0),)
    projected = project_encodings(info, tables, w_cross_k, w_cross_v)
    total, (keys, values) = lax.optimization_barrier((total, projected))

    partial, residual, up, down = cross_block(
        info,
        hidden_in,
        total,
        norm_gain.reshape(1, features),
        w_cross_q,
        keys,
        values,
        w_cross_out,
        n_db,
        scale,
    )
    up, down = reduce_scatter(info, partial, up, down)
    own = lax.dynamic_index_in_dim(partial, db_index, 0, keepdims=False).astype(jnp.float32)
    return residual + own + up.astype(jnp.float32) + down.astype(jnp.float32)


def solution(mesh):
    placed = (
        P("seq", None),
        P("seq", "db"),
        P("seq", "db"),
        P("seq", "db"),
        P("db", None),
        P(),
        P(None, "db"),
        P(None, "db"),
        P(None, "db"),
        P("db", None),
        P("db", None, None),
        P("seq", None),
        P("seq", None),
    )
    return jax.shard_map(
        per_device, mesh=mesh, in_specs=placed, out_specs=P(("seq", "db"), None), check_vma=False
    )
```

```python
import functools
import math

import jax
import jax.numpy as jnp
from jax import lax
from jax.experimental import pallas as pl
from jax.experimental.pallas import tpu as pltpu
from jax.sharding import PartitionSpec as P

HD = 128
SPAN = 64
NEIGH = 2
NLEN = 128
GROUP = NEIGH * NLEN

NEG_BIG = -1e30
LOG2E = 1.4426950408889634
VMEM_BYTES = 48 * 1024 * 1024
LARGE_BYTES = 58 * 1024 * 1024


def shift(block, axis, distance, senders):
    size = lax.axis_size(axis)
    route = [(k, k + distance) for k in senders if 0 <= k + distance < size]
    return lax.ppermute(block, axis, route)


def plane_swap(block, mask):
    return lax.ppermute(block, "seq", [(i, i ^ mask) for i in range(8)])


def plane_pieces(own, after):
    same = (own,) + tuple(plane_swap(own, mask) for mask in (2, 4, 6))
    same, after = lax.optimization_barrier((same, after))
    return same + tuple(plane_swap(one, 1) for one in same), after


def plane_slot(owner, me):
    apart = owner ^ me
    return (apart >> 1) + 4 * (apart & 1)


def self_kernel(qkv_ref, out_ref, *, blocks, rows, scale):
    for block in range(blocks):
        query = qkv_ref[block, 0]
        live = (block + 1) * rows
        keys = qkv_ref[0 : block + 1, 1].reshape(live, HD)
        values = qkv_ref[0 : block + 1, 2].reshape(live, HD)
        scores = lax.dot_general(
            query, keys, (((1,), (1,)), ((), ())), preferred_element_type=jnp.float32
        )
        query_pos = block * rows + lax.broadcasted_iota(jnp.int32, (rows, live), 0)
        key_pos = lax.broadcasted_iota(jnp.int32, (rows, live), 1)
        scores = jnp.where(key_pos <= query_pos, scores * (scale * LOG2E), NEG_BIG)
        top = jnp.max(scores, axis=-1, keepdims=True)
        weights = jnp.exp2(scores - top)
        total = jnp.sum(weights, axis=-1, keepdims=True)
        mixed = jnp.dot(weights.astype(jnp.bfloat16), values, preferred_element_type=jnp.float32)
        out_ref[block] = (mixed / total).astype(jnp.bfloat16)


def self_attend_head(qkv, scale):
    blocks, _, rows, _ = qkv.shape
    return pl.pallas_call(
        functools.partial(self_kernel, blocks=blocks, rows=rows, scale=scale),
        out_shape=jax.ShapeDtypeStruct((blocks, rows, HD), jnp.bfloat16),
        in_specs=[pl.BlockSpec(memory_space=pltpu.VMEM)],
        out_specs=pl.BlockSpec(memory_space=pltpu.VMEM),
        compiler_params=pltpu.CompilerParams(vmem_limit_bytes=VMEM_BYTES),
        cost_estimate=pl.CostEstimate(
            flops=2 * blocks * blocks * rows * rows * HD,
            bytes_accessed=8 * blocks * rows * HD,
            transcendentals=blocks * blocks * rows * rows // 2,
        ),
        name="self_attend",
    )(qkv)


def span_before(wanted):
    return shift(wanted[-1], "seq", 1, range(lax.axis_size("seq")))


def pack_kernel(index_ref, query_ref, key_ref, value_ref, part_ref, out_ref, part_out_ref):
    for which, ref in enumerate((query_ref, key_ref, value_ref)):
        for head in range(out_ref.shape[0]):
            out_ref[head, which] = ref[:, head * HD : (head + 1) * HD]
    part_out_ref[...] = part_ref[...]


def pack_heads(index, query_rows, key_rows, value_rows, encodings, piece):
    rows, width = query_rows.shape
    heads = width // HD
    depth = encodings.shape[1]
    steps = 4
    block, part = rows // steps, piece // steps
    row_block = pl.BlockSpec((block, width), lambda at, index_ref: (at, 0))
    return pl.pallas_call(
        pack_kernel,
        out_shape=[
            jax.ShapeDtypeStruct((heads, 3, rows, HD), jnp.bfloat16),
            jax.ShapeDtypeStruct((piece, depth), jnp.bfloat16),
        ],
        grid_spec=pltpu.PrefetchScalarGridSpec(
            num_scalar_prefetch=1,
            grid=(steps,),
            in_specs=[row_block] * 3
            + [pl.BlockSpec((part, depth), lambda at, index_ref: (index_ref[0] * steps + at, 0))],
            out_specs=[
                pl.BlockSpec((heads, 3, block, HD), lambda at, index_ref: (0, 0, at, 0)),
                pl.BlockSpec((part, depth), lambda at, index_ref: (at, 0)),
            ],
        ),
        compiler_params=pltpu.CompilerParams(
            vmem_limit_bytes=LARGE_BYTES, dimension_semantics=("arbitrary",)
        ),
        cost_estimate=pl.CostEstimate(
            flops=0, bytes_accessed=12 * rows * width, transcendentals=0
        ),
        name="pack_heads",
    )(index, query_rows, key_rows, value_rows, encodings)


def self_attention_gathered(query_rows, key_rows, value_rows, scale):
    rows, width = query_rows.shape
    heads = width // HD
    keys = lax.all_gather(key_rows, "seq", axis=0, tiled=True)
    values = lax.all_gather(value_rows, "seq", axis=0, tiled=True)
    count = keys.shape[0]
    query_pos = lax.axis_index("seq") * rows + jnp.arange(rows, dtype=jnp.int32)
    allowed = jnp.arange(count, dtype=jnp.int32)[None, :] <= query_pos[:, None]
    scores = (
        jnp.einsum(
            "qhd,khd->hqk",
            query_rows.reshape(rows, heads, HD),
            keys.reshape(count, heads, HD),
            preferred_element_type=jnp.float32,
        )
        * scale
    )
    scores = jnp.where(allowed[None], scores, NEG_BIG)
    weights = jnp.exp(scores - jnp.max(scores, axis=-1, keepdims=True))
    total = jnp.sum(weights, axis=-1)
    mixed = jnp.einsum(
        "hqk,khd->hqd",
        weights.astype(jnp.bfloat16),
        values.reshape(count, heads, HD),
        preferred_element_type=jnp.float32,
    )
    return (mixed / total[..., None]).astype(jnp.bfloat16)


def self_out_kernel(
    attended_ref, weight_hbm, first_ref, second_ref, rows_ref, weight_ref, sum_ref, sems, *, n_db
):
    heads, rows, _ = attended_ref.shape
    features = first_ref.shape[1]
    half = rows // n_db // 2
    width = weight_hbm.shape[0]
    cuts = 4
    depth = width // cuts
    copies = [
        pltpu.make_async_copy(
            weight_hbm.at[pl.ds(k * depth, depth)], weight_ref.at[pl.ds(k * depth, depth)], sems.at[k]
        )
        for k in range(cuts)
    ]
    for copy in copies:
        copy.start()
    for chunk in range(2):
        for owner in range(n_db):
            source = (2 * owner + chunk) * half
            target = (chunk * n_db + owner) * half
            for head in range(heads):
                rows_ref[target : target + half, head * HD : (head + 1) * HD] = attended_ref[
                    head, source : source + half, :
                ]
    step = math.gcd(features, 512)

    def columns(at, carried, begin, end):
        here = pl.ds(pl.multiple_of(at * step, step), step)
        inner = slice(begin * depth, end * depth)
        product = jnp.dot(
            rows_ref[:, inner], weight_ref[inner, here], preferred_element_type=jnp.float32
        )
        if begin == 0:
            sum_ref[:, here] = product
            return carried
        product = (product + sum_ref[:, here]).astype(jnp.bfloat16)
        first_ref[:, here] = product[: rows // 2]
        second_ref[:, here] = product[rows // 2 :]
        return carried

    for begin, end in ((0, cuts // 2), (cuts // 2, cuts)):
        for copy in copies[begin:end]:
            copy.wait()
        lax.fori_loop(
            0, features // step, functools.partial(columns, begin=begin, end=end), 0, unroll=4
        )


def self_out(attended, weight, n_db):
    heads, rows, _ = attended.shape
    width, features = weight.shape
    vmem = pl.BlockSpec(memory_space=pltpu.VMEM)
    return pl.pallas_call(
        functools.partial(self_out_kernel, n_db=n_db),
        out_shape=[jax.ShapeDtypeStruct((rows // 2, features), jnp.bfloat16)] * 2,
        in_specs=[vmem, pl.BlockSpec(memory_space=pl.ANY)],
        out_specs=[vmem] * 2,
        scratch_shapes=[
            pltpu.VMEM((rows, width), jnp.bfloat16),
            pltpu.VMEM((width, features), jnp.bfloat16),
            pltpu.VMEM((rows, features), jnp.float32),
            pltpu.SemaphoreType.DMA((4,)),
        ],
        compiler_params=pltpu.CompilerParams(vmem_limit_bytes=VMEM_BYTES),
        cost_estimate=pl.CostEstimate(
            flops=2 * rows * width * features,
            bytes_accessed=2 * (rows * width + width * features + rows * features),
            transcendentals=0,
        ),
        name="self_out",
    )(attended, weight)


def project_kernel(where_ref, *refs, cuts):
    wk_hbm, wv_hbm, keys_ref, values_ref = refs[-8:-4]
    rows_ref, wk_ref, wv_ref, sems = refs[-4:]
    tables = refs[:-8]
    entries = keys_ref.shape[0] // NLEN
    piece = NLEN // cuts
    bring = [
        pltpu.make_async_copy(source, target, sems.at[entries * cuts + at])
        for at, (source, target) in enumerate(
            ((wk_hbm, wk_ref), (wv_hbm, wv_ref))
        )
    ]
    for copy in bring:
        copy.start()

    def entry_copy(entry, cut, table, first, shard):
        return pltpu.make_async_copy(
            table.at[first + cut, shard],
            rows_ref.at[pl.ds(entry * NLEN + cut * piece, piece)],
            sems.at[entry * cuts + cut],
        )

    for entry in range(entries):
        for slot, table in enumerate(tables):

            @pl.when(where_ref[2 + 3 * entry] == slot)
            def _(entry=entry, table=table):
                for cut in range(cuts):
                    entry_copy(
                        entry, cut, table, where_ref[3 + 3 * entry], where_ref[4 + 3 * entry]
                    ).start()

    for copy in bring:
        copy.wait()
    width = keys_ref.shape[1]
    step = math.gcd(width, 512)
    for group in range(entries // NEIGH):
        for entry in range(NEIGH * group, NEIGH * (group + 1)):
            for cut in range(cuts):
                entry_copy(entry, cut, tables[0], 0, 0).wait()
        here = slice(group * GROUP, (group + 1) * GROUP)
        for at in range(0, width, step):
            lanes = slice(at, at + step)
            for weight, made in ((wk_ref, keys_ref), (wv_ref, values_ref)):
                made[here, lanes] = jnp.dot(
                    rows_ref[here, :], weight[:, lanes], preferred_element_type=jnp.float32
                ).astype(jnp.bfloat16)


def project_encodings(where, tables, w_cross_k, w_cross_v):
    entries = (where.shape[0] - 2) // 3
    piece, depth = tables[0].shape[2:]
    cuts = NLEN // piece
    width = w_cross_k.shape[1]
    vmem = pl.BlockSpec(memory_space=pltpu.VMEM)
    anywhere = pl.BlockSpec(memory_space=pl.ANY)
    made = jax.ShapeDtypeStruct((entries * NLEN, width), jnp.bfloat16)
    return pl.pallas_call(
        functools.partial(project_kernel, cuts=cuts),
        out_shape=[made, made],
        in_specs=[pl.BlockSpec(memory_space=pltpu.SMEM)] + [anywhere] * (len(tables) + 2),
        out_specs=[vmem] * 2,
        scratch_shapes=[
            pltpu.VMEM((entries * NLEN, depth), jnp.bfloat16),
            pltpu.VMEM(w_cross_k.shape, jnp.bfloat16),
            pltpu.VMEM(w_cross_v.shape, jnp.bfloat16),
            pltpu.SemaphoreType.DMA((entries * cuts + 2,)),
        ],
        compiler_params=pltpu.CompilerParams(vmem_limit_bytes=VMEM_BYTES),
        cost_estimate=pl.CostEstimate(
            flops=entries * NLEN * depth,
            bytes_accessed=2 * entries * NLEN * depth,
            transcendentals=0,
        ),
        name="project_encodings",
    )(where, *tables, w_cross_k, w_cross_v)


def apart_heads(query):
    first = lax.broadcasted_iota(jnp.int32, query.shape, 1) < HD
    nothing = jnp.zeros_like(query)
    return jnp.concatenate(
        (jnp.where(first, query, nothing), jnp.where(first, nothing, query)), axis=0
    )


def together_heads(mixed):
    rows = mixed.shape[0] // 2
    first = lax.broadcasted_iota(jnp.int32, (rows, 2 * HD), 1) < HD
    return jnp.where(first, mixed[:rows], mixed[rows:])


def cross_kernel(
    info_ref,
    hidden_hbm,
    total_ref,
    gain_ref,
    wq_hbm,
    keys_hbm,
    values_hbm,
    wo_hbm,
    out_ref,
    residual_ref,
    wq_ref,
    keys_ref,
    values_ref,
    wo_ref,
    hidden_ref,
    rows_ref,
    query_ref,
    mixed_ref,
    sems,
    *,
    chunk,
    n_db,
    scale,
):
    rows, features = total_ref.shape
    half = rows // n_db
    width = wq_ref.shape[1]
    pairs = width // HD // 2
    tail = 16
    cut = features // 4
    low = width // 4
    hidden_copies = [
        pltpu.make_async_copy(
            hidden_hbm.at[pl.ds((2 * owner + chunk) * half, half)],
            hidden_ref.at[pl.ds(owner * half, half)],
            sems.at[10 + owner],
        )
        for owner in range(n_db)
    ]
    wq_copies = [
        pltpu.make_async_copy(
            wq_hbm.at[pl.ds(k * cut, cut)], wq_ref.at[pl.ds(k * cut, cut)], sems.at[k]
        )
        for k in range(4)
    ]
    other_copies = [
        pltpu.make_async_copy(keys_hbm, keys_ref, sems.at[4]),
        pltpu.make_async_copy(values_hbm, values_ref, sems.at[5]),
    ] + [
        pltpu.make_async_copy(
            wo_hbm.at[pl.ds(k * low, low)], wo_ref.at[pl.ds(k * low, low)], sems.at[6 + k]
        )
        for k in range(4)
    ]
    for copy in hidden_copies + wq_copies + other_copies:
        copy.start()
    for copy in hidden_copies:
        copy.wait()
    block = math.gcd(rows, 32)

    def norm(at, carried):
        here = pl.ds(pl.multiple_of(at * block, block), block)
        residual = hidden_ref[here, :].astype(jnp.float32) + total_ref[here, :].astype(jnp.float32)
        mean_square = jnp.mean(residual * residual, axis=-1, keepdims=True)
        rows_ref[here, :] = (
            residual * lax.rsqrt(mean_square + 1e-05) * gain_ref[...].astype(jnp.float32)
        ).astype(jnp.bfloat16)
        return carried

    lax.fori_loop(0, rows // block, norm, 0)
    own = pl.ds(pl.multiple_of(info_ref[0] * half, half), half)
    residual_ref[...] = hidden_ref[own, :].astype(jnp.float32) + total_ref[own, :].astype(
        jnp.float32
    )
    lanes = [slice(2 * pair * HD, 2 * (pair + 1) * HD) for pair in range(pairs)]
    for k, copy in enumerate(wq_copies):
        copy.wait()
        inner = slice(k * cut, (k + 1) * cut)
        for at in lanes:
            part = jnp.dot(
                rows_ref[:, inner], wq_ref[inner, at], preferred_element_type=jnp.float32
            )
            query_ref[:, at] = part if k == 0 else query_ref[:, at] + part
    for copy in other_copies[:2]:
        copy.wait()
    row = lax.broadcasted_iota(jnp.int32, (tail, 2 * HD), 0)
    queries = [query_ref[:, at].astype(jnp.bfloat16) for at in lanes]
    for owner in range(n_db):
        top = owner * half
        place = (2 * owner + chunk) * half
        group = place // SPAN
        ends = (place + half) % SPAN == 0
        here, after = (slice((group + k) * GROUP, (group + k + 1) * GROUP) for k in (0, 1))
        work = [(query[top : top + half], here, at) for query, at in zip(queries, lanes)]
        if ends:
            work += [
                (query[top + half - tail : top + half], after, at)
                for query, at in zip(queries, lanes)
            ]
        scores = [
            lax.dot_general(
                apart_heads(query),
                keys_ref[which, at],
                (((1,), (1,)), ((), ())),
                preferred_element_type=jnp.float32,
            )
            * (scale * LOG2E)
            for query, which, at in work
        ]
        tops = [jnp.max(one, axis=-1, keepdims=True) for one in scores]
        weights = [jnp.exp2(one - top_one) for one, top_one in zip(scores, tops)]
        totals = [jnp.sum(one, axis=-1, keepdims=True) for one in weights]
        mixed = [
            jnp.dot(
                one.astype(jnp.bfloat16), values_ref[which, at], preferred_element_type=jnp.float32
            )
            for one, (_, which, at) in zip(weights, work)
        ]
        mixed = [together_heads(one / total) for one, total in zip(mixed, totals)]
        for pair, at in enumerate(lanes):
            main = mixed[pair]
            if group == 0:
                main = jnp.where(info_ref[1] > 0, main, 0.0)
            if ends:
                last = jnp.where(row == tail - 1, mixed[pairs + pair], main[half - tail :])
                if half > tail:
                    mixed_ref[top : top + half - tail, at] = main[: half - tail].astype(
                        jnp.bfloat16
                    )
                mixed_ref[top + half - tail : top + half, at] = last.astype(jnp.bfloat16)
            else:
                mixed_ref[top : top + half, at] = main.astype(jnp.bfloat16)

    for copy in other_copies[2:]:
        copy.wait()
    step = math.gcd(features, 512)

    def columns(at, carried):
        here = pl.ds(pl.multiple_of(at * step, step), step)
        product = jnp.dot(mixed_ref[...], wo_ref[:, here], preferred_element_type=jnp.float32)
        out_ref[:, here] = product.astype(jnp.bfloat16)
        return carried

    lax.fori_loop(0, features // step, columns, 0, unroll=4)


def cross_block(
    chunk, info, hidden, total, gain, w_cross_q, keys, values, w_cross_out, n_db, scale
):
    rows, features = total.shape
    width = w_cross_q.shape[1]
    vmem = pl.BlockSpec(memory_space=pltpu.VMEM)
    anywhere = pl.BlockSpec(memory_space=pl.ANY)
    return pl.pallas_call(
        functools.partial(cross_kernel, chunk=chunk, n_db=n_db, scale=scale),
        out_shape=[
            jax.ShapeDtypeStruct((rows, features), jnp.bfloat16),
            jax.ShapeDtypeStruct((rows // n_db, features), jnp.float32),
        ],
        in_specs=[pl.BlockSpec(memory_space=pltpu.SMEM), anywhere, vmem, vmem] + [anywhere] * 4,
        out_specs=[vmem] * 2,
        scratch_shapes=[
            pltpu.VMEM((features, width), jnp.bfloat16),
            pltpu.VMEM(keys.shape, jnp.bfloat16),
            pltpu.VMEM(values.shape, jnp.bfloat16),
            pltpu.VMEM((width, features), jnp.bfloat16),
            pltpu.VMEM((rows, features), jnp.bfloat16),
            pltpu.VMEM((rows, features), jnp.bfloat16),
            pltpu.VMEM((rows, width), jnp.float32),
            pltpu.VMEM((rows, width), jnp.bfloat16),
            pltpu.SemaphoreType.DMA((10 + n_db,)),
        ],
        compiler_params=pltpu.CompilerParams(vmem_limit_bytes=VMEM_BYTES),
        cost_estimate=pl.CostEstimate(
            flops=4 * rows * width * (features + GROUP),
            bytes_accessed=4 * width * (features + keys.shape[0]) + 8 * rows * features,
            transcendentals=rows * GROUP * width // HD,
        ),
        name="cross_block",
    )(info, hidden, total, gain, w_cross_q, keys, values, w_cross_out)


def per_device(
    hidden_in,
    query_rows,
    key_rows,
    value_rows,
    w_self_out,
    norm_gain,
    w_cross_q,
    w_cross_k,
    w_cross_v,
    w_cross_out,
    enc_table,
    nb_shard,
    nb_row,
):
    features = hidden_in.shape[1]
    heads = query_rows.shape[1] // HD
    n_seq, n_db = lax.axis_size("seq"), lax.axis_size("db")
    seq_index, db_index = lax.axis_index("seq"), lax.axis_index("db")
    scale = 1.0 / math.sqrt(HD)

    rows_shard, _, depth = enc_table.shape
    encodings = enc_table.reshape(rows_shard * NLEN, depth)
    piece = rows_shard * NLEN // n_seq
    packed, part = pack_heads(
        seq_index.reshape(1).astype(jnp.int32), query_rows, key_rows, value_rows, encodings, piece
    )
    along_db = lax.all_gather(part, "db", axis=0)

    packed, nb_row, nb_shard = lax.optimization_barrier((packed, nb_row, nb_shard))
    wanted = jnp.stack((nb_row, nb_shard), axis=-1).astype(jnp.int32)
    place = jnp.stack((db_index, (seq_index > 0).astype(jnp.int32))).astype(jnp.int32)
    nearest = jnp.concatenate((span_before(wanted)[None], wanted), axis=0)
    row, shard = nearest[..., 0], nearest[..., 1]
    in_plane = n_seq == 8 and piece == NLEN
    if in_plane:
        where = jnp.stack((plane_slot(row, seq_index), jnp.zeros_like(row), shard), axis=-1)
    else:
        where = jnp.stack((jnp.zeros_like(row), row * (NLEN // piece), shard), axis=-1)
    info = jnp.concatenate((place, where.reshape(-1))).astype(jnp.int32)
    if heads == n_seq:
        held = lax.all_to_all(packed, "seq", 0, 0, tiled=True)
        held, info = lax.optimization_barrier((held, info))
        attended = lax.all_to_all(self_attend_head(held, scale), "seq", 0, 0, tiled=True)
    else:
        attended = self_attention_gathered(query_rows, key_rows, value_rows, scale)

    along_db, attended = lax.optimization_barrier((along_db, attended))
    partial = self_out(attended, w_self_out, n_db)
    along_db, partial = lax.optimization_barrier((along_db, partial))
    total = lax.psum(partial[0], "db")
    if in_plane:
        tables, total = plane_pieces(along_db, total)
        tables = tuple(one[None] for one in tables)
    else:
        tables = (lax.all_gather(along_db, "seq", axis=0),)
    total, second = lax.optimization_barrier((total, partial[1]))
    totals = [total, lax.psum(second, "db")]
    projected = project_encodings(info, tables, w_cross_k, w_cross_v)
    totals[0], (keys, values) = lax.optimization_barrier((totals[0], projected))

    gain = norm_gain.reshape(1, features)
    blocks = []
    for chunk, total in enumerate(totals):
        out_partial, residual = cross_block(
            chunk, info, hidden_in, total, gain, w_cross_q, keys, values, w_cross_out, n_db, scale
        )
        summed = lax.psum_scatter(out_partial, "db", scatter_dimension=0, tiled=True)
        blocks.append(residual + summed.astype(jnp.float32))
    return jnp.concatenate(blocks, axis=0)


def solution(mesh):
    placed = (
        P("seq", None),
        P("seq", "db"),
        P("seq", "db"),
        P("seq", "db"),
        P("db", None),
        P(),
        P(None, "db"),
        P(None, "db"),
        P(None, "db"),
        P("db", None),
        P("db", None, None),
        P("seq", None),
        P("seq", None),
    )
    return jax.shard_map(
        per_device, mesh=mesh, in_specs=placed, out_specs=P(("seq", "db"), None), check_vma=False
    )
```

```python
import functools
import math

import jax
import jax.numpy as jnp
from jax import lax
from jax.experimental import pallas as pl
from jax.experimental.pallas import tpu as pltpu
from jax.sharding import PartitionSpec as P

HD = 128
SPAN = 64
NEIGH = 2
NLEN = 128
GROUP = NEIGH * NLEN

NEG_BIG = -1e30
LOG2E = 1.4426950408889634
VMEM_BYTES = 48 * 1024 * 1024
LARGE_BYTES = 58 * 1024 * 1024


def shift(block, axis, distance, senders):
    size = lax.axis_size(axis)
    route = [(k, k + distance) for k in senders if 0 <= k + distance < size]
    return lax.ppermute(block, axis, route)


def plane_swap(block, mask):
    return lax.ppermute(block, "seq", [(i, i ^ mask) for i in range(8)])


def plane_pieces(own):
    same = lax.optimization_barrier((own,) + tuple(plane_swap(own, mask) for mask in (2, 4, 6)))
    return same + tuple(plane_swap(one, 1) for one in same)


def plane_slot(owner, me):
    apart = owner ^ me
    return (apart >> 1) + 4 * (apart & 1)


def self_kernel(qkv_ref, out_ref, *, blocks, rows, scale):
    for block in range(blocks):
        query = qkv_ref[block, 0]
        live = (block + 1) * rows
        keys = qkv_ref[0 : block + 1, 1].reshape(live, HD)
        values = qkv_ref[0 : block + 1, 2].reshape(live, HD)
        scores = lax.dot_general(
            query, keys, (((1,), (1,)), ((), ())), preferred_element_type=jnp.float32
        )
        query_pos = block * rows + lax.broadcasted_iota(jnp.int32, (rows, live), 0)
        key_pos = lax.broadcasted_iota(jnp.int32, (rows, live), 1)
        scores = jnp.where(key_pos <= query_pos, scores * (scale * LOG2E), NEG_BIG)
        top = jnp.max(scores, axis=-1, keepdims=True)
        weights = jnp.exp2(scores - top)
        total = jnp.sum(weights, axis=-1, keepdims=True)
        mixed = jnp.dot(weights.astype(jnp.bfloat16), values, preferred_element_type=jnp.float32)
        out_ref[block] = (mixed / total).astype(jnp.bfloat16)


def self_attend_head(qkv, scale):
    blocks, _, rows, _ = qkv.shape
    return pl.pallas_call(
        functools.partial(self_kernel, blocks=blocks, rows=rows, scale=scale),
        out_shape=jax.ShapeDtypeStruct((blocks, rows, HD), jnp.bfloat16),
        in_specs=[pl.BlockSpec(memory_space=pltpu.VMEM)],
        out_specs=pl.BlockSpec(memory_space=pltpu.VMEM),
        compiler_params=pltpu.CompilerParams(vmem_limit_bytes=VMEM_BYTES),
        cost_estimate=pl.CostEstimate(
            flops=2 * blocks * blocks * rows * rows * HD,
            bytes_accessed=8 * blocks * rows * HD,
            transcendentals=blocks * blocks * rows * rows // 2,
        ),
        name="self_attend",
    )(qkv)


def span_before(wanted):
    return shift(wanted[-1], "seq", 1, range(lax.axis_size("seq")))


def pack_kernel(index_ref, query_ref, key_ref, value_ref, part_ref, out_ref, part_out_ref):
    for which, ref in enumerate((query_ref, key_ref, value_ref)):
        for head in range(out_ref.shape[0]):
            out_ref[head, which] = ref[:, head * HD : (head + 1) * HD]
    part_out_ref[...] = part_ref[...]


def pack_heads(index, query_rows, key_rows, value_rows, encodings, piece):
    rows, width = query_rows.shape
    heads = width // HD
    depth = encodings.shape[1]
    steps = 4
    block, part = rows // steps, piece // steps
    row_block = pl.BlockSpec((block, width), lambda at, index_ref: (at, 0))
    return pl.pallas_call(
        pack_kernel,
        out_shape=[
            jax.ShapeDtypeStruct((heads, 3, rows, HD), jnp.bfloat16),
            jax.ShapeDtypeStruct((piece, depth), jnp.bfloat16),
        ],
        grid_spec=pltpu.PrefetchScalarGridSpec(
            num_scalar_prefetch=1,
            grid=(steps,),
            in_specs=[row_block] * 3
            + [pl.BlockSpec((part, depth), lambda at, index_ref: (index_ref[0] * steps + at, 0))],
            out_specs=[
                pl.BlockSpec((heads, 3, block, HD), lambda at, index_ref: (0, 0, at, 0)),
                pl.BlockSpec((part, depth), lambda at, index_ref: (at, 0)),
            ],
        ),
        compiler_params=pltpu.CompilerParams(
            vmem_limit_bytes=LARGE_BYTES, dimension_semantics=("arbitrary",)
        ),
        cost_estimate=pl.CostEstimate(
            flops=0, bytes_accessed=12 * rows * width, transcendentals=0
        ),
        name="pack_heads",
    )(index, query_rows, key_rows, value_rows, encodings)


def self_attention_gathered(query_rows, key_rows, value_rows, scale):
    rows, width = query_rows.shape
    heads = width // HD
    keys = lax.all_gather(key_rows, "seq", axis=0, tiled=True)
    values = lax.all_gather(value_rows, "seq", axis=0, tiled=True)
    count = keys.shape[0]
    query_pos = lax.axis_index("seq") * rows + jnp.arange(rows, dtype=jnp.int32)
    allowed = jnp.arange(count, dtype=jnp.int32)[None, :] <= query_pos[:, None]
    scores = (
        jnp.einsum(
            "qhd,khd->hqk",
            query_rows.reshape(rows, heads, HD),
            keys.reshape(count, heads, HD),
            preferred_element_type=jnp.float32,
        )
        * scale
    )
    scores = jnp.where(allowed[None], scores, NEG_BIG)
    weights = jnp.exp(scores - jnp.max(scores, axis=-1, keepdims=True))
    total = jnp.sum(weights, axis=-1)
    mixed = jnp.einsum(
        "hqk,khd->hqd",
        weights.astype(jnp.bfloat16),
        values.reshape(count, heads, HD),
        preferred_element_type=jnp.float32,
    )
    return (mixed / total[..., None]).astype(jnp.bfloat16)


def self_out_kernel(
    attended_ref, weight_hbm, out_ref, rows_ref, weight_ref, sum_ref, sems
):
    heads, rows, _ = attended_ref.shape
    features = out_ref.shape[1]
    width = weight_hbm.shape[0]
    cuts = 4
    depth = width // cuts
    copies = [
        pltpu.make_async_copy(
            weight_hbm.at[pl.ds(k * depth, depth)], weight_ref.at[pl.ds(k * depth, depth)], sems.at[k]
        )
        for k in range(cuts)
    ]
    for copy in copies:
        copy.start()
    for head in range(heads):
        rows_ref[:, head * HD : (head + 1) * HD] = attended_ref[head]
    step = math.gcd(features, 512)

    def columns(at, carried, begin, end):
        here = pl.ds(pl.multiple_of(at * step, step), step)
        inner = slice(begin * depth, end * depth)
        product = jnp.dot(
            rows_ref[:, inner], weight_ref[inner, here], preferred_element_type=jnp.float32
        )
        if begin == 0:
            sum_ref[:, here] = product
            return carried
        out_ref[:, here] = (product + sum_ref[:, here]).astype(jnp.bfloat16)
        return carried

    for begin, end in ((0, cuts // 2), (cuts // 2, cuts)):
        for copy in copies[begin:end]:
            copy.wait()
        lax.fori_loop(
            0, features // step, functools.partial(columns, begin=begin, end=end), 0, unroll=4
        )


def self_out(attended, weight):
    heads, rows, _ = attended.shape
    width, features = weight.shape
    vmem = pl.BlockSpec(memory_space=pltpu.VMEM)
    return pl.pallas_call(
        self_out_kernel,
        out_shape=jax.ShapeDtypeStruct((rows, features), jnp.bfloat16),
        in_specs=[vmem, pl.BlockSpec(memory_space=pl.ANY)],
        out_specs=vmem,
        scratch_shapes=[
            pltpu.VMEM((rows, width), jnp.bfloat16),
            pltpu.VMEM((width, features), jnp.bfloat16),
            pltpu.VMEM((rows, features), jnp.float32),
            pltpu.SemaphoreType.DMA((4,)),
        ],
        compiler_params=pltpu.CompilerParams(vmem_limit_bytes=VMEM_BYTES),
        cost_estimate=pl.CostEstimate(
            flops=2 * rows * width * features,
            bytes_accessed=2 * (rows * width + width * features + rows * features),
            transcendentals=0,
        ),
        name="self_out",
    )(attended, weight)


def project_kernel(where_ref, *refs, cuts):
    wk_hbm, wv_hbm, keys_ref, values_ref = refs[-8:-4]
    rows_ref, wk_ref, wv_ref, sems = refs[-4:]
    tables = refs[:-8]
    entries = keys_ref.shape[0] // NLEN
    piece = NLEN // cuts
    bring = [
        pltpu.make_async_copy(source, target, sems.at[entries * cuts + at])
        for at, (source, target) in enumerate(
            ((wk_hbm, wk_ref), (wv_hbm, wv_ref))
        )
    ]
    for copy in bring:
        copy.start()

    def entry_copy(entry, cut, table, first, shard):
        return pltpu.make_async_copy(
            table.at[first + cut, shard],
            rows_ref.at[pl.ds(entry * NLEN + cut * piece, piece)],
            sems.at[entry * cuts + cut],
        )

    for entry in range(entries):
        for slot, table in enumerate(tables):

            @pl.when(where_ref[2 + 3 * entry] == slot)
            def _(entry=entry, table=table):
                for cut in range(cuts):
                    entry_copy(
                        entry, cut, table, where_ref[3 + 3 * entry], where_ref[4 + 3 * entry]
                    ).start()

    for copy in bring:
        copy.wait()
    width = keys_ref.shape[1]
    step = math.gcd(width, 512)
    for group in range(entries // NEIGH):
        for entry in range(NEIGH * group, NEIGH * (group + 1)):
            for cut in range(cuts):
                entry_copy(entry, cut, tables[0], 0, 0).wait()
        here = slice(group * GROUP, (group + 1) * GROUP)
        for at in range(0, width, step):
            lanes = slice(at, at + step)
            for weight, made in ((wk_ref, keys_ref), (wv_ref, values_ref)):
                made[here, lanes] = jnp.dot(
                    rows_ref[here, :], weight[:, lanes], preferred_element_type=jnp.float32
                ).astype(jnp.bfloat16)


def project_encodings(where, tables, w_cross_k, w_cross_v):
    entries = (where.shape[0] - 2) // 3
    piece, depth = tables[0].shape[2:]
    cuts = NLEN // piece
    width = w_cross_k.shape[1]
    vmem = pl.BlockSpec(memory_space=pltpu.VMEM)
    anywhere = pl.BlockSpec(memory_space=pl.ANY)
    made = jax.ShapeDtypeStruct((entries * NLEN, width), jnp.bfloat16)
    return pl.pallas_call(
        functools.partial(project_kernel, cuts=cuts),
        out_shape=[made, made],
        in_specs=[pl.BlockSpec(memory_space=pltpu.SMEM)] + [anywhere] * (len(tables) + 2),
        out_specs=[vmem] * 2,
        scratch_shapes=[
            pltpu.VMEM((entries * NLEN, depth), jnp.bfloat16),
            pltpu.VMEM(w_cross_k.shape, jnp.bfloat16),
            pltpu.VMEM(w_cross_v.shape, jnp.bfloat16),
            pltpu.SemaphoreType.DMA((entries * cuts + 2,)),
        ],
        compiler_params=pltpu.CompilerParams(vmem_limit_bytes=VMEM_BYTES),
        cost_estimate=pl.CostEstimate(
            flops=entries * NLEN * depth,
            bytes_accessed=2 * entries * NLEN * depth,
            transcendentals=0,
        ),
        name="project_encodings",
    )(where, *tables, w_cross_k, w_cross_v)


def apart_heads(query):
    first = lax.broadcasted_iota(jnp.int32, query.shape, 1) < HD
    nothing = jnp.zeros_like(query)
    return jnp.concatenate(
        (jnp.where(first, query, nothing), jnp.where(first, nothing, query)), axis=0
    )


def together_heads(mixed):
    rows = mixed.shape[0] // 2
    first = lax.broadcasted_iota(jnp.int32, (rows, 2 * HD), 1) < HD
    return jnp.where(first, mixed[:rows], mixed[rows:])


def cross_kernel(
    info_ref,
    hidden_ref,
    total_ref,
    gain_ref,
    wq_hbm,
    keys_hbm,
    values_hbm,
    wo_hbm,
    out_ref,
    residual_ref,
    wq_ref,
    keys_ref,
    values_ref,
    wo_ref,
    rows_ref,
    query_ref,
    mixed_ref,
    sems,
    *,
    scale,
):
    rows, features = hidden_ref.shape
    n_db, share, _ = out_ref.shape
    width = wq_ref.shape[1]
    pairs = width // HD // 2
    tail = 16
    parts = 8
    cut, low = features // parts, width // parts
    wq_copies = [
        pltpu.make_async_copy(
            wq_hbm.at[pl.ds(k * cut, cut)], wq_ref.at[pl.ds(k * cut, cut)], sems.at[k]
        )
        for k in range(parts)
    ]
    other_copies = [
        pltpu.make_async_copy(keys_hbm, keys_ref, sems.at[2 * parts]),
        pltpu.make_async_copy(values_hbm, values_ref, sems.at[2 * parts + 1]),
    ] + [
        pltpu.make_async_copy(
            wo_hbm.at[pl.ds(k * low, low)], wo_ref.at[pl.ds(k * low, low)], sems.at[parts + k]
        )
        for k in range(parts)
    ]
    for copy in wq_copies + other_copies:
        copy.start()
    block = math.gcd(rows, 32)

    def norm(at, carried):
        here = pl.ds(pl.multiple_of(at * block, block), block)
        residual = hidden_ref[here, :].astype(jnp.float32) + total_ref[here, :].astype(jnp.float32)
        mean_square = jnp.mean(residual * residual, axis=-1, keepdims=True)
        rows_ref[here, :] = (
            residual * lax.rsqrt(mean_square + 1e-05) * gain_ref[...].astype(jnp.float32)
        ).astype(jnp.bfloat16)
        return carried

    lax.fori_loop(0, rows // block, norm, 0)
    own = pl.ds(pl.multiple_of(info_ref[0] * share, share), share)
    residual_ref[...] = hidden_ref[own, :].astype(jnp.float32) + total_ref[own, :].astype(
        jnp.float32
    )
    lanes = [slice(2 * pair * HD, 2 * (pair + 1) * HD) for pair in range(pairs)]
    for k in range(0, parts, 2):
        for copy in wq_copies[k : k + 2]:
            copy.wait()
        inner = slice(k * cut, (k + 2) * cut)
        for at in lanes:
            part = jnp.dot(
                rows_ref[:, inner], wq_ref[inner, at], preferred_element_type=jnp.float32
            )
            query_ref[:, at] = part if k == 0 else query_ref[:, at] + part
    for copy in other_copies[:2]:
        copy.wait()
    row = lax.broadcasted_iota(jnp.int32, (tail, 2 * HD), 0)
    spans = rows // SPAN
    for span in range(spans):
        top = span * SPAN
        here, after = (slice((span + k) * GROUP, (span + k + 1) * GROUP) for k in (0, 1))
        work = [(slice(top, top + SPAN), here, at) for at in lanes]
        work += [(slice(top + SPAN - tail, top + SPAN), after, at) for at in lanes]
        scores = [
            lax.dot_general(
                apart_heads(query_ref[of, at].astype(jnp.bfloat16)),
                keys_ref[which, at],
                (((1,), (1,)), ((), ())),
                preferred_element_type=jnp.float32,
            )
            * (scale * LOG2E)
            for of, which, at in work
        ]
        tops = [jnp.max(one, axis=-1, keepdims=True) for one in scores]
        weights = [jnp.exp2(one - top_one) for one, top_one in zip(scores, tops)]
        totals = [jnp.sum(one, axis=-1, keepdims=True) for one in weights]
        mixed = [
            jnp.dot(
                one.astype(jnp.bfloat16), values_ref[which, at], preferred_element_type=jnp.float32
            )
            for one, (_, which, at) in zip(weights, work)
        ]
        mixed = [together_heads(one / total) for one, total in zip(mixed, totals)]
        for pair, at in enumerate(lanes):
            main, last = mixed[pair], mixed[pairs + pair]
            if span == 0:
                main = jnp.where(info_ref[1] > 0, main, 0.0)
            last = jnp.where(row == tail - 1, last, main[SPAN - tail :])
            mixed_ref[top : top + SPAN - tail, at] = main[: SPAN - tail].astype(jnp.bfloat16)
            mixed_ref[top + SPAN - tail : top + SPAN, at] = last.astype(jnp.bfloat16)
    for copy in other_copies[2:]:
        copy.wait()
    step = math.gcd(features, 512)

    def columns(at, carried):
        here = pl.ds(pl.multiple_of(at * step, step), step)
        product = jnp.dot(mixed_ref[...], wo_ref[:, here], preferred_element_type=jnp.float32)
        product = product.astype(jnp.bfloat16)
        for owner in range(n_db):
            out_ref[owner, :, here] = product[owner * share : (owner + 1) * share]
        return carried

    lax.fori_loop(0, features // step, columns, 0, unroll=4)


def cross_block(info, hidden, total, gain, w_cross_q, keys, values, w_cross_out, n_db, scale):
    rows, features = hidden.shape
    share = rows // n_db
    width = w_cross_q.shape[1]
    vmem = pl.BlockSpec(memory_space=pltpu.VMEM)
    anywhere = pl.BlockSpec(memory_space=pl.ANY)
    return pl.pallas_call(
        functools.partial(cross_kernel, scale=scale),
        out_shape=[
            jax.ShapeDtypeStruct((n_db, share, features), jnp.bfloat16),
            jax.ShapeDtypeStruct((share, features), jnp.float32),
        ],
        in_specs=[pl.BlockSpec(memory_space=pltpu.SMEM)] + [vmem] * 3 + [anywhere] * 4,
        out_specs=[vmem] * 2,
        scratch_shapes=[
            pltpu.VMEM((features, width), jnp.bfloat16),
            pltpu.VMEM(keys.shape, jnp.bfloat16),
            pltpu.VMEM(values.shape, jnp.bfloat16),
            pltpu.VMEM((width, features), jnp.bfloat16),
            pltpu.VMEM((rows, features), jnp.bfloat16),
            pltpu.VMEM((rows, width), jnp.float32),
            pltpu.VMEM((rows, width), jnp.bfloat16),
            pltpu.SemaphoreType.DMA((18,)),
        ],
        compiler_params=pltpu.CompilerParams(vmem_limit_bytes=VMEM_BYTES),
        cost_estimate=pl.CostEstimate(
            flops=4 * rows * width * (features + GROUP),
            bytes_accessed=4 * width * (features + keys.shape[0]) + 8 * rows * features,
            transcendentals=rows * GROUP * width // HD,
        ),
        name="cross_block",
    )(info, hidden, total, gain, w_cross_q, keys, values, w_cross_out)


def per_device(
    hidden_in,
    query_rows,
    key_rows,
    value_rows,
    w_self_out,
    norm_gain,
    w_cross_q,
    w_cross_k,
    w_cross_v,
    w_cross_out,
    enc_table,
    nb_shard,
    nb_row,
):
    features = hidden_in.shape[1]
    heads = query_rows.shape[1] // HD
    n_seq, n_db = lax.axis_size("seq"), lax.axis_size("db")
    seq_index, db_index = lax.axis_index("seq"), lax.axis_index("db")
    scale = 1.0 / math.sqrt(HD)

    rows_shard, _, depth = enc_table.shape
    encodings = enc_table.reshape(rows_shard * NLEN, depth)
    piece = rows_shard * NLEN // n_seq
    packed, part = pack_heads(
        seq_index.reshape(1).astype(jnp.int32), query_rows, key_rows, value_rows, encodings, piece
    )
    along_db = lax.all_gather(part, "db", axis=0)

    packed, nb_row, nb_shard = lax.optimization_barrier((packed, nb_row, nb_shard))
    wanted = jnp.stack((nb_row, nb_shard), axis=-1).astype(jnp.int32)
    place = jnp.stack((db_index, (seq_index > 0).astype(jnp.int32))).astype(jnp.int32)
    nearest = jnp.concatenate((span_before(wanted)[None], wanted), axis=0)
    row, shard = nearest[..., 0], nearest[..., 1]
    in_plane = n_seq == 8 and piece == NLEN
    if in_plane:
        where = jnp.stack((plane_slot(row, seq_index), jnp.zeros_like(row), shard), axis=-1)
    else:
        where = jnp.stack((jnp.zeros_like(row), row * (NLEN // piece), shard), axis=-1)
    info = jnp.concatenate((place, where.reshape(-1))).astype(jnp.int32)
    if heads == n_seq:
        held = lax.all_to_all(packed, "seq", 0, 0, tiled=True)
        held, info = lax.optimization_barrier((held, info))
        attended = lax.all_to_all(self_attend_head(held, scale), "seq", 0, 0, tiled=True)
    else:
        attended = self_attention_gathered(query_rows, key_rows, value_rows, scale)

    along_db, attended = lax.optimization_barrier((along_db, attended))
    partial = self_out(attended, w_self_out)
    along_db, partial = lax.optimization_barrier((along_db, partial))
    total = lax.psum(partial, "db")
    if in_plane:
        tables = tuple(one[None] for one in plane_pieces(along_db))
    else:
        tables = (lax.all_gather(along_db, "seq", axis=0),)
    projected = project_encodings(info, tables, w_cross_k, w_cross_v)
    total, (keys, values) = lax.optimization_barrier((total, projected))

    partial, residual = cross_block(
        info,
        hidden_in,
        total,
        norm_gain.reshape(1, features),
        w_cross_q,
        keys,
        values,
        w_cross_out,
        n_db,
        scale,
    )
    rows = hidden_in.shape[0]
    summed = lax.psum_scatter(
        partial.reshape(rows, features), "db", scatter_dimension=0, tiled=True
    )
    return residual + summed.astype(jnp.float32)


def solution(mesh):
    placed = (
        P("seq", None),
        P("seq", "db"),
        P("seq", "db"),
        P("seq", "db"),
        P("db", None),
        P(),
        P(None, "db"),
        P(None, "db"),
        P(None, "db"),
        P("db", None),
        P("db", None, None),
        P("seq", None),
        P("seq", None),
    )
    return jax.shard_map(
        per_device, mesh=mesh, in_specs=placed, out_specs=P(("seq", "db"), None), check_vma=False
    )
```

```python
import functools
import math

import jax
import jax.numpy as jnp
from jax import lax
from jax.experimental import pallas as pl
from jax.experimental.pallas import tpu as pltpu
from jax.sharding import PartitionSpec as P

HD = 128
SPAN = 64
NEIGH = 2
NLEN = 128
GROUP = NEIGH * NLEN

NEG_BIG = -1e30
LOG2E = 1.4426950408889634
VMEM_BYTES = 48 * 1024 * 1024
LARGE_BYTES = 58 * 1024 * 1024


def shift(block, axis, distance, senders):
    size = lax.axis_size(axis)
    route = [(k, k + distance) for k in senders if 0 <= k + distance < size]
    return lax.ppermute(block, axis, route)


def plane_swap(block, mask):
    return lax.ppermute(block, "seq", [(i, i ^ mask) for i in range(8)])


def plane_pieces(own):
    same = lax.optimization_barrier((own,) + tuple(plane_swap(own, mask) for mask in (2, 4, 6)))
    return same + tuple(plane_swap(one, 1) for one in same)


def plane_slot(owner, me):
    apart = owner ^ me
    return (apart >> 1) + 4 * (apart & 1)


def self_kernel(qkv_ref, out_ref, *, blocks, rows, scale):
    for block in range(blocks):
        query = qkv_ref[block, 0]
        live = (block + 1) * rows
        keys = qkv_ref[0 : block + 1, 1].reshape(live, HD)
        values = qkv_ref[0 : block + 1, 2].reshape(live, HD)
        scores = lax.dot_general(
            query, keys, (((1,), (1,)), ((), ())), preferred_element_type=jnp.float32
        )
        query_pos = block * rows + lax.broadcasted_iota(jnp.int32, (rows, live), 0)
        key_pos = lax.broadcasted_iota(jnp.int32, (rows, live), 1)
        scores = jnp.where(key_pos <= query_pos, scores * (scale * LOG2E), NEG_BIG)
        top = jnp.max(scores, axis=-1, keepdims=True)
        weights = jnp.exp2(scores - top)
        total = jnp.sum(weights, axis=-1, keepdims=True)
        mixed = jnp.dot(weights.astype(jnp.bfloat16), values, preferred_element_type=jnp.float32)
        out_ref[block] = (mixed / total).astype(jnp.bfloat16)


def self_attend_head(qkv, scale):
    blocks, _, rows, _ = qkv.shape
    return pl.pallas_call(
        functools.partial(self_kernel, blocks=blocks, rows=rows, scale=scale),
        out_shape=jax.ShapeDtypeStruct((blocks, rows, HD), jnp.bfloat16),
        in_specs=[pl.BlockSpec(memory_space=pltpu.VMEM)],
        out_specs=pl.BlockSpec(memory_space=pltpu.VMEM),
        compiler_params=pltpu.CompilerParams(vmem_limit_bytes=VMEM_BYTES),
        cost_estimate=pl.CostEstimate(
            flops=2 * blocks * blocks * rows * rows * HD,
            bytes_accessed=8 * blocks * rows * HD,
            transcendentals=blocks * blocks * rows * rows // 2,
        ),
        name="self_attend",
    )(qkv)


def span_before(wanted):
    return shift(wanted[-1], "seq", 1, range(lax.axis_size("seq")))


def pack_kernel(index_ref, query_ref, key_ref, value_ref, part_ref, out_ref, part_out_ref):
    for which, ref in enumerate((query_ref, key_ref, value_ref)):
        for head in range(out_ref.shape[0]):
            out_ref[head, which] = ref[:, head * HD : (head + 1) * HD]
    part_out_ref[...] = part_ref[...]


def pack_heads(index, query_rows, key_rows, value_rows, encodings, piece):
    rows, width = query_rows.shape
    heads = width // HD
    depth = encodings.shape[1]
    steps = 4
    block, part = rows // steps, piece // steps
    row_block = pl.BlockSpec((block, width), lambda at, index_ref: (at, 0))
    return pl.pallas_call(
        pack_kernel,
        out_shape=[
            jax.ShapeDtypeStruct((heads, 3, rows, HD), jnp.bfloat16),
            jax.ShapeDtypeStruct((piece, depth), jnp.bfloat16),
        ],
        grid_spec=pltpu.PrefetchScalarGridSpec(
            num_scalar_prefetch=1,
            grid=(steps,),
            in_specs=[row_block] * 3
            + [pl.BlockSpec((part, depth), lambda at, index_ref: (index_ref[0] * steps + at, 0))],
            out_specs=[
                pl.BlockSpec((heads, 3, block, HD), lambda at, index_ref: (0, 0, at, 0)),
                pl.BlockSpec((part, depth), lambda at, index_ref: (at, 0)),
            ],
        ),
        compiler_params=pltpu.CompilerParams(
            vmem_limit_bytes=LARGE_BYTES, dimension_semantics=("arbitrary",)
        ),
        cost_estimate=pl.CostEstimate(
            flops=0, bytes_accessed=12 * rows * width, transcendentals=0
        ),
        name="pack_heads",
    )(index, query_rows, key_rows, value_rows, encodings)


def self_attention_gathered(query_rows, key_rows, value_rows, scale):
    rows, width = query_rows.shape
    heads = width // HD
    keys = lax.all_gather(key_rows, "seq", axis=0, tiled=True)
    values = lax.all_gather(value_rows, "seq", axis=0, tiled=True)
    count = keys.shape[0]
    query_pos = lax.axis_index("seq") * rows + jnp.arange(rows, dtype=jnp.int32)
    allowed = jnp.arange(count, dtype=jnp.int32)[None, :] <= query_pos[:, None]
    scores = (
        jnp.einsum(
            "qhd,khd->hqk",
            query_rows.reshape(rows, heads, HD),
            keys.reshape(count, heads, HD),
            preferred_element_type=jnp.float32,
        )
        * scale
    )
    scores = jnp.where(allowed[None], scores, NEG_BIG)
    weights = jnp.exp(scores - jnp.max(scores, axis=-1, keepdims=True))
    total = jnp.sum(weights, axis=-1)
    mixed = jnp.einsum(
        "hqk,khd->hqd",
        weights.astype(jnp.bfloat16),
        values.reshape(count, heads, HD),
        preferred_element_type=jnp.float32,
    )
    return (mixed / total[..., None]).astype(jnp.bfloat16)


def self_out_kernel(
    attended_ref, weight_hbm, out_ref, rows_ref, weight_ref, sum_ref, sems
):
    heads, rows, _ = attended_ref.shape
    features = out_ref.shape[1]
    width = weight_hbm.shape[0]
    cuts = 4
    depth = width // cuts
    copies = [
        pltpu.make_async_copy(
            weight_hbm.at[pl.ds(k * depth, depth)], weight_ref.at[pl.ds(k * depth, depth)], sems.at[k]
        )
        for k in range(cuts)
    ]
    for copy in copies:
        copy.start()
    for head in range(heads):
        rows_ref[:, head * HD : (head + 1) * HD] = attended_ref[head]
    step = math.gcd(features, 512)

    def columns(at, carried, begin, end):
        here = pl.ds(pl.multiple_of(at * step, step), step)
        inner = slice(begin * depth, end * depth)
        product = jnp.dot(
            rows_ref[:, inner], weight_ref[inner, here], preferred_element_type=jnp.float32
        )
        if begin == 0:
            sum_ref[:, here] = product
            return carried
        out_ref[:, here] = (product + sum_ref[:, here]).astype(jnp.bfloat16)
        return carried

    for begin, end in ((0, cuts // 2), (cuts // 2, cuts)):
        for copy in copies[begin:end]:
            copy.wait()
        lax.fori_loop(
            0, features // step, functools.partial(columns, begin=begin, end=end), 0, unroll=4
        )


def self_out(attended, weight):
    heads, rows, _ = attended.shape
    width, features = weight.shape
    vmem = pl.BlockSpec(memory_space=pltpu.VMEM)
    return pl.pallas_call(
        self_out_kernel,
        out_shape=jax.ShapeDtypeStruct((rows, features), jnp.bfloat16),
        in_specs=[vmem, pl.BlockSpec(memory_space=pl.ANY)],
        out_specs=vmem,
        scratch_shapes=[
            pltpu.VMEM((rows, width), jnp.bfloat16),
            pltpu.VMEM((width, features), jnp.bfloat16),
            pltpu.VMEM((rows, features), jnp.float32),
            pltpu.SemaphoreType.DMA((4,)),
        ],
        compiler_params=pltpu.CompilerParams(vmem_limit_bytes=VMEM_BYTES),
        cost_estimate=pl.CostEstimate(
            flops=2 * rows * width * features,
            bytes_accessed=2 * (rows * width + width * features + rows * features),
            transcendentals=0,
        ),
        name="self_out",
    )(attended, weight)


def project_kernel(where_ref, *refs, cuts):
    wk_hbm, wv_hbm, keys_ref, values_ref = refs[-8:-4]
    rows_ref, wk_ref, wv_ref, sems = refs[-4:]
    tables = refs[:-8]
    entries = keys_ref.shape[0] // NLEN
    piece = NLEN // cuts
    bring = [
        pltpu.make_async_copy(source, target, sems.at[entries * cuts + at])
        for at, (source, target) in enumerate(
            ((wk_hbm, wk_ref), (wv_hbm, wv_ref))
        )
    ]
    for copy in bring:
        copy.start()

    def entry_copy(entry, cut, table, first, shard):
        return pltpu.make_async_copy(
            table.at[first + cut, shard],
            rows_ref.at[pl.ds(entry * NLEN + cut * piece, piece)],
            sems.at[entry * cuts + cut],
        )

    for entry in range(entries):
        for slot, table in enumerate(tables):

            @pl.when(where_ref[2 + 3 * entry] == slot)
            def _(entry=entry, table=table):
                for cut in range(cuts):
                    entry_copy(
                        entry, cut, table, where_ref[3 + 3 * entry], where_ref[4 + 3 * entry]
                    ).start()

    for copy in bring:
        copy.wait()
    width = keys_ref.shape[1]
    step = math.gcd(width, 512)
    for group in range(entries // NEIGH):
        for entry in range(NEIGH * group, NEIGH * (group + 1)):
            for cut in range(cuts):
                entry_copy(entry, cut, tables[0], 0, 0).wait()
        here = slice(group * GROUP, (group + 1) * GROUP)
        for at in range(0, width, step):
            lanes = slice(at, at + step)
            for weight, made in ((wk_ref, keys_ref), (wv_ref, values_ref)):
                made[here, lanes] = jnp.dot(
                    rows_ref[here, :], weight[:, lanes], preferred_element_type=jnp.float32
                ).astype(jnp.bfloat16)


def project_encodings(where, tables, w_cross_k, w_cross_v):
    entries = (where.shape[0] - 2) // 3
    piece, depth = tables[0].shape[2:]
    cuts = NLEN // piece
    width = w_cross_k.shape[1]
    vmem = pl.BlockSpec(memory_space=pltpu.VMEM)
    anywhere = pl.BlockSpec(memory_space=pl.ANY)
    made = jax.ShapeDtypeStruct((entries * NLEN, width), jnp.bfloat16)
    return pl.pallas_call(
        functools.partial(project_kernel, cuts=cuts),
        out_shape=[made, made],
        in_specs=[pl.BlockSpec(memory_space=pltpu.SMEM)] + [anywhere] * (len(tables) + 2),
        out_specs=[vmem] * 2,
        scratch_shapes=[
            pltpu.VMEM((entries * NLEN, depth), jnp.bfloat16),
            pltpu.VMEM(w_cross_k.shape, jnp.bfloat16),
            pltpu.VMEM(w_cross_v.shape, jnp.bfloat16),
            pltpu.SemaphoreType.DMA((entries * cuts + 2,)),
        ],
        compiler_params=pltpu.CompilerParams(vmem_limit_bytes=VMEM_BYTES),
        cost_estimate=pl.CostEstimate(
            flops=entries * NLEN * depth,
            bytes_accessed=2 * entries * NLEN * depth,
            transcendentals=0,
        ),
        name="project_encodings",
    )(where, *tables, w_cross_k, w_cross_v)


def apart_heads(query):
    first = lax.broadcasted_iota(jnp.int32, query.shape, 1) < HD
    nothing = jnp.zeros_like(query)
    return jnp.concatenate(
        (jnp.where(first, query, nothing), jnp.where(first, nothing, query)), axis=0
    )


def together_heads(mixed):
    rows = mixed.shape[0] // 2
    first = lax.broadcasted_iota(jnp.int32, (rows, 2 * HD), 1) < HD
    return jnp.where(first, mixed[:rows], mixed[rows:])


def cross_kernel(
    info_ref,
    hidden_ref,
    total_ref,
    gain_ref,
    wq_hbm,
    keys_hbm,
    values_hbm,
    wo_hbm,
    out_ref,
    residual_hbm,
    wq_ref,
    keys_ref,
    values_ref,
    wo_ref,
    rows_ref,
    query_ref,
    mixed_ref,
    residual_ref,
    sems,
    *,
    scale,
):
    rows, features = hidden_ref.shape
    n_db, share, _ = out_ref.shape
    width = wq_ref.shape[1]
    pairs = width // HD // 2
    tail = 16
    parts = 8
    cut, low = features // parts, width // parts
    wq_copies = [
        pltpu.make_async_copy(
            wq_hbm.at[pl.ds(k * cut, cut)], wq_ref.at[pl.ds(k * cut, cut)], sems.at[k]
        )
        for k in range(parts)
    ]
    other_copies = [
        pltpu.make_async_copy(keys_hbm, keys_ref, sems.at[2 * parts]),
        pltpu.make_async_copy(values_hbm, values_ref, sems.at[2 * parts + 1]),
    ] + [
        pltpu.make_async_copy(
            wo_hbm.at[pl.ds(k * low, low)], wo_ref.at[pl.ds(k * low, low)], sems.at[parts + k]
        )
        for k in range(parts)
    ]
    for copy in wq_copies + other_copies:
        copy.start()
    block = math.gcd(rows, 32)

    def norm(at, carried):
        here = pl.ds(pl.multiple_of(at * block, block), block)
        residual = hidden_ref[here, :].astype(jnp.float32) + total_ref[here, :].astype(jnp.float32)
        mean_square = jnp.mean(residual * residual, axis=-1, keepdims=True)
        rows_ref[here, :] = (
            residual * lax.rsqrt(mean_square + 1e-05) * gain_ref[...].astype(jnp.float32)
        ).astype(jnp.bfloat16)
        return carried

    lax.fori_loop(0, rows // block, norm, 0)
    own = pl.ds(pl.multiple_of(info_ref[0] * share, share), share)
    residual_ref[...] = hidden_ref[own, :].astype(jnp.float32) + total_ref[own, :].astype(
        jnp.float32
    )
    residual_copy = pltpu.make_async_copy(residual_ref, residual_hbm, sems.at[18])
    residual_copy.start()
    lanes = [slice(2 * pair * HD, 2 * (pair + 1) * HD) for pair in range(pairs)]
    for k in range(0, parts, 2):
        for copy in wq_copies[k : k + 2]:
            copy.wait()
        inner = slice(k * cut, (k + 2) * cut)
        for at in lanes:
            part = jnp.dot(
                rows_ref[:, inner], wq_ref[inner, at], preferred_element_type=jnp.float32
            )
            query_ref[:, at] = part if k == 0 else query_ref[:, at] + part
    for copy in other_copies[:2]:
        copy.wait()
    row = lax.broadcasted_iota(jnp.int32, (tail, 2 * HD), 0)
    spans = rows // SPAN
    for span in range(spans):
        top = span * SPAN
        here, after = (slice((span + k) * GROUP, (span + k + 1) * GROUP) for k in (0, 1))
        work = [(slice(top, top + SPAN), here, at) for at in lanes]
        work += [(slice(top + SPAN - tail, top + SPAN), after, at) for at in lanes]
        scores = [
            lax.dot_general(
                apart_heads(query_ref[of, at].astype(jnp.bfloat16)),
                keys_ref[which, at],
                (((1,), (1,)), ((), ())),
                preferred_element_type=jnp.float32,
            )
            * (scale * LOG2E)
            for of, which, at in work
        ]
        tops = [jnp.max(one, axis=-1, keepdims=True) for one in scores]
        weights = [jnp.exp2(one - top_one) for one, top_one in zip(scores, tops)]
        totals = [jnp.sum(one, axis=-1, keepdims=True) for one in weights]
        mixed = [
            jnp.dot(
                one.astype(jnp.bfloat16), values_ref[which, at], preferred_element_type=jnp.float32
            )
            for one, (_, which, at) in zip(weights, work)
        ]
        mixed = [together_heads(one / total) for one, total in zip(mixed, totals)]
        for pair, at in enumerate(lanes):
            main, last = mixed[pair], mixed[pairs + pair]
            if span == 0:
                main = jnp.where(info_ref[1] > 0, main, 0.0)
            last = jnp.where(row == tail - 1, last, main[SPAN - tail :])
            mixed_ref[top : top + SPAN - tail, at] = main[: SPAN - tail].astype(jnp.bfloat16)
            mixed_ref[top + SPAN - tail : top + SPAN, at] = last.astype(jnp.bfloat16)
    for copy in other_copies[2:]:
        copy.wait()
    step = math.gcd(features, 512)

    def columns(at, carried):
        here = pl.ds(pl.multiple_of(at * step, step), step)
        product = jnp.dot(mixed_ref[...], wo_ref[:, here], preferred_element_type=jnp.float32)
        product = product.astype(jnp.bfloat16)
        for owner in range(n_db):
            out_ref[owner, :, here] = product[owner * share : (owner + 1) * share]
        return carried

    lax.fori_loop(0, features // step, columns, 0, unroll=4)
    residual_copy.wait()


def cross_block(info, hidden, total, gain, w_cross_q, keys, values, w_cross_out, n_db, scale):
    rows, features = hidden.shape
    share = rows // n_db
    width = w_cross_q.shape[1]
    vmem = pl.BlockSpec(memory_space=pltpu.VMEM)
    anywhere = pl.BlockSpec(memory_space=pl.ANY)
    return pl.pallas_call(
        functools.partial(cross_kernel, scale=scale),
        out_shape=[
            jax.ShapeDtypeStruct((n_db, share, features), jnp.bfloat16),
            jax.ShapeDtypeStruct((share, features), jnp.float32),
        ],
        in_specs=[pl.BlockSpec(memory_space=pltpu.SMEM)] + [vmem] * 3 + [anywhere] * 4,
        out_specs=[vmem, anywhere],
        scratch_shapes=[
            pltpu.VMEM((features, width), jnp.bfloat16),
            pltpu.VMEM(keys.shape, jnp.bfloat16),
            pltpu.VMEM(values.shape, jnp.bfloat16),
            pltpu.VMEM((width, features), jnp.bfloat16),
            pltpu.VMEM((rows, features), jnp.bfloat16),
            pltpu.VMEM((rows, width), jnp.float32),
            pltpu.VMEM((rows, width), jnp.bfloat16),
            pltpu.VMEM((share, features), jnp.float32),
            pltpu.SemaphoreType.DMA((19,)),
        ],
        compiler_params=pltpu.CompilerParams(vmem_limit_bytes=VMEM_BYTES),
        cost_estimate=pl.CostEstimate(
            flops=4 * rows * width * (features + GROUP),
            bytes_accessed=4 * width * (features + keys.shape[0]) + 8 * rows * features,
            transcendentals=rows * GROUP * width // HD,
        ),
        name="cross_block",
    )(info, hidden, total, gain, w_cross_q, keys, values, w_cross_out)


def per_device(
    hidden_in,
    query_rows,
    key_rows,
    value_rows,
    w_self_out,
    norm_gain,
    w_cross_q,
    w_cross_k,
    w_cross_v,
    w_cross_out,
    enc_table,
    nb_shard,
    nb_row,
):
    features = hidden_in.shape[1]
    heads = query_rows.shape[1] // HD
    n_seq, n_db = lax.axis_size("seq"), lax.axis_size("db")
    seq_index, db_index = lax.axis_index("seq"), lax.axis_index("db")
    scale = 1.0 / math.sqrt(HD)

    rows_shard, _, depth = enc_table.shape
    encodings = enc_table.reshape(rows_shard * NLEN, depth)
    piece = rows_shard * NLEN // n_seq
    packed, part = pack_heads(
        seq_index.reshape(1).astype(jnp.int32), query_rows, key_rows, value_rows, encodings, piece
    )
    along_db = lax.all_gather(part, "db", axis=0)

    packed, nb_row, nb_shard = lax.optimization_barrier((packed, nb_row, nb_shard))
    wanted = jnp.stack((nb_row, nb_shard), axis=-1).astype(jnp.int32)
    place = jnp.stack((db_index, (seq_index > 0).astype(jnp.int32))).astype(jnp.int32)
    nearest = jnp.concatenate((span_before(wanted)[None], wanted), axis=0)
    row, shard = nearest[..., 0], nearest[..., 1]
    in_plane = n_seq == 8 and piece == NLEN
    if in_plane:
        where = jnp.stack((plane_slot(row, seq_index), jnp.zeros_like(row), shard), axis=-1)
    else:
        where = jnp.stack((jnp.zeros_like(row), row * (NLEN // piece), shard), axis=-1)
    info = jnp.concatenate((place, where.reshape(-1))).astype(jnp.int32)
    if heads == n_seq:
        held = lax.all_to_all(packed, "seq", 0, 0, tiled=True)
        held, info = lax.optimization_barrier((held, info))
        attended = lax.all_to_all(self_attend_head(held, scale), "seq", 0, 0, tiled=True)
    else:
        attended = self_attention_gathered(query_rows, key_rows, value_rows, scale)

    along_db, attended = lax.optimization_barrier((along_db, attended))
    partial = self_out(attended, w_self_out)
    along_db, partial = lax.optimization_barrier((along_db, partial))
    total = lax.psum(partial, "db")
    if in_plane:
        tables = tuple(one[None] for one in plane_pieces(along_db))
    else:
        tables = (lax.all_gather(along_db, "seq", axis=0),)
    projected = project_encodings(info, tables, w_cross_k, w_cross_v)
    total, (keys, values) = lax.optimization_barrier((total, projected))

    partial, residual = cross_block(
        info,
        hidden_in,
        total,
        norm_gain.reshape(1, features),
        w_cross_q,
        keys,
        values,
        w_cross_out,
        n_db,
        scale,
    )
    rows = hidden_in.shape[0]
    summed = lax.psum_scatter(
        partial.reshape(rows, features), "db", scatter_dimension=0, tiled=True
    )
    return residual + summed.astype(jnp.float32)


def solution(mesh):
    placed = (
        P("seq", None),
        P("seq", "db"),
        P("seq", "db"),
        P("seq", "db"),
        P("db", None),
        P(),
        P(None, "db"),
        P(None, "db"),
        P(None, "db"),
        P("db", None),
        P("db", None, None),
        P("seq", None),
        P("seq", None),
    )
    return jax.shard_map(
        per_device, mesh=mesh, in_specs=placed, out_specs=P(("seq", "db"), None), check_vma=False
    )
```
